32 devices in a mesh: wide: 8 (over z, x), narrow: 4 (over y, core).
Axes of the slice: x: 2, y: 2, z: 4, core: 2. Of those that a mesh axis runs over, the one named last changes fastest.
Arguments:
- inputs: bfloat16 [64, 512, 512], P(('wide', 'narrow')), may hold values from -6 to 6
- segment_ids: int32 [64, 512], P(('wide', 'narrow')), may hold values from 0 to 7, never falling along the last dimension, each value on 1 to 256 neighbouring positions
- cotangent: bfloat16 [64, 512, 512], P(('wide', 'narrow')), may hold values from -6 to 6
- w_query: bfloat16 [512, 512], P('wide', 'narrow'), may hold values from -0.25 to 0.25
- w_key: bfloat16 [512, 512], P('wide', 'narrow'), may hold values from -0.25 to 0.25
- w_value: bfloat16 [512, 512], P('wide', 'narrow'), may hold values from -0.25 to 0.25
- w_out: bfloat16 [512, 512], P('wide', 'narrow'), may hold values from -0.75 to 0.75
- w_in: bfloat16 [512, 2048], P('wide', 'narrow'), may hold values from -0.25 to 0.25
- w_back: bfloat16 [2048, 512], P('wide', 'narrow'), may hold values from -0.125 to 0.125
- position_table: bfloat16 [512, 512], P('wide', 'narrow'), may hold values from -3 to 3
- vectors: bfloat16 [8, 512], P('narrow', 'wide'), may hold values from -1.25 to 1.625, as said below
- in_bias: bfloat16 [2048], P(('wide', 'narrow')), may hold values from -3 to 3
Outputs:
- layer_output: bfloat16 [64, 512, 512], P(('wide', 'narrow'))
- input_grad: bfloat16 [64, 512, 512], P(('wide', 'narrow'))
- grad_query: float32 [512, 512], P('wide', 'narrow')
- grad_key: float32 [512, 512], P('wide', 'narrow')
- grad_value: float32 [512, 512], P('wide', 'narrow')
- grad_out: float32 [512, 512], P('wide', 'narrow')
- grad_in: float32 [512, 2048], P('wide', 'narrow')
- grad_back: float32 [2048, 512], P('wide', 'narrow')
- grad_table: float32 [512, 512], P('wide', 'narrow')
- grad_vectors: float32 [8, 512], P('narrow', 'wide')
- grad_in_bias: float32 [2048], P(('wide', 'narrow'))
The draws below stay inside these ranges and needn't reach their ends.
Inputs may be any that keep to these rules, and one draw needn't show every extreme that they name: `segment_ids`: within each window of 512 characters the ids never fall; a document spans 1 to 256 characters, and document lengths are heavy-tailed. `vectors`: rows 4 and 6 (the norms' gains) lie from 0.375 to 1.625, the other rows from -1.25 to 1.25.
All inputs are finite; a program needn't handle non-finite values.
Results may differ from the reference program's by a relative error of at most 0.015.
The reference program's roundings to bfloat16 on the way count: a program that leaves them out, or rounds other values in their place, can miss the bound.
Values may be sent and summed in bfloat16 or wider, within the bound.
No kernel may reach another device: no remote copies, remote signals or barrier semaphores. Data moves between devices by JAX's collectives and lax.ppermute only.
A program may use at most 128 MiB of HBM per device.

```python
import math
import jax
import jax.numpy as jnp
import numpy as np
from jax import lax

D = 512
HEADS = 8
HEAD = 64
FF = 2048
WIN = 512
NWIN = 64


def draw_vectors(key, part):
    key = jax.random.fold_in(key, 7)
    noise = jnp.clip(jax.random.normal(key, (8, D), jnp.float32), -2.5, 2.5)
    lifted = jnp.array([0.0, 0.0, 0.0, 0.0, 1.0, 0.0, 1.0, 0.0], jnp.float32)[:, None]
    spread = jnp.array([0.5, 0.5, 0.5, 0.5, 0.25, 0.5, 0.25, 0.5], jnp.float32)[:, None]
    return (lifted + spread * noise).astype(jnp.bfloat16)


def raised(values, stream_key, source, target, shards_of, factor):
    def block_of(axis_at):
        return (jnp.arange(values.shape[axis_at]) // (values.shape[axis_at] // shards_of)).reshape((-1,) + (1,) * (values.ndim - 1 - axis_at))

    one_side = jax.random.permutation(stream_key, shards_of)[block_of(target)]
    other_side = (block_of(target) + shards_of // 2) % shards_of
    return jnp.where((block_of(source) == one_side) | (block_of(source) == other_side), factor * values, values)


def shard_levels(own_key, dims, split, smallest, top_value):
    loudness = 1.0
    for position, blocks in split:
        draws = jax.random.uniform(jax.random.fold_in(jax.random.fold_in(own_key, 6), position), (blocks,), jnp.float32, smallest / len(split), top_value / len(split))
        loudness = loudness * jnp.repeat(jnp.exp(draws), dims[position] // blocks).reshape((-1,) + (1,) * (len(dims) - 1 - position))
    return loudness


def split_up(count, total, most, skew):
    loads = [(1 << 20) // math.isqrt(standing ** skew) + 1 for standing in range(2, count + 1)]
    surplus, counts = total - most - (count - 1), [1] * (count - 1)
    while surplus > 0:
        candidates = [i for i in range(count - 1) if counts[i] < most]
        mass, budget = sum([loads[i] for i in candidates]), surplus
        for i in candidates:
            extra = min(most - counts[i], max(1, budget * loads[i] // mass), surplus)
            counts[i] = counts[i] + extra
            surplus = surplus - extra
    return np.array([most] + counts)


def uneven(key, count, total, bound, skew):
    if count == 2:
        one = jax.random.randint(key, (), max(1, total - bound), min(bound, total - 1) + 1)
        return jnp.stack([one, total - one])
    lengths = jnp.asarray(split_up(count, total, bound, skew), jnp.int32)
    pairs = (count - 1) // 2
    donor, taker = lengths[1:1 + 2 * pairs:2], lengths[2:2 + 2 * pairs:2]
    margin = jnp.minimum(donor - 1, bound - taker)
    moved = jax.random.randint(jax.random.fold_in(key, 1), (pairs,), 0, 1 << 20) % (margin + 1)
    lengths = lengths.at[1:1 + 2 * pairs:2].set(donor - moved).at[2:2 + 2 * pairs:2].set(taker + moved)
    return lengths[jax.random.permutation(jax.random.fold_in(key, 2), count)]


def scatter_about(stream_key, shape, scale, bound, cuts=(), dtype=jnp.bfloat16):
    drawn = scale * jax.random.normal(stream_key, shape, jnp.float32)
    if cuts:
        drawn = drawn * shard_levels(stream_key, shape, cuts, -0.22, 0.18)
    return jnp.clip(drawn, -bound, bound).astype(dtype)


def bell_draw_with(stream_key, extent, width, limit, pieces, heavy, held_as=jnp.bfloat16):
    drawn = width * jax.random.normal(stream_key, extent, jnp.float32)
    if pieces:
        drawn = drawn * shard_levels(stream_key, extent, pieces, -0.22, 0.18)
    return jnp.clip(raised(drawn, jax.random.fold_in(stream_key, 3), *heavy), -limit, limit).astype(held_as)


def setup_inputs(seed: int = 0) -> dict:
    arg_keys = jax.random.split(jax.random.key(seed), 13)
    inputs = bell_draw_with(arg_keys[0], (NWIN, WIN, D), 1.0, 6.0, ((0, 32),), (0, 2, 32, 2.75))
    segment_ids = jax.vmap(lambda own: jnp.searchsorted(jnp.cumsum(uneven(own, 8, WIN, WIN // 2, 2)), jnp.arange(WIN), side="right"))(jax.random.split(arg_keys[1], NWIN)).reshape((NWIN, WIN)).astype(jnp.int32)
    cotangent = bell_draw_with(arg_keys[2], (NWIN, WIN, D), 1.0, 6.0, ((0, 32),), (0, 2, 32, 2.75))
    w_query = scatter_about(arg_keys[3], (D, D), D ** -0.5, 0.25, ((0, 8), (1, 4)))
    w_key = scatter_about(arg_keys[4], (D, D), D ** -0.5, 0.25, ((0, 8), (1, 4)))
    w_value = scatter_about(arg_keys[5], (D, D), D ** -0.5, 0.25, ((0, 8), (1, 4)))
    w_out = scatter_about(arg_keys[6], (D, D), (D // 8) ** -0.5, 0.75, ((0, 8), (1, 4)))
    w_in = scatter_about(arg_keys[7], (D, FF), D ** -0.5, 0.25, ((0, 8), (1, 4)))
    w_back = scatter_about(arg_keys[8], (FF, D), FF ** -0.5, 0.125, ((0, 8), (1, 4)))
    position_table = scatter_about(arg_keys[9], (WIN, D), 0.5, 3.0, ((0, 8), (1, 4)))
    vectors = draw_vectors(jax.random.fold_in(arg_keys[12], 71), 0)
    in_bias = scatter_about(arg_keys[11], (FF,), 0.5, 3.0, ((0, 32),))
    return dict(inputs=inputs, segment_ids=segment_ids, cotangent=cotangent, w_query=w_query, w_key=w_key, w_value=w_value, w_out=w_out, w_in=w_in, w_back=w_back, position_table=position_table, vectors=vectors, in_bias=in_bias)


PRECISE = lax.Precision.HIGHEST
EPSILON = 1e-05

@jax.custom_vjp
def low(v):
    return lax.optimization_barrier(v.astype(jnp.bfloat16)).astype(jnp.float32)

@jax.custom_vjp
def low_back(v):
    return v

def low_keep(v):
    return (low(v), None)

def low_pass(kept, grad):
    return (grad,)

def back_keep(v):
    return (v, None)

def back_low(kept, grad):
    return (low(grad),)
low.defvjp(low_keep, low_pass)
low_back.defvjp(back_keep, back_low)

def matmul_high(left, right):
    return jnp.dot(left, right, precision=PRECISE)

def layer_norm(values, gains, offset):
    average = lax.optimization_barrier(jnp.mean(values, axis=-1, keepdims=True))
    centred = values - average
    variance = lax.optimization_barrier(jnp.mean(centred * centred, axis=-1, keepdims=True))
    return centred * lax.rsqrt(variance + EPSILON) * gains + offset

def forward(stream_in, segments, parameters):
    w_query, w_key, w_value, w_out, w_in, w_back, position_table, vectors, in_bias = parameters
    windows = stream_in.shape[0]
    passed = (stream_in + position_table[None]).reshape(windows * WIN, D)
    mixed_low = low(passed)
    queries = low_back(low(matmul_high(mixed_low, w_query) + vectors[0]))
    key_rows = low_back(low(matmul_high(mixed_low, w_key)))
    value_rows = low_back(low(matmul_high(mixed_low, w_value) + vectors[1]))
    head_shape = (windows, WIN, HEADS, HEAD)
    scaling = 1.0 / math.sqrt(HEAD)
    scores = low_back(jnp.einsum('gqhe,gkhe->ghqk', queries.reshape(head_shape), key_rows.reshape(head_shape), precision=PRECISE) * scaling)
    places = jnp.arange(WIN)
    causal = (places[:, None] >= places[None, :])[None, None]
    same_doc = segments[:, None, :, None] == segments[:, None, None, :]
    scores = jnp.where(causal & same_doc, scores, -1e+30)
    row_peak = lax.optimization_barrier(jnp.max(scores, axis=-1, keepdims=True))
    weight = jnp.exp(scores - row_peak)
    shares = low(weight / lax.optimization_barrier(jnp.sum(weight, axis=-1, keepdims=True)))
    attended = jnp.einsum('ghqk,gkhe->gqhe', shares, value_rows.reshape(head_shape), precision=PRECISE)
    attended = low_back(low(attended.reshape(windows * WIN, D)))
    branch = low_back(matmul_high(attended, w_out) + vectors[2])
    hidden = layer_norm(passed + branch, vectors[4], vectors[5])
    pre_act = low_back(matmul_high(low(hidden), w_in) + in_bias)
    active = low(jax.nn.gelu(pre_act))
    ffn_out = low_back(matmul_high(active, w_back) + vectors[3])
    result = layer_norm(hidden + ffn_out, vectors[6], vectors[7])
    return result.reshape(windows, WIN, D)

def reference(inputs, segment_ids, cotangent, w_query, w_key, w_value, w_out, w_in, w_back, position_table, vectors, in_bias):
    parameters = tuple((p.astype(jnp.float32) for p in (w_query, w_key, w_value, w_out, w_in, w_back, position_table, vectors, in_bias)))
    group = min(NWIN, 4096 // WIN)
    blocks = NWIN // group
    input_blocks = inputs.astype(jnp.float32).reshape(blocks, group, WIN, D)
    segment_blocks = segment_ids.reshape(blocks, group, WIN)
    cot_blocks = cotangent.astype(jnp.float32).reshape(blocks, group, WIN, D)

    def accumulate(running, block_item):
        block_in, block_segments, block_cot = block_item

        def layer_fn(stream_in, *params_in):
            return forward(stream_in, block_segments, params_in)
        layer_out, pullback = jax.vjp(layer_fn, block_in, *parameters)
        gradients = pullback(block_cot)
        updated = tuple((a + b for a, b in zip(running, gradients[1:])))
        return (updated, (layer_out.astype(jnp.bfloat16), gradients[0].astype(jnp.bfloat16)))
    zero_grads = tuple((jnp.zeros_like(p) for p in parameters))
    totals, (outputs, in_grads) = lax.scan(accumulate, zero_grads, (input_blocks, segment_blocks, cot_blocks))
    return (outputs.reshape(NWIN, WIN, D), in_grads.reshape(NWIN, WIN, D), totals[0], totals[1], totals[2], totals[3], totals[4], totals[5], totals[6], totals[7], totals[8])
```

```python
from functools import partial
import math

import jax
import jax.numpy as jnp
from jax import lax
from jax.experimental import pallas as pl
from jax.experimental.pallas import tpu as pltpu
from jax.sharding import PartitionSpec as P

HEADS = 8
EPSILON = 1e-05
AXES = ("wide", "narrow")
F32 = jnp.float32
BF16 = jnp.bfloat16
NEG = -1e30
VMEM_LIMIT = 60 * 1024 * 1024

WIDE = 8
NARROW = 4
PLACES = WIDE * NARROW
HALF = PLACES // 2

Z1, Z0, X, Y = 16, 8, 4, 2
ORDER_FIRST = ((Z1, Z0, X, Y), (Y, Z1, Z0, X))
ORDER_SECOND = ((Z1, Z0, X, Y), (Y, Z1, Z0, X))


def nn(left, right):
    return lax.dot_general(left, right, (((1,), (0,)), ((), ())), preferred_element_type=F32)


def nt(left, right):
    return lax.dot_general(left, right, (((1,), (1,)), ((), ())), preferred_element_type=F32)


def step_mask(order, step, core):
    return jnp.where(core == 0, order[0][step], order[1][step])


def relative_mask(order, block, core):
    masks = []
    for own in order:
        total = 0
        for step in range(4):
            if block >> step & 1:
                total ^= own[step]
        masks.append(total)
    return jnp.where(core == 0, masks[0], masks[1])


def place_of(order, direct, me, half, block):
    if not direct:
        where = half * HALF + block
        return where // NARROW, where % NARROW
    core = me & 1
    if half == 0:
        where = me ^ relative_mask(order, block, core)
    else:
        where = me ^ 1 ^ relative_mask(order, block, 1 - core)
    return where >> 2, where & 3


def pairs(order, step):
    found = []
    for place in range(PLACES):
        mask = 1 if step == 4 else order[place & 1][step]
        found.append((place, place ^ mask))
    return found


def my_place():
    return lax.axis_index("wide") * NARROW + lax.axis_index("narrow")


def head_masks(rows):
    lane = lax.broadcasted_iota(jnp.int32, (rows, 128), 1)
    return lane < 64


def stack_heads(pair_rows, low):
    zero = jnp.zeros_like(pair_rows)
    return jnp.concatenate(
        [jnp.where(low, pair_rows, zero), jnp.where(low, zero, pair_rows)], axis=0
    )


def fill_bias(segments_ref, bias_ref, windows):
    length = segments_ref.shape[1]
    for window in range(windows):
        row = segments_ref[window : window + 1, :].astype(F32)
        column = jnp.transpose(jnp.broadcast_to(row, (128, length)))
        for block in range(length // 128):
            start = max(0, block * 128 - 256)
            stop = block * 128 + 128
            span = stop - start
            key_at = start + lax.broadcasted_iota(jnp.int32, (span, 128), 0)
            query_at = block * 128 + lax.broadcasted_iota(jnp.int32, (span, 128), 1)
            same = column[start:stop, :] == row[:, block * 128 : block * 128 + 128]
            bias_ref[window, block, 0:span, :] = jnp.where(
                (key_at <= query_at) & same, 0.0, NEG
            )


def wait_whole(ref, sem):
    pltpu.make_async_copy(ref, ref, sem).wait()


def attend_kernel(
    direct,
    segments_ref,
    x_ref,
    p0_ref,
    p1_ref,
    p2_ref,
    p3_ref,
    qkv_ref,
    attended_ref,
    lse_ref,
    passed_ref,
    mixed_ref,
    vec_ref,
    bin_ref,
    weights,
    table,
    small,
    bias,
    sems,
):
    windows, length = segments_ref.shape
    me = my_place() if direct else 0
    for block in range(HALF):
        for half in range(2):
            source = ((p0_ref, p1_ref), (p2_ref, p3_ref))[half][block // 8].at[block % 8]
            wide, narrow = place_of(ORDER_FIRST, direct, me, half, block)
            rows = pl.ds(pl.multiple_of(wide * 64, 64), 64)
            pltpu.make_async_copy(
                source.at[pl.ds(192, 64)],
                table.at[rows, pl.ds(pl.multiple_of(narrow * 128, 128), 128)],
                sems.at[0],
            ).start()
            pltpu.make_async_copy(
                source.at[pl.ds(256, 16)], small.at[half * HALF + block], sems.at[1]
            ).start()
            for part in range(3):
                pltpu.make_async_copy(
                    source.at[pl.ds(part * 64, 64)],
                    weights.at[narrow, rows, pl.ds(part * 128, 128)],
                    sems.at[2],
                ).start()
    fill_bias(segments_ref, bias, windows)
    wait_whole(table, sems.at[0])
    for window in range(windows):
        rows = slice(window * length, (window + 1) * length)
        passed = x_ref[rows, :].astype(F32) + table[...].astype(F32)
        passed_ref[rows, :] = passed
        mixed_ref[rows, :] = passed.astype(BF16)
    wait_whole(small, sems.at[1])
    vec_ref[...] = jnp.zeros_like(vec_ref)
    bin_ref[...] = jnp.zeros_like(bin_ref)
    for half in range(2):
        for block in range(HALF):
            wide, narrow = place_of(ORDER_FIRST, direct, me, half, block)
            piece = small[half * HALF + block].astype(F32)
            vec_ref[wide // 2] += piece[0:8]
            bin_ref[wide // 4] += piece[8:16]
    wait_whole(weights, sems.at[2])
    low = head_masks(128)

    def per_pair(pair, unused):
        projected = nn(mixed_ref[...], weights[pair])
        vec = vec_ref[pair]
        queries = (projected[:, 0:128] + vec[0:1]).astype(BF16) * BF16(0.125)
        qkv_ref[pair, :, 0:128] = queries
        qkv_ref[pair, :, 128:256] = projected[:, 128:256].astype(BF16)
        qkv_ref[pair, :, 256:384] = (projected[:, 256:384] + vec[1:2]).astype(BF16)
        for window in range(windows):
            base = window * length
            values_t = jnp.transpose(qkv_ref[pair, base : base + length, 256:384])
            for block in range(length // 128):
                start = max(0, block * 128 - 256)
                stop = block * 128 + 128
                span = stop - start
                query = stack_heads(
                    qkv_ref[pair, base + block * 128 : base + block * 128 + 128, 0:128], low
                )
                keys = qkv_ref[pair, base + start : base + stop, 128:256]
                mask = bias[window, block, 0:span, :]
                scores = nt(keys, query) + jnp.concatenate([mask, mask], axis=1)
                peak = jnp.max(scores, axis=0, keepdims=True)
                weight = jnp.exp(scores - peak)
                total = jnp.sum(weight, axis=0, keepdims=True)
                shares = (weight * (1.0 / total)).astype(BF16)
                lse_ref[pair, window, block : block + 1, :] = peak + jnp.log(total)
                joined = nn(values_t[:, start:stop], shares)
                both = jnp.concatenate([joined[0:64, 0:128], joined[64:128, 128:256]], axis=0)
                attended_ref[
                    base + block * 128 : base + block * 128 + 128,
                    pl.ds(pl.multiple_of(pair * 128, 128), 128),
                ] = jnp.transpose(both).astype(BF16)
        return unused

    lax.fori_loop(0, NARROW, per_pair, 0)


def norm_parts(values):
    average = jnp.mean(values, axis=-1, keepdims=True)
    centred = values - average
    variance = jnp.mean(centred * centred, axis=-1, keepdims=True)
    scale = lax.rsqrt(variance + EPSILON)
    return centred * scale, scale


def norm_back(hat, scale, gains, grad):
    scaled = grad * gains
    first = jnp.mean(scaled, axis=-1, keepdims=True)
    second = jnp.mean(scaled * hat, axis=-1, keepdims=True)
    return scale * (scaled - first - hat * second)


def vec_row(vec_ref, row):
    return jnp.concatenate([vec_ref[tile, row : row + 1, :] for tile in range(4)], axis=1)


def column_sum(values):
    return jnp.sum(values, axis=0, keepdims=True)


GELU_SCALE = math.sqrt(2.0 / math.pi)


def gelu_both(pre):
    square = pre * pre
    curve = jnp.tanh(pre * (GELU_SCALE + (GELU_SCALE * 0.044715) * square))
    half = 0.5 + 0.5 * curve
    slope = (0.5 * pre) * (1.0 - curve * curve) * (
        GELU_SCALE + (3.0 * GELU_SCALE * 0.044715) * square
    )
    return pre * half, half + slope


def load_second(direct, blocks, w_out, w_in, w_back, sems):
    me = my_place() if direct else 0
    for block in range(HALF):
        for half in range(2):
            source = blocks[half * 2 + block // 8].at[block % 8]
            wide, narrow = place_of(ORDER_SECOND, direct, me, half, block)
            rows = pl.ds(pl.multiple_of(wide * 64, 64), 64)
            columns = pl.ds(pl.multiple_of(narrow * 128, 128), 128)
            pltpu.make_async_copy(source.at[0], w_out.at[rows, columns], sems.at[0]).start()
            pltpu.make_async_copy(
                source.at[pl.ds(1, 4)], w_in.at[pl.ds(narrow * 4, 4), rows, :], sems.at[1]
            ).start()
            pltpu.make_async_copy(
                source.at[pl.ds(5, 4)], w_back.at[pl.ds(wide * 4, 4), :, columns], sems.at[2]
            ).start()


def w_in_columns(w_in, chunk):
    return jnp.concatenate([w_in[chunk * 2], w_in[chunk * 2 + 1]], axis=1)


def forward_kernel(
    direct,
    attended_ref,
    passed_ref,
    cotangent_ref,
    vec_ref,
    bin_ref,
    p0_ref,
    p1_ref,
    p2_ref,
    p3_ref,
    output_ref,
    slope_ref,
    grad_second_ref,
    first_ref,
    low_ref,
    keep_ref,
    send_ref,
    sums_ref,
    w_out,
    w_in,
    w_back,
    active,
    grad_t,
    sems,
):
    step = pl.program_id(0)
    rows = attended_ref.shape[0]

    @pl.when(step == 0)
    def _():
        load_second(direct, (p0_ref, p1_ref, p2_ref, p3_ref), w_out, w_in, w_back, sems)
        sums_ref[...] = jnp.zeros_like(sums_ref)
        wait_whole(w_out, sems.at[0])

    first_sum = passed_ref[...] + nn(attended_ref[...], w_out[...]) + vec_row(vec_ref, 2)
    first_ref[...] = first_sum
    hat, unused_scale = norm_parts(first_sum)
    hidden = hat * vec_row(vec_ref, 4) + vec_row(vec_ref, 5)
    low = hidden.astype(BF16)
    low_ref[...] = low

    @pl.when(step == 0)
    def _():
        wait_whole(w_in, sems.at[1])
        wait_whole(w_back, sems.at[2])

    total = hidden + vec_row(vec_ref, 3)
    for chunk in range(8):
        offset = jnp.concatenate(
            [bin_ref[chunk // 4, 2 * (chunk % 4) + part : 2 * (chunk % 4) + part + 1, :] for part in range(2)],
            axis=1,
        )
        value, slope = gelu_both(nn(low, w_in_columns(w_in, chunk)) + offset)
        value = value.astype(BF16)
        active[pl.ds(pl.multiple_of(step * rows, rows), rows), chunk * 256 : chunk * 256 + 256] = value
        slope_ref[:, chunk * 256 : chunk * 256 + 256] = slope
        weight = w_back[chunk * 4 : chunk * 4 + 4].reshape(256, 512)
        total += nn(value, weight)
    hat, scale = norm_parts(total)
    gains = vec_row(vec_ref, 6)
    output_ref[...] = (hat * gains + vec_row(vec_ref, 7)).astype(BF16)
    cotangent = cotangent_ref[...].astype(F32)
    grad_second = norm_back(hat, scale, gains, cotangent)
    grad_second_ref[...] = grad_second
    grad_low = grad_second.astype(BF16)
    grad_t[:, pl.ds(pl.multiple_of(step * rows, rows), rows)] = jnp.transpose(grad_low)
    sums_ref[0:1, :] += column_sum(grad_low.astype(F32))
    sums_ref[1:2, :] += column_sum(cotangent * hat)
    sums_ref[2:3, :] += column_sum(cotangent)

    @pl.when(step == pl.num_programs(0) - 1)
    def _():
        me = my_place() if direct else 0
        for half, target in ((0, keep_ref), (1, send_ref)):
            for block in range(HALF):
                wide, narrow = place_of(ORDER_SECOND, direct, me, half, block)
                piece = nn(
                    grad_t[pl.ds(pl.multiple_of(narrow * 128, 128), 128), :],
                    active[:, pl.ds(pl.multiple_of(wide * 256, 256), 256)],
                )
                target[block, 0:128, :] = piece[:, 0:128].astype(target.dtype)
                target[block, 128:256, :] = piece[:, 128:256].astype(target.dtype)


def backward_kernel(
    direct,
    slope_ref,
    grad_second_ref,
    first_ref,
    low_ref,
    attended_ref,
    vec_ref,
    p0_ref,
    p1_ref,
    p2_ref,
    p3_ref,
    grad_first_ref,
    grad_attended_ref,
    keep_ref,
    send_ref,
    sums_ref,
    bin_sums_ref,
    w_out,
    w_in,
    w_back,
    grad_pre,
    grad_branch,
    low_t,
    attended_t,
    sems,
):
    step = pl.program_id(0)
    rows = attended_ref.shape[0]
    here = pl.ds(pl.multiple_of(step * rows, rows), rows)

    @pl.when(step == 0)
    def _():
        load_second(direct, (p0_ref, p1_ref, p2_ref, p3_ref), w_out, w_in, w_back, sems)
        sums_ref[...] = jnp.zeros_like(sums_ref)
        bin_sums_ref[...] = jnp.zeros_like(bin_sums_ref)

    low_t[:, here] = jnp.transpose(low_ref[...])
    attended_t[:, here] = jnp.transpose(attended_ref[...])

    @pl.when(step == 0)
    def _():
        wait_whole(w_out, sems.at[0])
        wait_whole(w_in, sems.at[1])
        wait_whole(w_back, sems.at[2])

    grad_hidden = grad_second_ref[...]
    grad_low = grad_hidden.astype(BF16)
    for chunk in range(8):
        weight = w_back[chunk * 4 : chunk * 4 + 4].reshape(256, 512)
        grad = nt(grad_low, weight) * slope_ref[:, chunk * 256 : chunk * 256 + 256]
        grad = grad.astype(BF16)
        grad_pre[here, chunk * 256 : chunk * 256 + 256] = grad
        grad_hidden += nt(grad, w_in_columns(w_in, chunk))
        sums = column_sum(grad.astype(F32))
        for part in range(2):
            row = 2 * (chunk % 4) + part
            bin_sums_ref[chunk // 4, row : row + 1, :] += sums[:, part * 128 : part * 128 + 128]
    hat, scale = norm_parts(first_ref[...])
    gains = vec_row(vec_ref, 4)
    grad_first = norm_back(hat, scale, gains, grad_hidden)
    grad_first_ref[...] = grad_first
    branch = grad_first.astype(BF16)
    grad_branch[here, :] = branch
    sums_ref[0:1, :] += column_sum(branch.astype(F32))
    sums_ref[1:2, :] += column_sum(grad_hidden * hat)
    sums_ref[2:3, :] += column_sum(grad_hidden)
    grad_attended_ref[...] = nt(branch, w_out[...]).astype(BF16)

    @pl.when(step == pl.num_programs(0) - 1)
    def _():
        me = my_place() if direct else 0
        for half, target in ((0, keep_ref), (1, send_ref)):
            for block in range(HALF):
                wide, narrow = place_of(ORDER_SECOND, direct, me, half, block)
                own = pl.ds(pl.multiple_of(wide * 64, 64), 64)
                piece = nn(
                    low_t[own, :], grad_pre[:, pl.ds(pl.multiple_of(narrow * 512, 512), 512)]
                )
                for part in range(4):
                    target[block, part] = piece[:, part * 128 : part * 128 + 128].astype(target.dtype)
                piece = nn(
                    attended_t[own, :],
                    grad_branch[:, pl.ds(pl.multiple_of(narrow * 128, 128), 128)],
                )
                target[block, 4] = piece.astype(target.dtype)


def attend_back_kernel(
    direct,
    segments_ref,
    qkv_ref,
    grad_attended_ref,
    lse_ref,
    mixed_ref,
    grad_first_ref,
    sums_a_ref,
    sums_b_ref,
    bin_sums_ref,
    p0_ref,
    p1_ref,
    p2_ref,
    p3_ref,
    stream_ref,
    keep_ref,
    send_ref,
    weights,
    bias,
    mixed_t,
    grads,
    accumulate,
    stream,
    vec_sums,
    sems,
):
    windows, length = segments_ref.shape
    me = my_place() if direct else 0
    for block in range(HALF):
        for half in range(2):
            source = ((p0_ref, p1_ref), (p2_ref, p3_ref))[half][block // 8].at[block % 8]
            wide, narrow = place_of(ORDER_FIRST, direct, me, half, block)
            rows = pl.ds(pl.multiple_of(wide * 64, 64), 64)
            for part in range(3):
                pltpu.make_async_copy(
                    source.at[pl.ds(part * 64, 64)],
                    weights.at[narrow, rows, pl.ds(part * 128, 128)],
                    sems.at[0],
                ).start()
    fill_bias(segments_ref, bias, windows)
    mixed_t[...] = jnp.transpose(mixed_ref[...])
    stream[...] = grad_first_ref[...]
    for tile in range(4):
        lanes = slice(tile * 128, tile * 128 + 128)
        vec_sums[tile, 2:3, :] = sums_b_ref[0:1, lanes]
        vec_sums[tile, 3:4, :] = sums_a_ref[0:1, lanes]
        vec_sums[tile, 4:6, :] = sums_b_ref[1:3, lanes]
        vec_sums[tile, 6:8, :] = sums_a_ref[1:3, lanes]
    wait_whole(weights, sems.at[0])
    low = head_masks(128)

    def per_pair(pair, unused):
        for window in range(windows):
            base = window * length
            keys_t = jnp.transpose(qkv_ref[pair, base : base + length, 128:256])
            accumulate[...] = jnp.zeros_like(accumulate)
            for block in range(length // 128):
                start = max(0, block * 128 - 256)
                stop = block * 128 + 128
                span = stop - start
                here = slice(base + block * 128, base + block * 128 + 128)
                query = stack_heads(qkv_ref[pair, here, 0:128], low)
                above = stack_heads(
                    grad_attended_ref[here, pl.ds(pl.multiple_of(pair * 128, 128), 128)], low
                )
                keys = qkv_ref[pair, base + start : base + stop, 128:256]
                values = qkv_ref[pair, base + start : base + stop, 256:384]
                mask = bias[window, block, 0:span, :]
                mask = jnp.concatenate([mask, mask], axis=1)
                shares = jnp.exp(
                    nt(keys, query) + mask - lse_ref[pair, window, block : block + 1, :]
                )
                grad_shares = nt(values, above)
                inner = jnp.sum(shares * grad_shares, axis=0, keepdims=True)
                grad_scores = (shares * (grad_shares - inner)).astype(BF16)
                accumulate[start:stop, 0:128] += nn(grad_scores, query)
                accumulate[start:stop, 128:256] += nn(shares.astype(BF16), above)
                joined = nn(keys_t[:, start:stop], grad_scores)
                both = jnp.concatenate([joined[0:64, 0:128], joined[64:128, 128:256]], axis=0)
                grads[here, 0:128] = (jnp.transpose(both) * 0.125).astype(BF16)
            grads[base : base + length, 128:384] = accumulate[...].astype(BF16)
        grad = grads[...]
        vec_sums[pair, 0:1, :] = column_sum(grad[:, 0:128].astype(F32))
        vec_sums[pair, 1:2, :] = column_sum(grad[:, 256:384].astype(F32))
        stream[...] += nt(grad, weights[pair])
        weight_grads = nn(mixed_t[...], grad)
        for wide in range(WIDE):
            half, block = index_of(ORDER_FIRST, direct, me, wide, pair)
            piece = weight_grads[wide * 64 : wide * 64 + 64, :]

            for which, target in ((0, keep_ref), (1, send_ref)):

                @pl.when(half == which)
                def _(target=target, piece=piece, block=block):
                    for part in range(3):
                        target[block, part * 64 : part * 64 + 64, :] = piece[
                            :, part * 128 : part * 128 + 128
                        ].astype(target.dtype)

        return unused

    lax.fori_loop(0, NARROW, per_pair, 0)
    total = jnp.zeros((length, stream.shape[1]), F32)
    for window in range(windows):
        rows = slice(window * length, (window + 1) * length)
        stream_ref[rows, :] = stream[rows, :].astype(BF16)
        total += stream[rows, :]
    stream[0:length, :] = total
    for half, target in ((0, keep_ref), (1, send_ref)):
        for block in range(HALF):
            wide, narrow = place_of(ORDER_FIRST, direct, me, half, block)
            target[block, 192:256, :] = stream[
                pl.ds(pl.multiple_of(wide * 64, 64), 64),
                pl.ds(pl.multiple_of(narrow * 128, 128), 128),
            ].astype(target.dtype)
            target[block, 256:264, :] = vec_sums[wide // 2].astype(target.dtype)
            target[block, 264:272, :] = bin_sums_ref[wide // 4].astype(target.dtype)


def index_of(order, direct, me, wide, narrow):
    where = wide * NARROW + narrow
    if not direct:
        return where // HALF, where % HALF
    core = where & 1
    apart = me ^ where
    half = apart & 1
    apart = apart ^ half
    block = 0
    for step in range(4):
        bit = jnp.where((apart & step_mask(order, step, core)) != 0, 1 << step, 0)
        block = block + bit
    return half, block


def vmem():
    return pl.BlockSpec(memory_space=pltpu.VMEM)


def hbm():
    return pl.BlockSpec(memory_space=pl.ANY)


def params(**more):
    return pltpu.CompilerParams(vmem_limit_bytes=VMEM_LIMIT, **more)


def shape(dims, dtype):
    return jax.ShapeDtypeStruct(dims, dtype)


def attend_call(direct, segments, x, blocks):
    windows, length = segments.shape
    total = windows * length
    return pl.pallas_call(
        partial(attend_kernel, direct),
        out_shape=(
            shape((NARROW, total, 384), BF16),
            shape((total, 512), BF16),
            shape((NARROW, windows, length // 128, 256), F32),
            shape((total, 512), F32),
            shape((total, 512), BF16),
            shape((4, 8, 128), F32),
            shape((2, 8, 128), F32),
        ),
        in_specs=[vmem(), vmem()] + [hbm()] * 4,
        out_specs=tuple([vmem()] * 7),
        scratch_shapes=[
            pltpu.VMEM((NARROW, 512, 384), BF16),
            pltpu.VMEM((512, 512), BF16),
            pltpu.VMEM((PLACES, 16, 128), BF16),
            pltpu.VMEM((windows, length // 128, 384, 128), F32),
            pltpu.SemaphoreType.DMA((3,)),
        ],
        compiler_params=params(),
        name="attend",
    )(segments, x, *blocks)


ROWS = 256


def second_scratch():
    return [
        pltpu.VMEM((512, 512), BF16),
        pltpu.VMEM((16, 512, 128), BF16),
        pltpu.VMEM((32, 64, 512), BF16),
    ]


def row_block(columns):
    return pl.BlockSpec((ROWS, columns), lambda step: (step, 0))


def forward_call(direct, attended, passed, cotangent, vec, bins, blocks):
    total = attended.shape[0]
    return pl.pallas_call(
        partial(forward_kernel, direct),
        grid=(total // ROWS,),
        out_shape=(
            shape((total, 512), BF16),
            shape((total, 2048), F32),
            shape((total, 512), F32),
            shape((total, 512), F32),
            shape((total, 512), BF16),
            shape((HALF, 256, 128), F32),
            shape((HALF, 256, 128), BF16),
            shape((8, 512), F32),
        ),
        in_specs=[row_block(512)] * 3 + [vmem()] * 2 + [hbm()] * 4,
        out_specs=(
            row_block(512),
            row_block(2048),
            row_block(512),
            row_block(512),
            row_block(512),
            vmem(),
            vmem(),
            vmem(),
        ),
        scratch_shapes=second_scratch()
        + [
            pltpu.VMEM((total, 2048), BF16),
            pltpu.VMEM((512, total), BF16),
            pltpu.SemaphoreType.DMA((3,)),
        ],
        compiler_params=params(),
        name="forward",
    )(attended, passed, cotangent, vec, bins, *blocks)


def backward_call(direct, slope, grad_second, first_sum, low, attended, vec, blocks):
    total = attended.shape[0]
    return pl.pallas_call(
        partial(backward_kernel, direct),
        grid=(total // ROWS,),
        out_shape=(
            shape((total, 512), F32),
            shape((total, 512), BF16),
            shape((HALF, 5, 64, 128), F32),
            shape((HALF, 5, 64, 128), BF16),
            shape((8, 512), F32),
            shape((2, 8, 128), F32),
        ),
        in_specs=[row_block(2048)] + [row_block(512)] * 4 + [vmem()] + [hbm()] * 4,
        out_specs=(row_block(512), row_block(512), vmem(), vmem(), vmem(), vmem()),
        scratch_shapes=second_scratch()
        + [
            pltpu.VMEM((total, 2048), BF16),
            pltpu.VMEM((total, 512), BF16),
            pltpu.VMEM((512, total), BF16),
            pltpu.VMEM((512, total), BF16),
            pltpu.SemaphoreType.DMA((3,)),
        ],
        compiler_params=params(),
        name="backward",
    )(slope, grad_second, first_sum, low, attended, vec, *blocks)


def attend_back_call(direct, segments, qkv, grad_attended, lse, mixed, grad_first, sums, blocks):
    windows, length = segments.shape
    total = windows * length
    return pl.pallas_call(
        partial(attend_back_kernel, direct),
        out_shape=(
            shape((total, 512), BF16),
            shape((HALF, 272, 128), F32),
            shape((HALF, 272, 128), BF16),
        ),
        in_specs=[vmem()] * 9 + [hbm()] * 4,
        out_specs=(vmem(), vmem(), vmem()),
        scratch_shapes=[
            pltpu.VMEM((NARROW, 512, 384), BF16),
            pltpu.VMEM((windows, length // 128, 384, 128), F32),
            pltpu.VMEM((512, total), BF16),
            pltpu.VMEM((total, 384), BF16),
            pltpu.VMEM((length, 256), F32),
            pltpu.VMEM((total, 512), F32),
            pltpu.VMEM((4, 8, 128), F32),
            pltpu.SemaphoreType.DMA((1,)),
        ],
        compiler_params=params(),
        name="attend_back",
    )(segments, qkv, grad_attended, lse, mixed, grad_first, *sums, *blocks)


def gather_blocks(own, order):
    held = own[None]
    for step in range(3):
        held = jnp.concatenate([held, lax.ppermute(held, AXES, pairs(order, step))], axis=0)
    far = lax.ppermute(held, AXES, pairs(order, 3))
    return (
        held,
        far,
        lax.ppermute(held, AXES, pairs(order, 4)),
        lax.ppermute(far, AXES, pairs(order, 4)),
    )


def scatter_sum(keep, send, order):
    total = keep + lax.ppermute(send, AXES, pairs(order, 4)).astype(F32)
    for step in (3, 2, 1, 0):
        size = 1 << step
        total = total[:size] + lax.ppermute(
            total[size:].astype(BF16), AXES, pairs(order, step)
        ).astype(F32)
    return total[0]


def small_block(vectors, in_bias, wide, narrow):
    row = lax.broadcasted_iota(jnp.int32, (8, 128), 0)
    side = lax.broadcasted_iota(jnp.int32, (8, 128), 1) // 64
    spread = jnp.tile(vectors, (4, 2))
    first = jnp.where((row // 2 == narrow) & (side == wide % 2), spread, 0)
    spread = jnp.tile(in_bias[None], (8, 2))
    second = jnp.where((row == 2 * (wide % 4) + narrow // 2) & (side == narrow % 2), spread, 0)
    return jnp.concatenate([first, second], axis=0).astype(BF16)


def first_block(w_query, w_key, w_value, table, small):
    return jnp.concatenate([w_query, w_key, w_value, table, small], axis=0)


def second_block(w_out, w_in, w_back):
    return jnp.concatenate(
        [w_out[None]]
        + [w_in[None, :, part * 128 : part * 128 + 128] for part in range(4)]
        + [w_back.reshape(4, 64, 128)],
        axis=0,
    )


def turned(total):
    return jnp.concatenate([total[0:128].T, total[128:256].T], axis=0)


def layer(direct, inputs, segment_ids, cotangent, first, second):
    windows, length, features = inputs.shape
    rows = windows * length
    x = inputs.reshape(rows, features)
    qkv, attended, lse, passed, mixed, vec, bins = attend_call(direct, segment_ids, x, first)
    output, slope, grad_second, first_sum, low, keep_back, send_back, sums_a = forward_call(
        direct, attended, passed, cotangent.reshape(rows, features), vec, bins, second
    )
    grad_first, grad_attended, keep_in, send_in, sums_b, bin_sums = backward_call(
        direct, slope, grad_second, first_sum, low, attended, vec, second
    )
    stream, keep_first, send_first = attend_back_call(
        direct,
        segment_ids,
        qkv,
        grad_attended,
        lse,
        mixed,
        grad_first,
        (sums_a, sums_b, bin_sums),
        first,
    )
    return (
        output.reshape(inputs.shape),
        stream.reshape(inputs.shape),
        (keep_back, send_back),
        (keep_in, send_in),
        (keep_first, send_first),
    )


def per_device(
    inputs,
    segment_ids,
    cotangent,
    w_query,
    w_key,
    w_value,
    w_out,
    w_in,
    w_back,
    position_table,
    vectors,
    in_bias,
):
    wide, narrow = lax.axis_index("wide"), lax.axis_index("narrow")
    small = small_block(vectors, in_bias, wide, narrow)
    first = gather_blocks(
        first_block(w_query, w_key, w_value, position_table, small), ORDER_FIRST
    )
    second = gather_blocks(second_block(w_out, w_in, w_back), ORDER_SECOND)
    output, stream, back, inner, outer = layer(
        True, inputs, segment_ids, cotangent, first, second
    )
    back = scatter_sum(*back, ORDER_SECOND)
    inner = scatter_sum(*inner, ORDER_SECOND)
    outer = scatter_sum(*outer, ORDER_FIRST)
    grad_in = jnp.concatenate([inner[part] for part in range(4)], axis=1)
    vec = outer[256:264]
    vec = jnp.where(wide % 2 == 0, vec[:, 0:64], vec[:, 64:128])
    vec = lax.dynamic_slice_in_dim(vec, narrow * 2, 2, 0)
    bins = lax.dynamic_slice_in_dim(outer[264:272], 2 * (wide % 4) + narrow // 2, 1, 0)[0]
    bins = jnp.where(narrow % 2 == 0, bins[0:64], bins[64:128])
    return (
        output,
        stream,
        outer[0:64],
        outer[64:128],
        outer[128:192],
        inner[4],
        grad_in,
        turned(back),
        outer[192:256],
        vec,
        bins,
    )


def canonical(array, axis_tiles):
    rows, columns = array.shape
    across, along = axis_tiles
    return (
        array.reshape(across, rows // across, along, columns // along)
        .transpose(0, 2, 1, 3)
        .reshape(PLACES, rows // across, columns // along)
    )


def uncanonical(blocks, rows, columns):
    return (
        blocks.reshape(WIDE, NARROW, rows // WIDE, columns // NARROW)
        .transpose(0, 2, 1, 3)
        .reshape(rows, columns)
    )


def per_device_any(
    inputs,
    segment_ids,
    cotangent,
    w_query,
    w_key,
    w_value,
    w_out,
    w_in,
    w_back,
    position_table,
    vectors,
    in_bias,
):
    def whole(array):
        array = lax.all_gather(array, "narrow", axis=1, tiled=True)
        return lax.all_gather(array, "wide", axis=0, tiled=True)

    def fours(blocks):
        return tuple(blocks[at * 8 : at * 8 + 8] for at in range(4))

    vectors = lax.all_gather(vectors, "narrow", axis=0, tiled=True)
    vectors = lax.all_gather(vectors, "wide", axis=1, tiled=True)
    in_bias = lax.all_gather(in_bias, AXES, axis=0, tiled=True)
    places = jnp.arange(PLACES)
    pieces = vectors.reshape(NARROW, 2, WIDE, 64).transpose(2, 0, 1, 3).reshape(PLACES, 2, 64)
    small = jax.vmap(small_block)(
        pieces, in_bias.reshape(PLACES, 64), places // NARROW, places % NARROW
    )
    tiles = (WIDE, NARROW)
    first = jax.vmap(first_block)(
        canonical(whole(w_query), tiles),
        canonical(whole(w_key), tiles),
        canonical(whole(w_value), tiles),
        canonical(whole(position_table), tiles),
        small,
    )
    second = jax.vmap(second_block)(
        canonical(whole(w_out), tiles),
        canonical(whole(w_in), tiles),
        canonical(whole(w_back), tiles),
    )
    output, stream, back, inner, outer = layer(
        False, inputs, segment_ids, cotangent, fours(first), fours(second)
    )

    def joined(pair):
        return jnp.concatenate([pair[0], pair[1].astype(F32)], axis=0)

    def summed(array):
        array = lax.psum_scatter(array, "wide", scatter_dimension=0, tiled=True)
        return lax.psum_scatter(array, "narrow", scatter_dimension=1, tiled=True)

    back, inner, outer = joined(back), joined(inner), joined(outer)
    back = jax.vmap(turned)(back)
    grad_in = inner[:, 0:4].transpose(0, 2, 1, 3).reshape(PLACES, 64, 512)
    vec = outer.reshape(WIDE, NARROW, 272, 128)[::2, 0, 256:264]
    vec = vec.transpose(1, 0, 2).reshape(8, 512)
    vec = lax.psum_scatter(vec, "wide", scatter_dimension=1, tiled=True)
    vec = lax.psum_scatter(vec, "narrow", scatter_dimension=0, tiled=True)
    bins = outer.reshape(WIDE, NARROW, 272, 128)[::4, 0, 264:272].reshape(2048)
    bins = lax.psum_scatter(bins, AXES, scatter_dimension=0, tiled=True)
    return (
        output,
        stream,
        summed(uncanonical(outer[:, 0:64], 512, 512)),
        summed(uncanonical(outer[:, 64:128], 512, 512)),
        summed(uncanonical(outer[:, 128:192], 512, 512)),
        summed(uncanonical(inner[:, 4], 512, 512)),
        summed(uncanonical(grad_in, 512, 2048)),
        summed(uncanonical(back, 2048, 512)),
        summed(uncanonical(outer[:, 192:256], 512, 512)),
        vec,
        bins,
    )


def solution(mesh):
    matrix = P("wide", "narrow")
    rows = P(AXES, None, None)
    direct = mesh.shape["wide"] == WIDE and mesh.shape["narrow"] == NARROW
    return jax.shard_map(
        per_device if direct else per_device_any,
        mesh=mesh,
        in_specs=(
            rows,
            P(AXES, None),
            rows,
            matrix,
            matrix,
            matrix,
            matrix,
            matrix,
            matrix,
            matrix,
            P("narrow", "wide"),
            P(AXES),
        ),
        out_specs=(
            rows,
            rows,
            matrix,
            matrix,
            matrix,
            matrix,
            matrix,
            matrix,
            matrix,
            P("narrow", "wide"),
            P(AXES),
        ),
        check_vma=False,
    )
```

```python
from functools import partial
import math

import jax
import jax.numpy as jnp
from jax import lax
from jax.experimental import pallas as pl
from jax.experimental.pallas import tpu as pltpu
from jax.sharding import PartitionSpec as P

HEADS = 8
EPSILON = 1e-05
AXES = ("wide", "narrow")
F32 = jnp.float32
BF16 = jnp.bfloat16
NEG = -1e30
VMEM_LIMIT = 60 * 1024 * 1024

WIDE = 8
NARROW = 4
PLACES = WIDE * NARROW
HALF = PLACES // 2

Z1, Z0, X, Y = 16, 8, 4, 2
ORDER_FIRST = ((Z1, X, Y, Z0), (Z0, Y, X, Z1))
ORDER_SECOND = ((Z1, Z0, X, Y), (Z0, Z1, Y, X))


def nn(left, right):
    return lax.dot_general(left, right, (((1,), (0,)), ((), ())), preferred_element_type=F32)


def nt(left, right):
    return lax.dot_general(left, right, (((1,), (1,)), ((), ())), preferred_element_type=F32)


def block_masks(order, core):
    masks = []
    for block in range(HALF):
        total = 0
        for step in range(4):
            if block >> step & 1:
                total ^= order[core][step]
        masks.append(total)
    return masks


def place_of(order, me, half, block):
    core = (me & 1) ^ half
    apart = jnp.where(core == 0, block_masks(order, 0)[block], block_masks(order, 1)[block])
    where = me ^ half ^ apart
    return where >> 2, where & 3


def block_at(order, me, apart):
    half = apart & 1
    core = (me & 1) ^ half
    first, second = (block_masks(order, of).index(apart ^ half) for of in range(2))
    return jnp.where(core == 0, first, second)


def pairs(order, step):
    found = []
    for place in range(PLACES):
        mask = 1 if step == 4 else order[place & 1][step]
        found.append((place, place ^ mask))
    return found


def my_place():
    return lax.axis_index("wide") * NARROW + lax.axis_index("narrow")


def head_masks(rows):
    lane = lax.broadcasted_iota(jnp.int32, (rows, 128), 1)
    return lane < 64


def stack_heads(pair_rows, low):
    zero = jnp.zeros_like(pair_rows)
    return jnp.concatenate(
        [jnp.where(low, pair_rows, zero), jnp.where(low, zero, pair_rows)], axis=0
    )


def fill_bias(segments_ref, bias_ref, windows):
    length = segments_ref.shape[1]
    for window in range(windows):
        row = segments_ref[window : window + 1, :].astype(F32)
        column = jnp.transpose(jnp.broadcast_to(row, (128, length)))
        for block in range(length // 128):
            start = max(0, block * 128 - 256)
            stop = block * 128 + 128
            span = stop - start
            key_at = start + lax.broadcasted_iota(jnp.int32, (span, 128), 0)
            query_at = block * 128 + lax.broadcasted_iota(jnp.int32, (span, 128), 1)
            same = column[start:stop, :] == row[:, block * 128 : block * 128 + 128]
            bias_ref[window, block, 0:span, :] = jnp.where(
                (key_at <= query_at) & same, 0.0, NEG
            )


def block_spans(windows, length):
    spans = []
    for window in range(windows):
        for block in range(length // 128):
            stop = block * 128 + 128
            start = max(0, stop - 384)
            base = window * length
            spans.append(
                (
                    window,
                    block,
                    slice(base + stop - 128, base + stop),
                    slice(base + start, base + stop),
                    stop - start,
                )
            )
    return spans


def part_lanes(pair, part):
    return pl.ds(pl.multiple_of(pair * 384 + part * 128, 128), 128)


def wait_whole(ref, sem):
    pltpu.make_async_copy(ref, ref, sem).wait()


def attend_kernel(
    direct,
    segments_ref,
    x_ref,
    p0_ref,
    p1_ref,
    p2_ref,
    p3_ref,
    qkv_ref,
    attended_ref,
    lse_ref,
    passed_ref,
    mixed_ref,
    vec_ref,
    bin_ref,
    weights,
    bias,
    table,
    small,
    sems,
):
    windows, length = segments_ref.shape
    me = my_place() if direct else jnp.int32(0)
    for block in range(HALF):
        for half in range(2):
            source = ((p0_ref, p1_ref), (p2_ref, p3_ref))[half][block // 8].at[block % 8]
            wide, narrow = place_of(ORDER_FIRST, me, half, block)
            rows = pl.ds(pl.multiple_of(wide * 64, 64), 64)
            pltpu.make_async_copy(
                source.at[pl.ds(192, 64)],
                table.at[rows, pl.ds(pl.multiple_of(narrow * 128, 128), 128)],
                sems.at[0],
            ).start()
            pltpu.make_async_copy(
                source.at[pl.ds(256, 16)], small.at[half * HALF + block], sems.at[1]
            ).start()
            for part in range(3):
                pltpu.make_async_copy(
                    source.at[pl.ds(part * 64, 64)],
                    weights.at[
                        rows, pl.ds(pl.multiple_of(narrow * 384 + part * 128, 128), 128)
                    ],
                    sems.at[2],
                ).start()
    fill_bias(segments_ref, bias, windows)
    wait_whole(table, sems.at[0])
    for window in range(windows):
        rows = slice(window * length, (window + 1) * length)
        passed = x_ref[rows, :].astype(F32) + table[...].astype(F32)
        passed_ref[rows, :] = passed
        mixed_ref[rows, :] = passed.astype(BF16)
    wait_whole(small, sems.at[1])
    vec_ref[...] = jnp.zeros_like(vec_ref)
    bin_ref[...] = jnp.zeros_like(bin_ref)
    for half in range(2):
        for block in range(HALF):
            wide, narrow = place_of(ORDER_FIRST, me, half, block)
            piece = small[half * HALF + block].astype(F32)
            vec_ref[wide // 2] += piece[0:8]
            bin_ref[wide // 4] += piece[8:16]
    wait_whole(weights, sems.at[2])
    low = head_masks(128)

    for chunk in range(6):
        projected = nn(mixed_ref[...], weights[:, chunk * 256 : chunk * 256 + 256])
        for side in range(2):
            pair, part = divmod(chunk * 2 + side, 3)
            own = projected[:, side * 128 : side * 128 + 128]
            if part != 1:
                own = own + vec_ref[pair, part // 2 : part // 2 + 1, :]
            own = own.astype(BF16)
            if part == 0:
                own = own * BF16(0.125)
            qkv_ref[:, (chunk * 2 + side) * 128 : (chunk * 2 + side) * 128 + 128] = own

    def per_pair(pair, unused):
        spans = block_spans(windows, length)
        turned_values = [
            jnp.transpose(
                qkv_ref[window * length : (window + 1) * length, part_lanes(pair, 2)]
            )
            for window in range(windows)
        ]
        scores = []
        for window, block, here, there, span in spans:
            query = stack_heads(qkv_ref[here, part_lanes(pair, 0)], low)
            mask = bias[window, block, 0:span, :]
            scores.append(
                nt(qkv_ref[there, part_lanes(pair, 1)], query)
                + jnp.concatenate([mask, mask], axis=1)
            )
        shares = []
        for (window, block, here, there, span), score in zip(spans, scores):
            peak = jnp.max(score, axis=0, keepdims=True)
            weight = jnp.exp(score - peak)
            total = jnp.sum(weight, axis=0, keepdims=True)
            shares.append((weight * (1.0 / total)).astype(BF16))
            lse_ref[pair, window, block : block + 1, :] = peak + jnp.log(total)
        for (window, block, here, there, span), share in zip(spans, shares):
            stop = block * 128 + 128
            joined = nn(turned_values[window][:, stop - span : stop], share)
            both = jnp.concatenate([joined[0:64, 0:128], joined[64:128, 128:256]], axis=0)
            attended_ref[here, pl.ds(pl.multiple_of(pair * 128, 128), 128)] = jnp.transpose(
                both
            ).astype(BF16)
        return unused

    lax.fori_loop(0, NARROW, per_pair, 0)


def norm_parts(values):
    average = jnp.mean(values, axis=-1, keepdims=True)
    centred = values - average
    variance = jnp.mean(centred * centred, axis=-1, keepdims=True)
    scale = lax.rsqrt(variance + EPSILON)
    return centred * scale, scale


def norm_back(hat, scale, gains, grad):
    scaled = grad * gains
    first = jnp.mean(scaled, axis=-1, keepdims=True)
    second = jnp.mean(scaled * hat, axis=-1, keepdims=True)
    return scale * (scaled - first - hat * second)


def vec_row(vec_ref, row):
    return jnp.concatenate([vec_ref[tile, row : row + 1, :] for tile in range(4)], axis=1)


def column_sum(values):
    return jnp.sum(values, axis=0, keepdims=True)


GELU_SCALE = math.sqrt(2.0 / math.pi)


def gelu_both(pre):
    square = pre * pre
    curve = jnp.tanh(pre * (GELU_SCALE + (GELU_SCALE * 0.044715) * square))
    half = 0.5 + 0.5 * curve
    slope = (0.5 * pre) * (1.0 - curve * curve) * (
        GELU_SCALE + (3.0 * GELU_SCALE * 0.044715) * square
    )
    return pre * half, half + slope


def load_second(me, blocks, w_out, w_in, w_back, sems):
    for block in range(HALF):
        for half in range(2):
            source = blocks[half * 2 + block // 8].at[block % 8]
            wide, narrow = place_of(ORDER_SECOND, me, half, block)
            rows = pl.ds(pl.multiple_of(wide * 64, 64), 64)
            columns = pl.ds(pl.multiple_of(narrow * 128, 128), 128)
            pltpu.make_async_copy(source.at[0], w_out.at[rows, columns], sems.at[0]).start()
            pltpu.make_async_copy(
                source.at[pl.ds(1, 4)], w_in.at[pl.ds(narrow * 4, 4), rows, :], sems.at[1]
            ).start()
            pltpu.make_async_copy(
                source.at[pl.ds(5, 4)], w_back.at[pl.ds(wide * 4, 4), :, columns], sems.at[2]
            ).start()


def w_in_columns(w_in, chunk):
    return jnp.concatenate([w_in[chunk * 2], w_in[chunk * 2 + 1]], axis=1)


def rows_at(step, rows):
    return pl.ds(pl.multiple_of(step * rows, rows), rows)


def forward_kernel(
    direct,
    attended_ref,
    passed_ref,
    cotangent_ref,
    vec_ref,
    bin_ref,
    p0_ref,
    p1_ref,
    p2_ref,
    p3_ref,
    output_ref,
    slope_ref,
    grad_second_ref,
    first_ref,
    low_t,
    keep_ref,
    send_ref,
    sums_ref,
    w_out,
    w_in,
    w_back,
    active,
    grad_t,
    sems,
):
    rows = ROWS
    me = my_place() if direct else jnp.int32(0)
    load_second(me, (p0_ref, p1_ref, p2_ref, p3_ref), w_out, w_in, w_back, sems)
    sums_ref[...] = jnp.zeros_like(sums_ref)
    wait_whole(w_out, sems.at[0])
    wait_whole(w_in, sems.at[1])
    wait_whole(w_back, sems.at[2])

    def per_rows(step, unused):
        here = rows_at(step, rows)
        first_sum = passed_ref[here, :] + nn(attended_ref[here, :], w_out[...]) + vec_row(vec_ref, 2)
        first_ref[here, :] = first_sum
        hat, unused_scale = norm_parts(first_sum)
        hidden = hat * vec_row(vec_ref, 4) + vec_row(vec_ref, 5)
        low = hidden.astype(BF16)
        turned_low = jnp.transpose(low)
        for wide in range(WIDE):
            low_t[wide ^ (me >> 2), :, here] = turned_low[wide * 64 : wide * 64 + 64, :]
        total = hidden + vec_row(vec_ref, 3)
        for chunk in range(8):
            offset = jnp.concatenate(
                [
                    bin_ref[chunk // 4, 2 * (chunk % 4) + part : 2 * (chunk % 4) + part + 1, :]
                    for part in range(2)
                ],
                axis=1,
            )
            columns = slice(chunk * 256, chunk * 256 + 256)
            value, slope = gelu_both(nn(low, w_in_columns(w_in, chunk)) + offset)
            value = value.astype(BF16)
            active[here, columns] = value
            slope_ref[here, columns] = slope
            total += nn(value, w_back[chunk * 4 : chunk * 4 + 4].reshape(256, 512))
        hat, scale = norm_parts(total)
        gains = vec_row(vec_ref, 6)
        output_ref[here, :] = (hat * gains + vec_row(vec_ref, 7)).astype(BF16)
        cotangent = cotangent_ref[here, :].astype(F32)
        grad_second = norm_back(hat, scale, gains, cotangent)
        grad_second_ref[here, :] = grad_second
        grad_low = grad_second.astype(BF16)
        turned_low = jnp.transpose(grad_low)
        for narrow in range(NARROW):
            grad_t[narrow ^ (me & 3), :, here] = turned_low[narrow * 128 : narrow * 128 + 128, :]
        sums_ref[0:1, :] += column_sum(grad_low.astype(F32))
        sums_ref[1:2, :] += column_sum(cotangent * hat)
        sums_ref[2:3, :] += column_sum(cotangent)
        return unused

    total_rows = attended_ref.shape[0]
    lax.fori_loop(0, total_rows // rows, per_rows, 0)
    grads = grad_t[...].reshape(512, total_rows)
    for wide in range(WIDE):
        columns = pl.ds(pl.multiple_of((wide ^ (me >> 2)) * 256, 256), 256)
        piece = nn(grads, active[:, columns])
        for narrow in range(NARROW):
            target = (keep_ref, send_ref)[narrow & 1]
            block = block_at(ORDER_SECOND, me, wide * NARROW + narrow)
            own = piece[narrow * 128 : narrow * 128 + 128]
            target[block, 0:128, :] = own[:, 0:128].astype(target.dtype)
            target[block, 128:256, :] = own[:, 128:256].astype(target.dtype)


def backward_kernel(
    direct,
    slope_ref,
    grad_second_ref,
    first_ref,
    low_t,
    attended_ref,
    vec_ref,
    w_out,
    w_in,
    w_back,
    grad_first_ref,
    grad_attended_ref,
    keep_ref,
    send_ref,
    sums_ref,
    bin_sums_ref,
    grad_pre,
    grad_branch,
    attended_t,
):
    rows = ROWS
    me = my_place() if direct else jnp.int32(0)
    sums_ref[...] = jnp.zeros_like(sums_ref)
    bin_sums_ref[...] = jnp.zeros_like(bin_sums_ref)

    def per_rows(step, unused):
        here = rows_at(step, rows)
        turned_low = jnp.transpose(attended_ref[here, :])
        for wide in range(WIDE):
            attended_t[wide ^ (me >> 2), :, here] = turned_low[wide * 64 : wide * 64 + 64, :]
        grad_hidden = grad_second_ref[here, :]
        grad_low = grad_hidden.astype(BF16)
        for chunk in range(8):
            columns = slice(chunk * 256, chunk * 256 + 256)
            weight = w_back[chunk * 4 : chunk * 4 + 4].reshape(256, 512)
            grad = (nt(grad_low, weight) * slope_ref[here, columns]).astype(BF16)
            grad_pre[here, columns] = grad
            grad_hidden += nt(grad, w_in_columns(w_in, chunk))
            sums = column_sum(grad.astype(F32))
            for part in range(2):
                row = 2 * (chunk % 4) + part
                bin_sums_ref[chunk // 4, row : row + 1, :] += sums[:, part * 128 : part * 128 + 128]
        hat, scale = norm_parts(first_ref[here, :])
        gains = vec_row(vec_ref, 4)
        grad_first = norm_back(hat, scale, gains, grad_hidden)
        grad_first_ref[here, :] = grad_first
        branch = grad_first.astype(BF16)
        grad_branch[here, :] = branch
        sums_ref[0:1, :] += column_sum(branch.astype(F32))
        sums_ref[1:2, :] += column_sum(grad_hidden * hat)
        sums_ref[2:3, :] += column_sum(grad_hidden)
        grad_attended_ref[here, :] = nt(branch, w_out[...]).astype(BF16)
        return unused

    total_rows = attended_ref.shape[0]
    lax.fori_loop(0, total_rows // rows, per_rows, 0)
    lows = low_t[...].reshape(512, total_rows)
    joined = attended_t[...].reshape(512, total_rows)
    for narrow in range(NARROW):
        target = (keep_ref, send_ref)[narrow & 1]
        at = narrow ^ (me & 3)
        for part in range(2):
            columns = pl.ds(pl.multiple_of(at * 512 + part * 256, 256), 256)
            piece = nn(lows, grad_pre[:, columns])
            for wide in range(WIDE):
                block = block_at(ORDER_SECOND, me, wide * NARROW + narrow)
                own = piece[wide * 64 : wide * 64 + 64]
                target[block, part * 2] = own[:, 0:128].astype(target.dtype)
                target[block, part * 2 + 1] = own[:, 128:256].astype(target.dtype)
        piece = nn(joined, grad_branch[:, pl.ds(pl.multiple_of(at * 128, 128), 128)])
        for wide in range(WIDE):
            block = block_at(ORDER_SECOND, me, wide * NARROW + narrow)
            target[block, 4] = piece[wide * 64 : wide * 64 + 64].astype(target.dtype)


def attend_back_kernel(
    direct,
    qkv_ref,
    grad_attended_ref,
    lse_ref,
    mixed_ref,
    grad_first_ref,
    sums_a_ref,
    sums_b_ref,
    bin_sums_ref,
    weights,
    bias,
    stream_ref,
    keep_ref,
    send_ref,
    mixed_t,
    grads,
    stream,
    vec_sums,
):
    windows, blocks = lse_ref.shape[1:3]
    length = blocks * 128
    me = my_place() if direct else jnp.int32(0)
    turned_low = jnp.transpose(mixed_ref[...])
    for wide in range(WIDE):
        mixed_t[wide ^ (me >> 2), :, :] = turned_low[wide * 64 : wide * 64 + 64, :]
    vec_sums[...] = jnp.zeros_like(vec_sums)
    for tile in range(4):
        lanes = slice(tile * 128, tile * 128 + 128)
        vec_sums[tile, 2:3, :] = sums_b_ref[0:1, lanes]
        vec_sums[tile, 3:4, :] = sums_a_ref[0:1, lanes]
        vec_sums[tile, 4:6, :] = sums_b_ref[1:3, lanes]
        vec_sums[tile, 6:8, :] = sums_a_ref[1:3, lanes]
    low = head_masks(128)

    def per_pair(core, upper, unused):
        apart = 2 * upper + core
        pair = (me & 3) ^ apart
        spans = block_spans(windows, length)
        lanes = pl.ds(pl.multiple_of(pair * 128, 128), 128)
        turned_keys = [
            jnp.transpose(
                qkv_ref[window * length : (window + 1) * length, part_lanes(pair, 1)]
            )
            for window in range(windows)
        ]
        queries, aboves, scores, grad_shares = [], [], [], []
        for window, block, here, there, span in spans:
            queries.append(stack_heads(qkv_ref[here, part_lanes(pair, 0)], low))
            aboves.append(stack_heads(grad_attended_ref[here, lanes], low))
            mask = bias[window, block, 0:span, :]
            mask = jnp.concatenate([mask, mask], axis=1)
            scores.append(
                nt(qkv_ref[there, part_lanes(pair, 1)], queries[-1])
                + (mask - lse_ref[pair, window, block : block + 1, :])
            )
            grad_shares.append(nt(qkv_ref[there, part_lanes(pair, 2)], aboves[-1]))
        shares, grad_scores = [], []
        for score, grad_share in zip(scores, grad_shares):
            share = jnp.exp(score)
            inner = jnp.sum(share * grad_share, axis=0, keepdims=True)
            shares.append(share.astype(BF16))
            grad_scores.append((share * (grad_share - inner)).astype(BF16))
        grad_keys = [[None] * (length // 128) for window in range(windows)]
        grad_values = [[None] * (length // 128) for window in range(windows)]
        for at, (window, block, here, there, span) in enumerate(spans):
            stop = block * 128 + 128
            for found, sums in (
                (nn(grad_scores[at], queries[at]), grad_keys[window]),
                (nn(shares[at], aboves[at]), grad_values[window]),
            ):
                for part in range(span // 128):
                    of = block - span // 128 + 1 + part
                    piece = found[part * 128 : part * 128 + 128]
                    sums[of] = piece if sums[of] is None else sums[of] + piece
            joined = nn(turned_keys[window][:, stop - span : stop], grad_scores[at])
            both = jnp.concatenate([joined[0:64, 0:128], joined[64:128, 128:256]], axis=0)
            grad = (jnp.transpose(both) * 0.125).astype(BF16)
            grads[here, part_lanes(apart, 0)] = grad
            vec_sums[pair, 0:1, :] += column_sum(grad.astype(F32))
        for window, block, here, there, span in spans:
            grads[here, part_lanes(apart, 1)] = grad_keys[window][block].astype(BF16)
            grad = grad_values[window][block].astype(BF16)
            grads[here, part_lanes(apart, 2)] = grad
            vec_sums[pair, 1:2, :] += column_sum(grad.astype(F32))
        return unused

    lax.fori_loop(0, 2, partial(per_pair, 0), 0)
    lax.fori_loop(0, 2, partial(per_pair, 1), 0)
    turned_mixed = mixed_t[...].reshape(512, windows * length)
    for chunk in range(6):
        weight_grads = nn(turned_mixed, grads[:, chunk * 256 : chunk * 256 + 256])
        for side in range(2):
            apart, part = divmod(chunk * 2 + side, 3)
            target = (keep_ref, send_ref)[apart & 1]
            for wide in range(WIDE):
                block = block_at(ORDER_FIRST, me, wide * NARROW + apart)
                target[block, part * 64 : part * 64 + 64, :] = weight_grads[
                    wide * 64 : wide * 64 + 64, side * 128 : side * 128 + 128
                ].astype(target.dtype)
    for row in range(0, length, 256):
        total = None
        for window in range(windows):
            rows = slice(window * length + row, window * length + row + 256)
            sums = grad_first_ref[rows, :]
            for apart in range(NARROW):
                lanes = pl.ds(pl.multiple_of(((me & 3) ^ apart) * 384, 128), 384)
                sums += nt(grads[rows, apart * 384 : apart * 384 + 384], weights[:, lanes])
            stream_ref[rows, :] = sums.astype(BF16)
            total = sums if total is None else total + sums
        stream[row : row + 256, :] = total
    for half, target in ((0, keep_ref), (1, send_ref)):
        for block in range(HALF):
            wide, narrow = place_of(ORDER_FIRST, me, half, block)
            target[block, 192:256, :] = stream[
                pl.ds(pl.multiple_of(wide * 64, 64), 64),
                pl.ds(pl.multiple_of(narrow * 128, 128), 128),
            ].astype(target.dtype)
            target[block, 256:264, :] = vec_sums[wide // 2].astype(target.dtype)
            target[block, 264:272, :] = bin_sums_ref[wide // 4].astype(target.dtype)


def doubled(row):
    return jnp.concatenate([row, row], axis=1)


def pack_kernel(
    w_query_ref,
    w_key_ref,
    w_value_ref,
    w_out_ref,
    w_in_ref,
    w_back_ref,
    table_ref,
    vectors_ref,
    in_bias_ref,
    first_ref,
    second_ref,
):
    wide, narrow = lax.axis_index("wide"), lax.axis_index("narrow")
    first_ref[0:64, :] = w_query_ref[...]
    first_ref[64:128, :] = w_key_ref[...]
    first_ref[128:192, :] = w_value_ref[...]
    first_ref[192:256, :] = table_ref[...]
    row = lax.broadcasted_iota(jnp.int32, (8, 128), 0)
    side = lax.broadcasted_iota(jnp.int32, (8, 128), 1) // 64
    vectors = doubled(vectors_ref[...].astype(F32))
    spread = jnp.where(row % 2 == 0, vectors[0:1], vectors[1:2])
    upper = jnp.where((row // 2 == narrow) & (side == wide % 2), spread, 0.0)
    spread = doubled(in_bias_ref[...].astype(F32))
    lower = jnp.where(
        (row == 2 * (wide % 4) + narrow // 2) & (side == narrow % 2), spread, 0.0
    )
    first_ref[256:272, :] = jnp.concatenate([upper, lower], axis=0).astype(BF16)
    second_ref[0] = w_out_ref[...]
    for part in range(4):
        second_ref[1 + part] = w_in_ref[:, part * 128 : part * 128 + 128]
        second_ref[5 + part] = w_back_ref[part * 64 : part * 64 + 64, :]


def finish_kernel(
    held_ref, came_ref, query_ref, key_ref, value_ref, table_ref, vectors_ref, in_bias_ref
):
    wide, narrow = lax.axis_index("wide"), lax.axis_index("narrow")
    total = held_ref[0] + came_ref[0].astype(F32)
    query_ref[...] = total[0:64]
    key_ref[...] = total[64:128]
    value_ref[...] = total[128:192]
    table_ref[...] = total[192:256]
    row = lax.broadcasted_iota(jnp.int32, (8, 128), 0)

    def side_of(rows, second):
        return jnp.where(second == 1, rows[:, 64:128], rows[:, 0:64])

    def row_of(rows, which):
        return column_sum(jnp.where(row == which, rows, 0.0))

    vectors = jnp.concatenate(
        [row_of(total[256:264], narrow * 2), row_of(total[256:264], narrow * 2 + 1)], axis=0
    )
    vectors_ref[...] = side_of(vectors, wide % 2)
    bins = row_of(total[264:272], 2 * (wide % 4) + narrow // 2)
    in_bias_ref[...] = side_of(bins, narrow % 2)


def vmem():
    return pl.BlockSpec(memory_space=pltpu.VMEM)


def hbm():
    return pl.BlockSpec(memory_space=pl.ANY)


def cost(macs, touched):
    return pl.CostEstimate(flops=2 * macs, bytes_accessed=touched, transcendentals=0)


def params(mebibytes):
    return pltpu.CompilerParams(vmem_limit_bytes=mebibytes << 20)


def shape(dims, dtype):
    return jax.ShapeDtypeStruct(dims, dtype)


def attend_call(direct, segments, x, blocks):
    windows, length = segments.shape
    total = windows * length
    return pl.pallas_call(
        partial(attend_kernel, direct),
        out_shape=(
            shape((total, 1536), BF16),
            shape((total, 512), BF16),
            shape((NARROW, windows, length // 128, 256), F32),
            shape((total, 512), F32),
            shape((total, 512), BF16),
            shape((4, 8, 128), F32),
            shape((2, 8, 128), F32),
            shape((512, 1536), BF16),
            shape((windows, length // 128, 384, 128), F32),
        ),
        in_specs=[vmem(), vmem()] + [hbm()] * 4,
        out_specs=tuple([vmem()] * 9),
        scratch_shapes=[
            pltpu.VMEM((512, 512), BF16),
            pltpu.VMEM((PLACES, 16, 128), BF16),
            pltpu.SemaphoreType.DMA((3,)),
        ],
        compiler_params=params(ATTEND_MIB),
        cost_estimate=cost(6000 << 20, 12 << 20),
        name="attend",
    )(segments, x, *blocks)


ROWS = 512
ATTEND_MIB = 24
FORWARD_MIB = 20
BACKWARD_MIB = 16
ATTEND_BACK_MIB = 32


def forward_call(direct, attended, passed, cotangent, vec, bins, blocks):
    total = attended.shape[0]
    return pl.pallas_call(
        partial(forward_kernel, direct),
        out_shape=(
            shape((total, 512), BF16),
            shape((total, 2048), F32),
            shape((total, 512), F32),
            shape((total, 512), F32),
            shape((WIDE, 64, total), BF16),
            shape((HALF, 256, 128), F32),
            shape((HALF, 256, 128), BF16),
            shape((8, 512), F32),
            shape((512, 512), BF16),
            shape((16, 512, 128), BF16),
            shape((32, 64, 512), BF16),
        ),
        in_specs=[vmem()] * 5 + [hbm()] * 4,
        out_specs=tuple([vmem()] * 11),
        scratch_shapes=[
            pltpu.VMEM((total, 2048), BF16),
            pltpu.VMEM((NARROW, 128, total), BF16),
            pltpu.SemaphoreType.DMA((3,)),
        ],
        compiler_params=params(FORWARD_MIB),
        cost_estimate=cost(6000 << 20, 24 << 20),
        name="forward",
    )(attended, passed, cotangent, vec, bins, *blocks)


def backward_call(direct, slope, grad_second, first_sum, low_t, attended, vec, weights):
    total = attended.shape[0]
    return pl.pallas_call(
        partial(backward_kernel, direct),
        out_shape=(
            shape((total, 512), F32),
            shape((total, 512), BF16),
            shape((HALF, 5, 64, 128), F32),
            shape((HALF, 5, 64, 128), BF16),
            shape((8, 512), F32),
            shape((2, 8, 128), F32),
        ),
        in_specs=[vmem()] * 9,
        out_specs=tuple([vmem()] * 6),
        scratch_shapes=[
            pltpu.VMEM((total, 2048), BF16),
            pltpu.VMEM((total, 512), BF16),
            pltpu.VMEM((WIDE, 64, total), BF16),
        ],
        compiler_params=params(BACKWARD_MIB),
        cost_estimate=cost(7000 << 20, 24 << 20),
        name="backward",
    )(slope, grad_second, first_sum, low_t, attended, vec, *weights)


def attend_back_call(direct, qkv, grad_attended, lse, mixed, grad_first, sums, weights, bias):
    windows, blocks = lse.shape[1:3]
    length = blocks * 128
    total = windows * length
    return pl.pallas_call(
        partial(attend_back_kernel, direct),
        out_shape=(
            shape((total, 512), BF16),
            shape((HALF, 272, 128), F32),
            shape((HALF, 272, 128), BF16),
        ),
        in_specs=[vmem()] * 10,
        out_specs=(vmem(), vmem(), vmem()),
        scratch_shapes=[
            pltpu.VMEM((WIDE, 64, total), BF16),
            pltpu.VMEM((total, 1536), BF16),
            pltpu.VMEM((length, 512), F32),
            pltpu.VMEM((4, 8, 128), F32),
        ],
        compiler_params=params(ATTEND_BACK_MIB),
        cost_estimate=cost(7000 << 20, 16 << 20),
        name="attend_back",
    )(qkv, grad_attended, lse, mixed, grad_first, *sums, weights, bias)


def pack_call(*shards):
    return pl.pallas_call(
        pack_kernel,
        out_shape=(shape((272, 128), BF16), shape((9, 64, 128), BF16)),
        in_specs=[vmem()] * 9,
        out_specs=(vmem(), vmem()),
        name="pack",
    )(*shards)


def finish_call(held, came):
    return pl.pallas_call(
        finish_kernel,
        out_shape=tuple([shape((64, 128), F32)] * 4 + [shape((2, 64), F32), shape((1, 64), F32)]),
        in_specs=[vmem()] * 2,
        out_specs=tuple([vmem()] * 6),
        name="finish",
    )(held, came)


def swap(array, order, step):
    return lax.ppermute(array, AXES, pairs(order, step))


def after(value, *others):
    return lax.optimization_barrier((value,) + others)[0]


def grow(held, order, step):
    return jnp.concatenate([held, swap(held, order, step)], axis=0)


def start_halving(keep, send, order):
    return keep, swap(send, order, 4)


def halve(held, came, order, step):
    size = 1 << step
    upper = (held[size:] + came[size:].astype(F32)).astype(BF16)
    lower = held[:size] + came[:size].astype(F32)
    return lower, swap(upper, order, step)


def small_block(vectors, in_bias, wide, narrow):
    row = lax.broadcasted_iota(jnp.int32, (8, 128), 0)
    side = lax.broadcasted_iota(jnp.int32, (8, 128), 1) // 64
    spread = jnp.tile(vectors, (4, 2))
    first = jnp.where((row // 2 == narrow) & (side == wide % 2), spread, 0)
    spread = jnp.tile(in_bias[None], (8, 2))
    second = jnp.where((row == 2 * (wide % 4) + narrow // 2) & (side == narrow % 2), spread, 0)
    return jnp.concatenate([first, second], axis=0).astype(BF16)


def first_block(w_query, w_key, w_value, table, small):
    return jnp.concatenate([w_query, w_key, w_value, table, small], axis=0)


def second_block(w_out, w_in, w_back):
    return jnp.concatenate(
        [w_out[None]]
        + [w_in[None, :, part * 128 : part * 128 + 128] for part in range(4)]
        + [w_back.reshape(4, 64, 128)],
        axis=0,
    )


def turned(total):
    return jnp.concatenate([total[0:128].T, total[128:256].T], axis=0)


def per_device(
    inputs,
    segment_ids,
    cotangent,
    w_query,
    w_key,
    w_value,
    w_out,
    w_in,
    w_back,
    position_table,
    vectors,
    in_bias,
):
    windows, length, features = inputs.shape
    rows = windows * length
    x = inputs.reshape(rows, features)
    early, late = pack_call(
        w_query, w_key, w_value, w_out, w_in, w_back, position_table, vectors, in_bias[None]
    )
    early, late = early[None], late[None]
    early = grow(early, ORDER_FIRST, 0)
    for step in range(3):
        early_came = swap(early, ORDER_FIRST, step + 1)
        late_came = swap(late, ORDER_SECOND, step)
        early_came, late_came = lax.optimization_barrier((early_came, late_came))
        if step < 2:
            early = jnp.concatenate([early, early_came], axis=0)
        else:
            early_far = early_came
        late = jnp.concatenate([late, late_came], axis=0)
    first = (early, early_far, swap(early, ORDER_FIRST, 4), swap(early_far, ORDER_FIRST, 4))
    late_far = swap(late, ORDER_SECOND, 3)
    qkv, attended, lse, passed, mixed, vec, bins, w_qkv, bias = attend_call(
        True, segment_ids, after(x, late), first
    )
    late_far = after(late_far, attended)
    second = (late, late_far, swap(late, ORDER_SECOND, 4), swap(late_far, ORDER_SECOND, 4))
    output, slope, grad_second, first_sum, low_t, keep_back, send_back, sums_a, *whole = forward_call(
        True, attended, passed, cotangent.reshape(rows, features), vec, bins, second
    )
    back = start_halving(keep_back, send_back, ORDER_SECOND)
    grad_first, grad_attended, keep_in, send_in, sums_b, bin_sums = backward_call(
        True, slope, grad_second, first_sum, low_t, attended, vec, whole
    )
    back = halve(*back, ORDER_SECOND, 3)
    inner = start_halving(keep_in, send_in, ORDER_SECOND)
    stream, keep_first, send_first = attend_back_call(
        True,
        qkv,
        after(grad_attended, back[0]),
        lse,
        mixed,
        grad_first,
        (sums_a, sums_b, bin_sums),
        w_qkv,
        bias,
    )
    keep_first, send_first, back_came, inner_came = lax.optimization_barrier(
        (keep_first, send_first, back[1], inner[1])
    )
    outer = start_halving(keep_first, send_first, ORDER_FIRST)
    back = halve(back[0], back_came, ORDER_SECOND, 2)
    inner = halve(inner[0], inner_came, ORDER_SECOND, 3)
    for step in (2, 1, 0):
        outer = halve(*outer, ORDER_FIRST, step + 1)
        if step > 0:
            back = halve(back[0], after(back[1], outer[1]), ORDER_SECOND, step - 1)
        inner = halve(inner[0], after(inner[1], outer[1]), ORDER_SECOND, step)
    outer = halve(*outer, ORDER_FIRST, 0)
    back = back[0][0] + back[1][0].astype(F32)
    inner = inner[0][0] + inner[1][0].astype(F32)
    grad_query, grad_key, grad_value, grad_table, vec, bins = finish_call(*outer)
    return (
        output.reshape(inputs.shape),
        stream.reshape(inputs.shape),
        grad_query,
        grad_key,
        grad_value,
        inner[4],
        jnp.concatenate([inner[part] for part in range(4)], axis=1),
        turned(back),
        grad_table,
        vec,
        bins[0],
    )


def listed(order):
    return block_masks(order, 0) + [1 ^ mask for mask in block_masks(order, 1)]


def canonical(array, axis_tiles):
    rows, columns = array.shape
    across, along = axis_tiles
    return (
        array.reshape(across, rows // across, along, columns // along)
        .transpose(0, 2, 1, 3)
        .reshape(PLACES, rows // across, columns // along)
    )


def uncanonical(blocks, rows, columns):
    return (
        blocks.reshape(WIDE, NARROW, rows // WIDE, columns // NARROW)
        .transpose(0, 2, 1, 3)
        .reshape(rows, columns)
    )


def per_device_any(
    inputs,
    segment_ids,
    cotangent,
    w_query,
    w_key,
    w_value,
    w_out,
    w_in,
    w_back,
    position_table,
    vectors,
    in_bias,
):
    def whole(array):
        array = lax.all_gather(array, "narrow", axis=1, tiled=True)
        return lax.all_gather(array, "wide", axis=0, tiled=True)

    def fours(blocks, order):
        blocks = jnp.stack([blocks[place] for place in listed(order)])
        return tuple(blocks[at * 8 : at * 8 + 8] for at in range(4))

    vectors = lax.all_gather(vectors, "narrow", axis=0, tiled=True)
    vectors = lax.all_gather(vectors, "wide", axis=1, tiled=True)
    in_bias = lax.all_gather(in_bias, AXES, axis=0, tiled=True)
    places = jnp.arange(PLACES)
    pieces = vectors.reshape(NARROW, 2, WIDE, 64).transpose(2, 0, 1, 3).reshape(PLACES, 2, 64)
    small = jax.vmap(small_block)(
        pieces, in_bias.reshape(PLACES, 64), places // NARROW, places % NARROW
    )
    tiles = (WIDE, NARROW)
    first = jax.vmap(first_block)(
        canonical(whole(w_query), tiles),
        canonical(whole(w_key), tiles),
        canonical(whole(w_value), tiles),
        canonical(whole(position_table), tiles),
        small,
    )
    second = jax.vmap(second_block)(
        canonical(whole(w_out), tiles),
        canonical(whole(w_in), tiles),
        canonical(whole(w_back), tiles),
    )
    windows, length, features = inputs.shape
    rows = windows * length
    first, second = fours(first, ORDER_FIRST), fours(second, ORDER_SECOND)
    qkv, attended, lse, passed, mixed, vec, bins, w_qkv, bias = attend_call(
        False, segment_ids, inputs.reshape(rows, features), first
    )
    output, slope, grad_second, first_sum, low_t, keep_back, send_back, sums_a, *whole_w = forward_call(
        False, attended, passed, cotangent.reshape(rows, features), vec, bins, second
    )
    grad_first, grad_attended, keep_in, send_in, sums_b, bin_sums = backward_call(
        False, slope, grad_second, first_sum, low_t, attended, vec, whole_w
    )
    stream, keep_first, send_first = attend_back_call(
        False,
        qkv,
        grad_attended,
        lse,
        mixed,
        grad_first,
        (sums_a, sums_b, bin_sums),
        w_qkv,
        bias,
    )

    def joined(pair, order):
        both = jnp.concatenate([pair[0], pair[1].astype(F32)], axis=0)
        return jnp.stack([both[listed(order).index(place)] for place in range(PLACES)])

    def summed(array):
        array = lax.psum_scatter(array, "wide", scatter_dimension=0, tiled=True)
        return lax.psum_scatter(array, "narrow", scatter_dimension=1, tiled=True)

    back = joined((keep_back, send_back), ORDER_SECOND)
    inner = joined((keep_in, send_in), ORDER_SECOND)
    outer = joined((keep_first, send_first), ORDER_FIRST)
    back = jax.vmap(turned)(back)
    grad_in = inner[:, 0:4].transpose(0, 2, 1, 3).reshape(PLACES, 64, 512)
    vec = outer.reshape(WIDE, NARROW, 272, 128)[::2, 0, 256:264]
    vec = vec.transpose(1, 0, 2).reshape(8, 512)
    vec = lax.psum_scatter(vec, "wide", scatter_dimension=1, tiled=True)
    vec = lax.psum_scatter(vec, "narrow", scatter_dimension=0, tiled=True)
    bins = outer.reshape(WIDE, NARROW, 272, 128)[::4, 0, 264:272].reshape(2048)
    bins = lax.psum_scatter(bins, AXES, scatter_dimension=0, tiled=True)
    return (
        output.reshape(inputs.shape),
        stream.reshape(inputs.shape),
        summed(uncanonical(outer[:, 0:64], 512, 512)),
        summed(uncanonical(outer[:, 64:128], 512, 512)),
        summed(uncanonical(outer[:, 128:192], 512, 512)),
        summed(uncanonical(inner[:, 4], 512, 512)),
        summed(uncanonical(grad_in, 512, 2048)),
        summed(uncanonical(back, 2048, 512)),
        summed(uncanonical(outer[:, 192:256], 512, 512)),
        vec,
        bins,
    )


def solution(mesh):
    matrix = P("wide", "narrow")
    rows = P(AXES, None, None)
    direct = mesh.shape["wide"] == WIDE and mesh.shape["narrow"] == NARROW
    return jax.shard_map(
        per_device if direct else per_device_any,
        mesh=mesh,
        in_specs=(
            rows,
            P(AXES, None),
            rows,
            matrix,
            matrix,
            matrix,
            matrix,
            matrix,
            matrix,
            matrix,
            P("narrow", "wide"),
            P(AXES),
        ),
        out_specs=(
            rows,
            rows,
            matrix,
            matrix,
            matrix,
            matrix,
            matrix,
            matrix,
            matrix,
            P("narrow", "wide"),
            P(AXES),
        ),
        check_vma=False,
    )
```

```python
from functools import partial
import math

import jax
import jax.numpy as jnp
from jax import lax
from jax.experimental import pallas as pl
from jax.experimental.pallas import tpu as pltpu
from jax.sharding import PartitionSpec as P

HEADS = 8
EPSILON = 1e-05
AXES = ("wide", "narrow")
F32 = jnp.float32
BF16 = jnp.bfloat16
NEG = -1e30
VMEM_LIMIT = 60 * 1024 * 1024

WIDE = 8
NARROW = 4
PLACES = WIDE * NARROW
HALF = PLACES // 2

Z1, Z0, X, Y = 16, 8, 4, 2
ORDER_FIRST = ((X, Y, Z1, Z0), (X, Y, Z0, Z1))
ORDER_SECOND = ((Z1, Z0, X, Y), (Z0, Z1, Y, X))
ORDER_OUTER = ((Z1, Z0, X, Y), (Z0, Z1, Y, X))
ORDER_INNER = ((X, Z1, Z0, Y), (Y, Z0, Z1, X))
ORDER_BACK = ((Z1, Y, Z0, X), (Y, X, Z1, Z0))


def nn(left, right):
    return lax.dot_general(left, right, (((1,), (0,)), ((), ())), preferred_element_type=F32)


def nt(left, right):
    return lax.dot_general(left, right, (((1,), (1,)), ((), ())), preferred_element_type=F32)


def block_masks(order, core):
    masks = []
    for block in range(HALF):
        total = 0
        for step in range(4):
            if block >> step & 1:
                total ^= order[core][step]
        masks.append(total)
    return masks


def place_of(order, me, half, block):
    core = (me & 1) ^ half
    apart = jnp.where(core == 0, block_masks(order, 0)[block], block_masks(order, 1)[block])
    where = me ^ half ^ apart
    return where >> 2, where & 3


def block_at(order, me, apart):
    half = apart & 1
    core = (me & 1) ^ half
    first, second = (block_masks(order, of).index(apart ^ half) for of in range(2))
    return jnp.where(core == 0, first, second)


def pairs(order, step):
    found = []
    for place in range(PLACES):
        mask = 1 if step == 4 else order[place & 1][step]
        found.append((place, place ^ mask))
    return found


def my_place():
    return lax.axis_index("wide") * NARROW + lax.axis_index("narrow")


def head_masks(rows):
    lane = lax.broadcasted_iota(jnp.int32, (rows, 128), 1)
    return lane < 64


def stack_heads(pair_rows, low):
    zero = jnp.zeros_like(pair_rows)
    return jnp.concatenate(
        [jnp.where(low, pair_rows, zero), jnp.where(low, zero, pair_rows)], axis=0
    )


def fill_bias(segments_ref, bias_ref, windows):
    length = segments_ref.shape[1]
    for window in range(windows):
        row = segments_ref[window : window + 1, :].astype(F32)
        column = jnp.transpose(jnp.broadcast_to(row, (128, length)))
        for block in range(length // 128):
            start = max(0, block * 128 - 256)
            stop = block * 128 + 128
            span = stop - start
            key_at = start + lax.broadcasted_iota(jnp.int32, (span, 128), 0)
            query_at = block * 128 + lax.broadcasted_iota(jnp.int32, (span, 128), 1)
            same = column[start:stop, :] == row[:, block * 128 : block * 128 + 128]
            bias_ref[window, block, 0:span, :] = jnp.where(
                (key_at <= query_at) & same, 0.0, NEG
            )


def block_spans(windows, length):
    spans = []
    for window in range(windows):
        for block in range(length // 128):
            stop = block * 128 + 128
            start = max(0, stop - 384)
            base = window * length
            spans.append(
                (
                    window,
                    block,
                    slice(base + stop - 128, base + stop),
                    slice(base + start, base + stop),
                    stop - start,
                )
            )
    return spans


def part_lanes(pair, part):
    return pl.ds(pl.multiple_of(pair * 384 + part * 128, 128), 128)


def wait_whole(ref, sem):
    pltpu.make_async_copy(ref, ref, sem).wait()


def attend_kernel(
    direct,
    segments_ref,
    x_ref,
    p0_ref,
    p1_ref,
    p2_ref,
    p3_ref,
    qkv_ref,
    attended_ref,
    lse_ref,
    passed_ref,
    mixed_ref,
    vec_ref,
    bin_ref,
    weights,
    bias,
    qkv,
    table,
    small,
    sems,
):
    windows, length = segments_ref.shape
    me = my_place() if direct else jnp.int32(0)
    for block in range(HALF):
        for half in range(2):
            source = ((p0_ref, p1_ref), (p2_ref, p3_ref))[half][block // 8].at[block % 8]
            wide, narrow = place_of(ORDER_FIRST, me, half, block)
            rows = pl.ds(pl.multiple_of(wide * 64, 64), 64)
            pltpu.make_async_copy(
                source.at[pl.ds(192, 64)],
                table.at[rows, pl.ds(pl.multiple_of(narrow * 128, 128), 128)],
                sems.at[0],
            ).start()
            pltpu.make_async_copy(
                source.at[pl.ds(256, 16)], small.at[half * HALF + block], sems.at[1]
            ).start()
            for part in range(3):
                pltpu.make_async_copy(
                    source.at[pl.ds(part * 64, 64)],
                    weights.at[
                        rows, pl.ds(pl.multiple_of(narrow * 384 + part * 128, 128), 128)
                    ],
                    sems.at[2],
                ).start()
    fill_bias(segments_ref, bias, windows)
    wait_whole(table, sems.at[0])
    for window in range(windows):
        rows = slice(window * length, (window + 1) * length)
        passed = x_ref[rows, :].astype(F32) + table[...].astype(F32)
        passed_ref[rows, :] = passed
        mixed_ref[rows, :] = passed.astype(BF16)
    wait_whole(small, sems.at[1])
    vec_ref[...] = jnp.zeros_like(vec_ref)
    bin_ref[...] = jnp.zeros_like(bin_ref)
    for half in range(2):
        for block in range(HALF):
            wide, narrow = place_of(ORDER_FIRST, me, half, block)
            piece = small[half * HALF + block].astype(F32)
            vec_ref[wide // 2] += piece[0:8]
            bin_ref[wide // 4] += piece[8:16]
    wait_whole(weights, sems.at[2])
    low = head_masks(128)

    for chunk in range(6):
        projected = nn(mixed_ref[...], weights[:, chunk * 256 : chunk * 256 + 256])
        for side in range(2):
            pair, part = divmod(chunk * 2 + side, 3)
            own = projected[:, side * 128 : side * 128 + 128]
            if part != 1:
                own = own + vec_ref[pair, part // 2 : part // 2 + 1, :]
            own = own.astype(BF16)
            if part == 0:
                own = own * BF16(0.125)
            qkv[:, (chunk * 2 + side) * 128 : (chunk * 2 + side) * 128 + 128] = own

    leave = pltpu.make_async_copy(qkv, qkv_ref, sems.at[3])
    leave.start()

    def per_pair(pair, unused):
        spans = block_spans(windows, length)
        turned_values = [
            jnp.transpose(
                qkv[window * length : (window + 1) * length, part_lanes(pair, 2)]
            )
            for window in range(windows)
        ]
        scores = []
        for window, block, here, there, span in spans:
            query = stack_heads(qkv[here, part_lanes(pair, 0)], low)
            mask = bias[window, block, 0:span, :]
            scores.append(
                nt(qkv[there, part_lanes(pair, 1)], query)
                + jnp.concatenate([mask, mask], axis=1)
            )
        shares = []
        for (window, block, here, there, span), score in zip(spans, scores):
            peak = jnp.max(score, axis=0, keepdims=True)
            weight = jnp.exp(score - peak)
            total = jnp.sum(weight, axis=0, keepdims=True)
            shares.append((weight * (1.0 / total)).astype(BF16))
            lse_ref[pair, window, block : block + 1, :] = peak + jnp.log(total)
        for (window, block, here, there, span), share in zip(spans, shares):
            stop = block * 128 + 128
            joined = nn(turned_values[window][:, stop - span : stop], share)
            both = jnp.concatenate([joined[0:64, 0:128], joined[64:128, 128:256]], axis=0)
            attended_ref[here, pl.ds(pl.multiple_of(pair * 128, 128), 128)] = jnp.transpose(
                both
            ).astype(BF16)
        return unused

    lax.fori_loop(0, NARROW, per_pair, 0)
    leave.wait()


def norm_parts(values):
    average = jnp.mean(values, axis=-1, keepdims=True)
    centred = values - average
    variance = jnp.mean(centred * centred, axis=-1, keepdims=True)
    scale = lax.rsqrt(variance + EPSILON)
    return centred * scale, scale


def norm_back(hat, scale, gains, grad):
    scaled = grad * gains
    first = jnp.mean(scaled, axis=-1, keepdims=True)
    second = jnp.mean(scaled * hat, axis=-1, keepdims=True)
    return scale * (scaled - first - hat * second)


def vec_row(vec_ref, row):
    return jnp.concatenate([vec_ref[tile, row : row + 1, :] for tile in range(4)], axis=1)


def column_sum(values):
    return jnp.sum(values, axis=0, keepdims=True)


GELU_SCALE = math.sqrt(2.0 / math.pi)


def gelu_both(pre):
    square = pre * pre
    curve = jnp.tanh(pre * (GELU_SCALE + (GELU_SCALE * 0.044715) * square))
    half = 0.5 + 0.5 * curve
    slope = (0.5 * pre) * (1.0 - curve * curve) * (
        GELU_SCALE + (3.0 * GELU_SCALE * 0.044715) * square
    )
    return pre * half, half + slope


def load_second(me, blocks, w_out, w_in, w_back, sems):
    for block in range(HALF):
        for half in range(2):
            source = blocks[half * 2 + block // 8].at[block % 8]
            wide, narrow = place_of(ORDER_SECOND, me, half, block)
            rows = pl.ds(pl.multiple_of(wide * 64, 64), 64)
            columns = pl.ds(pl.multiple_of(narrow * 128, 128), 128)
            pltpu.make_async_copy(source.at[0], w_out.at[rows, columns], sems.at[0]).start()
            pltpu.make_async_copy(
                source.at[pl.ds(1, 4)], w_in.at[pl.ds(narrow * 4, 4), rows, :], sems.at[1]
            ).start()
            pltpu.make_async_copy(
                source.at[pl.ds(5, 4)], w_back.at[pl.ds(wide * 4, 4), :, columns], sems.at[2]
            ).start()


def w_in_columns(w_in, chunk):
    return jnp.concatenate([w_in[chunk * 2], w_in[chunk * 2 + 1]], axis=1)


def rows_at(step, rows):
    return pl.ds(pl.multiple_of(step * rows, rows), rows)


def forward_kernel(
    direct,
    attended_ref,
    passed_ref,
    cotangent_ref,
    vec_ref,
    bin_ref,
    p0_ref,
    p1_ref,
    p2_ref,
    p3_ref,
    output_ref,
    slope_ref,
    grad_second_ref,
    first_ref,
    low_t,
    keep_ref,
    send_ref,
    sums_ref,
    w_out,
    w_in,
    w_back,
    active,
    grad_t,
    sems,
):
    rows = ROWS
    me = my_place() if direct else jnp.int32(0)
    load_second(me, (p0_ref, p1_ref, p2_ref, p3_ref), w_out, w_in, w_back, sems)
    sums_ref[...] = jnp.zeros_like(sums_ref)
    wait_whole(w_out, sems.at[0])
    wait_whole(w_in, sems.at[1])
    wait_whole(w_back, sems.at[2])

    def per_rows(step, unused):
        here = rows_at(step, rows)
        first_sum = passed_ref[here, :] + nn(attended_ref[here, :], w_out[...]) + vec_row(vec_ref, 2)
        first_ref[here, :] = first_sum
        hat, unused_scale = norm_parts(first_sum)
        hidden = hat * vec_row(vec_ref, 4) + vec_row(vec_ref, 5)
        low = hidden.astype(BF16)
        turned_low = jnp.transpose(low)
        for wide in range(WIDE):
            low_t[wide ^ (me >> 2), :, here] = turned_low[wide * 64 : wide * 64 + 64, :]
        total = hidden + vec_row(vec_ref, 3)
        for chunk in range(8):
            offset = jnp.concatenate(
                [
                    bin_ref[chunk // 4, 2 * (chunk % 4) + part : 2 * (chunk % 4) + part + 1, :]
                    for part in range(2)
                ],
                axis=1,
            )
            columns = slice(chunk * 256, chunk * 256 + 256)
            value, slope = gelu_both(nn(low, w_in_columns(w_in, chunk)) + offset)
            value = value.astype(BF16)
            active[here, columns] = value
            slope_ref[here, columns] = slope
            total += nn(value, w_back[chunk * 4 : chunk * 4 + 4].reshape(256, 512))
        hat, scale = norm_parts(total)
        gains = vec_row(vec_ref, 6)
        output_ref[here, :] = (hat * gains + vec_row(vec_ref, 7)).astype(BF16)
        cotangent = cotangent_ref[here, :].astype(F32)
        grad_second = norm_back(hat, scale, gains, cotangent)
        grad_second_ref[here, :] = grad_second
        grad_low = grad_second.astype(BF16)
        turned_low = jnp.transpose(grad_low)
        for narrow in range(NARROW):
            grad_t[narrow ^ (me & 3), :, here] = turned_low[narrow * 128 : narrow * 128 + 128, :]
        sums_ref[0:1, :] += column_sum(grad_low.astype(F32))
        sums_ref[1:2, :] += column_sum(cotangent * hat)
        sums_ref[2:3, :] += column_sum(cotangent)
        return unused

    total_rows = attended_ref.shape[0]
    lax.fori_loop(0, total_rows // rows, per_rows, 0)
    grads = grad_t[...].reshape(512, total_rows)
    for wide in range(WIDE):
        columns = pl.ds(pl.multiple_of((wide ^ (me >> 2)) * 256, 256), 256)
        piece = nn(grads, active[:, columns])
        for narrow in range(NARROW):
            target = (keep_ref, send_ref)[narrow & 1]
            block = block_at(ORDER_BACK, me, wide * NARROW + narrow)
            own = piece[narrow * 128 : narrow * 128 + 128]
            target[block, 0:128, :] = own[:, 0:128].astype(target.dtype)
            target[block, 128:256, :] = own[:, 128:256].astype(target.dtype)


def backward_kernel(
    direct,
    slope_ref,
    grad_second_ref,
    first_ref,
    low_t,
    attended_ref,
    vec_ref,
    w_out,
    w_in,
    w_back,
    grad_first_ref,
    grad_attended_ref,
    keep_ref,
    send_ref,
    sums_ref,
    bin_sums_ref,
    grad_pre,
    grad_branch,
    attended_t,
):
    rows = ROWS
    me = my_place() if direct else jnp.int32(0)
    sums_ref[...] = jnp.zeros_like(sums_ref)
    bin_sums_ref[...] = jnp.zeros_like(bin_sums_ref)

    def per_rows(step, unused):
        here = rows_at(step, rows)
        turned_low = jnp.transpose(attended_ref[here, :])
        for wide in range(WIDE):
            attended_t[wide ^ (me >> 2), :, here] = turned_low[wide * 64 : wide * 64 + 64, :]
        grad_hidden = grad_second_ref[here, :]
        grad_low = grad_hidden.astype(BF16)
        for chunk in range(8):
            columns = slice(chunk * 256, chunk * 256 + 256)
            weight = w_back[chunk * 4 : chunk * 4 + 4].reshape(256, 512)
            grad = (nt(grad_low, weight) * slope_ref[here, columns]).astype(BF16)
            grad_pre[here, columns] = grad
            grad_hidden += nt(grad, w_in_columns(w_in, chunk))
            sums = column_sum(grad.astype(F32))
            for part in range(2):
                row = 2 * (chunk % 4) + part
                bin_sums_ref[chunk // 4, row : row + 1, :] += sums[:, part * 128 : part * 128 + 128]
        hat, scale = norm_parts(first_ref[here, :])
        gains = vec_row(vec_ref, 4)
        grad_first = norm_back(hat, scale, gains, grad_hidden)
        grad_first_ref[here, :] = grad_first
        branch = grad_first.astype(BF16)
        grad_branch[here, :] = branch
        sums_ref[0:1, :] += column_sum(branch.astype(F32))
        sums_ref[1:2, :] += column_sum(grad_hidden * hat)
        sums_ref[2:3, :] += column_sum(grad_hidden)
        grad_attended_ref[here, :] = nt(branch, w_out[...]).astype(BF16)
        return unused

    total_rows = attended_ref.shape[0]
    lax.fori_loop(0, total_rows // rows, per_rows, 0)
    lows = low_t[...].reshape(512, total_rows)
    joined = attended_t[...].reshape(512, total_rows)
    for narrow in range(NARROW):
        target = (keep_ref, send_ref)[narrow & 1]
        at = narrow ^ (me & 3)
        for part in range(2):
            columns = pl.ds(pl.multiple_of(at * 512 + part * 256, 256), 256)
            piece = nn(lows, grad_pre[:, columns])
            for wide in range(WIDE):
                block = block_at(ORDER_INNER, me, wide * NARROW + narrow)
                own = piece[wide * 64 : wide * 64 + 64]
                target[block, part * 2] = own[:, 0:128].astype(target.dtype)
                target[block, part * 2 + 1] = own[:, 128:256].astype(target.dtype)
        piece = nn(joined, grad_branch[:, pl.ds(pl.multiple_of(at * 128, 128), 128)])
        for wide in range(WIDE):
            block = block_at(ORDER_INNER, me, wide * NARROW + narrow)
            target[block, 4] = piece[wide * 64 : wide * 64 + 64].astype(target.dtype)


def attend_back_kernel(
    direct,
    segments_ref,
    qkv_ref,
    grad_attended_ref,
    lse_ref,
    grads,
    vec_sums,
    bias,
):
    windows, length = segments_ref.shape
    me = my_place() if direct else jnp.int32(0)
    fill_bias(segments_ref, bias, windows)
    vec_sums[...] = jnp.zeros_like(vec_sums)
    low = head_masks(128)

    def per_pair(apart, unused):
        pair = (me & 3) ^ apart
        spans = block_spans(windows, length)
        lanes = pl.ds(pl.multiple_of(pair * 128, 128), 128)
        turned_keys = [
            jnp.transpose(
                qkv_ref[window * length : (window + 1) * length, part_lanes(pair, 1)]
            )
            for window in range(windows)
        ]
        queries, aboves, scores, grad_shares = [], [], [], []
        for window, block, here, there, span in spans:
            queries.append(stack_heads(qkv_ref[here, part_lanes(pair, 0)], low))
            aboves.append(stack_heads(grad_attended_ref[here, lanes], low))
            mask = bias[window, block, 0:span, :]
            mask = jnp.concatenate([mask, mask], axis=1)
            scores.append(
                nt(qkv_ref[there, part_lanes(pair, 1)], queries[-1])
                + (mask - lse_ref[pair, window, block : block + 1, :])
            )
            grad_shares.append(nt(qkv_ref[there, part_lanes(pair, 2)], aboves[-1]))
        shares, grad_scores = [], []
        for score, grad_share in zip(scores, grad_shares):
            share = jnp.exp(score)
            inner = jnp.sum(share * grad_share, axis=0, keepdims=True)
            shares.append(share.astype(BF16))
            grad_scores.append((share * (grad_share - inner)).astype(BF16))
        grad_keys = [[None] * (length // 128) for window in range(windows)]
        grad_values = [[None] * (length // 128) for window in range(windows)]
        for at, (window, block, here, there, span) in enumerate(spans):
            stop = block * 128 + 128
            for found, sums in (
                (nn(grad_scores[at], queries[at]), grad_keys[window]),
                (nn(shares[at], aboves[at]), grad_values[window]),
            ):
                for part in range(span // 128):
                    of = block - span // 128 + 1 + part
                    piece = found[part * 128 : part * 128 + 128]
                    sums[of] = piece if sums[of] is None else sums[of] + piece
            joined = nn(turned_keys[window][:, stop - span : stop], grad_scores[at])
            both = jnp.concatenate([joined[0:64, 0:128], joined[64:128, 128:256]], axis=0)
            grad = (jnp.transpose(both) * 0.125).astype(BF16)
            grads[here, part_lanes(apart, 0)] = grad
            vec_sums[pair, 0:1, :] += column_sum(grad.astype(F32))
        for window, block, here, there, span in spans:
            grads[here, part_lanes(apart, 1)] = grad_keys[window][block].astype(BF16)
            grad = grad_values[window][block].astype(BF16)
            grads[here, part_lanes(apart, 2)] = grad
            vec_sums[pair, 1:2, :] += column_sum(grad.astype(F32))
        return unused

    lax.fori_loop(0, NARROW, per_pair, 0)


def project_back_kernel(
    direct,
    windows,
    grads,
    mixed_ref,
    grad_first_ref,
    pair_sums_ref,
    sums_a_ref,
    sums_b_ref,
    bin_sums_ref,
    weights,
    stream_ref,
    keep_ref,
    send_ref,
    mixed_t,
    stream,
    vec_sums,
):
    length = mixed_ref.shape[0] // windows
    me = my_place() if direct else jnp.int32(0)
    turned_low = jnp.transpose(mixed_ref[...])
    for wide in range(WIDE):
        mixed_t[wide ^ (me >> 2), :, :] = turned_low[wide * 64 : wide * 64 + 64, :]
    for tile in range(4):
        lanes = slice(tile * 128, tile * 128 + 128)
        vec_sums[tile, 0:2, :] = pair_sums_ref[tile, 0:2, :]
        vec_sums[tile, 2:3, :] = sums_b_ref[0:1, lanes]
        vec_sums[tile, 3:4, :] = sums_a_ref[0:1, lanes]
        vec_sums[tile, 4:6, :] = sums_b_ref[1:3, lanes]
        vec_sums[tile, 6:8, :] = sums_a_ref[1:3, lanes]
    turned_mixed = mixed_t[...].reshape(512, windows * length)
    for chunk in range(6):
        weight_grads = nn(turned_mixed, grads[:, chunk * 256 : chunk * 256 + 256])
        for side in range(2):
            apart, part = divmod(chunk * 2 + side, 3)
            target = (keep_ref, send_ref)[apart & 1]
            for wide in range(WIDE):
                block = block_at(ORDER_OUTER, me, wide * NARROW + apart)
                target[block, part * 64 : part * 64 + 64, :] = weight_grads[
                    wide * 64 : wide * 64 + 64, side * 128 : side * 128 + 128
                ].astype(target.dtype)
    for row in range(0, length, 256):
        total = None
        for window in range(windows):
            rows = slice(window * length + row, window * length + row + 256)
            sums = grad_first_ref[rows, :]
            for apart in range(NARROW):
                lanes = pl.ds(pl.multiple_of(((me & 3) ^ apart) * 384, 128), 384)
                sums += nt(grads[rows, apart * 384 : apart * 384 + 384], weights[:, lanes])
            stream_ref[rows, :] = sums.astype(BF16)
            total = sums if total is None else total + sums
        stream[row : row + 256, :] = total
    for half, target in ((0, keep_ref), (1, send_ref)):
        for block in range(HALF):
            wide, narrow = place_of(ORDER_OUTER, me, half, block)
            target[block, 192:256, :] = stream[
                pl.ds(pl.multiple_of(wide * 64, 64), 64),
                pl.ds(pl.multiple_of(narrow * 128, 128), 128),
            ].astype(target.dtype)
            target[block, 256:264, :] = vec_sums[wide // 2].astype(target.dtype)
            target[block, 264:272, :] = bin_sums_ref[wide // 4].astype(target.dtype)


def doubled(row):
    return jnp.concatenate([row, row], axis=1)


def pack_kernel(
    w_query_ref,
    w_key_ref,
    w_value_ref,
    w_out_ref,
    w_in_ref,
    w_back_ref,
    table_ref,
    vectors_ref,
    in_bias_ref,
    first_ref,
    second_ref,
):
    wide, narrow = lax.axis_index("wide"), lax.axis_index("narrow")
    first_ref[0:64, :] = w_query_ref[...]
    first_ref[64:128, :] = w_key_ref[...]
    first_ref[128:192, :] = w_value_ref[...]
    first_ref[192:256, :] = table_ref[...]
    row = lax.broadcasted_iota(jnp.int32, (8, 128), 0)
    side = lax.broadcasted_iota(jnp.int32, (8, 128), 1) // 64
    vectors = doubled(vectors_ref[...].astype(F32))
    spread = jnp.where(row % 2 == 0, vectors[0:1], vectors[1:2])
    upper = jnp.where((row // 2 == narrow) & (side == wide % 2), spread, 0.0)
    spread = doubled(in_bias_ref[...].astype(F32))
    lower = jnp.where(
        (row == 2 * (wide % 4) + narrow // 2) & (side == narrow % 2), spread, 0.0
    )
    first_ref[256:272, :] = jnp.concatenate([upper, lower], axis=0).astype(BF16)
    second_ref[0] = w_out_ref[...]
    for part in range(4):
        second_ref[1 + part] = w_in_ref[:, part * 128 : part * 128 + 128]
        second_ref[5 + part] = w_back_ref[part * 64 : part * 64 + 64, :]


def finish_kernel(
    outer_ref,
    outer_came_ref,
    inner_ref,
    inner_came_ref,
    back_ref,
    back_came_ref,
    query_ref,
    key_ref,
    value_ref,
    out_ref,
    in_ref,
    w_back_ref,
    table_ref,
    vectors_ref,
    in_bias_ref,
):
    wide, narrow = lax.axis_index("wide"), lax.axis_index("narrow")
    total = back_ref[0] + back_came_ref[0].astype(F32)
    w_back_ref[0:128, :] = jnp.transpose(total[0:128])
    w_back_ref[128:256, :] = jnp.transpose(total[128:256])
    for part in range(4):
        in_ref[:, part * 128 : part * 128 + 128] = inner_ref[0, part] + inner_came_ref[
            0, part
        ].astype(F32)
    out_ref[...] = inner_ref[0, 4] + inner_came_ref[0, 4].astype(F32)
    total = outer_ref[0] + outer_came_ref[0].astype(F32)
    query_ref[...] = total[0:64]
    key_ref[...] = total[64:128]
    value_ref[...] = total[128:192]
    table_ref[...] = total[192:256]
    row = lax.broadcasted_iota(jnp.int32, (8, 128), 0)

    def side_of(rows, second):
        return jnp.where(second == 1, rows[:, 64:128], rows[:, 0:64])

    def row_of(rows, which):
        return column_sum(jnp.where(row == which, rows, 0.0))

    vectors = jnp.concatenate(
        [row_of(total[256:264], narrow * 2), row_of(total[256:264], narrow * 2 + 1)], axis=0
    )
    vectors_ref[...] = side_of(vectors, wide % 2)
    bins = row_of(total[264:272], 2 * (wide % 4) + narrow // 2)
    in_bias_ref[...] = side_of(bins, narrow % 2)


def vmem():
    return pl.BlockSpec(memory_space=pltpu.VMEM)


def hbm():
    return pl.BlockSpec(memory_space=pl.ANY)


def cost(macs, touched):
    return pl.CostEstimate(flops=2 * macs, bytes_accessed=touched, transcendentals=0)


def params(mebibytes):
    return pltpu.CompilerParams(vmem_limit_bytes=mebibytes << 20)


def shape(dims, dtype):
    return jax.ShapeDtypeStruct(dims, dtype)


def near(dims, dtype):
    return pltpu.VMEM(dims, dtype)


def kept(array):
    return pltpu.with_memory_space_constraint(array, pltpu.VMEM)


def attend_call(direct, segments, x, blocks):
    windows, length = segments.shape
    total = windows * length
    return pl.pallas_call(
        partial(attend_kernel, direct),
        out_shape=(
            pltpu.HBM((total, 1536), BF16),
            shape((total, 512), BF16),
            shape((NARROW, windows, length // 128, 256), F32),
            near((total, 512), F32),
            shape((total, 512), BF16),
            shape((4, 8, 128), F32),
            shape((2, 8, 128), F32),
            shape((512, 1536), BF16),
        ),
        in_specs=[vmem(), vmem()] + [hbm()] * 4,
        out_specs=(pl.BlockSpec(memory_space=pltpu.HBM),) + tuple([vmem()] * 7),
        scratch_shapes=[
            pltpu.VMEM((windows, length // 128, 384, 128), F32),
            pltpu.VMEM((total, 1536), BF16),
            pltpu.VMEM((512, 512), BF16),
            pltpu.VMEM((PLACES, 16, 128), BF16),
            pltpu.SemaphoreType.DMA((4,)),
        ],
        compiler_params=params(ATTEND_MIB),
        cost_estimate=cost(6000 << 20, 12 << 20),
        name="attend",
    )(segments, x, *blocks)


ROWS = 512
ATTEND_MIB = 24
FORWARD_MIB = 14
BACKWARD_MIB = 14
ATTEND_BACK_MIB = 20
PROJECT_BACK_MIB = 16


def forward_call(direct, attended, passed, cotangent, vec, bins, blocks):
    total = attended.shape[0]
    return pl.pallas_call(
        partial(forward_kernel, direct),
        out_shape=(
            shape((total, 512), BF16),
            near((total, 2048), F32),
            near((total, 512), F32),
            near((total, 512), F32),
            near((WIDE, 64, total), BF16),
            near((HALF, 256, 128), F32),
            near((HALF, 256, 128), BF16),
            shape((8, 512), F32),
            near((512, 512), BF16),
            near((16, 512, 128), BF16),
            near((32, 64, 512), BF16),
        ),
        in_specs=[vmem()] * 5 + [hbm()] * 4,
        out_specs=tuple([vmem()] * 11),
        scratch_shapes=[
            pltpu.VMEM((total, 2048), BF16),
            pltpu.VMEM((NARROW, 128, total), BF16),
            pltpu.SemaphoreType.DMA((3,)),
        ],
        compiler_params=params(FORWARD_MIB),
        cost_estimate=cost(6000 << 20, 24 << 20),
        input_output_aliases={1: 3},
        name="forward",
    )(attended, kept(passed), cotangent, vec, bins, *blocks)


def backward_call(direct, slope, grad_second, first_sum, low_t, attended, vec, weights):
    total = attended.shape[0]
    return pl.pallas_call(
        partial(backward_kernel, direct),
        out_shape=(
            shape((total, 512), F32),
            shape((total, 512), BF16),
            shape((HALF, 5, 64, 128), F32),
            shape((HALF, 5, 64, 128), BF16),
            shape((8, 512), F32),
            shape((2, 8, 128), F32),
        ),
        in_specs=[vmem()] * 9,
        out_specs=tuple([vmem()] * 6),
        scratch_shapes=[
            pltpu.VMEM((total, 2048), BF16),
            pltpu.VMEM((total, 512), BF16),
            pltpu.VMEM((WIDE, 64, total), BF16),
        ],
        compiler_params=params(BACKWARD_MIB),
        cost_estimate=cost(7000 << 20, 24 << 20),
        name="backward",
    )(
        kept(slope),
        kept(grad_second),
        kept(first_sum),
        kept(low_t),
        attended,
        vec,
        *(kept(weight) for weight in weights),
    )


def attend_back_call(direct, segments, qkv, grad_attended, lse):
    windows, length = segments.shape
    total = windows * length
    return pl.pallas_call(
        partial(attend_back_kernel, direct),
        out_shape=(shape((total, 1536), BF16), shape((4, 8, 128), F32)),
        in_specs=[vmem()] * 4,
        out_specs=(vmem(), vmem()),
        scratch_shapes=[pltpu.VMEM((windows, length // 128, 384, 128), F32)],
        compiler_params=params(ATTEND_BACK_MIB),
        cost_estimate=cost(4000 << 20, 8 << 20),
        name="attend_back",
    )(segments, qkv, grad_attended, lse)


def project_back_call(direct, windows, grads, mixed, grad_first, sums, weights):
    total = mixed.shape[0]
    return pl.pallas_call(
        partial(project_back_kernel, direct, windows),
        out_shape=(
            shape((total, 512), BF16),
            shape((HALF, 272, 128), F32),
            shape((HALF, 272, 128), BF16),
        ),
        in_specs=[vmem()] * 8,
        out_specs=(vmem(), vmem(), vmem()),
        scratch_shapes=[
            pltpu.VMEM((WIDE, 64, total), BF16),
            pltpu.VMEM((total // windows, 512), F32),
            pltpu.VMEM((4, 8, 128), F32),
        ],
        compiler_params=params(PROJECT_BACK_MIB),
        cost_estimate=cost(3000 << 20, 8 << 20),
        name="project_back",
    )(grads, mixed, grad_first, *sums, weights)


def pack_call(*shards):
    return pl.pallas_call(
        pack_kernel,
        out_shape=(near((272, 128), BF16), near((9, 64, 128), BF16)),
        in_specs=[vmem()] * 9,
        out_specs=(vmem(), vmem()),
        name="pack",
    )(*shards)


def join_kernel(first_ref, second_ref, joined_ref):
    half = first_ref.shape[0]
    joined_ref[0:half] = first_ref[...]
    joined_ref[half:] = second_ref[...]


def joined_blocks(first, second):
    count = 2 * first.shape[0]
    return pl.pallas_call(
        join_kernel,
        out_shape=near((count,) + first.shape[1:], first.dtype),
        in_specs=[vmem()] * 2,
        out_specs=vmem(),
        compiler_params=params(2),
        name="join",
    )(kept(first), kept(second))


def finish_call(outer, inner, back):
    block = shape((64, 128), F32)
    return pl.pallas_call(
        finish_kernel,
        out_shape=(
            block,
            block,
            block,
            block,
            shape((64, 512), F32),
            shape((256, 128), F32),
            block,
            shape((2, 64), F32),
            shape((1, 64), F32),
        ),
        in_specs=[vmem()] * 6,
        out_specs=tuple([vmem()] * 9),
        compiler_params=params(6),
        name="finish",
    )(*outer, *inner, *back)


def swap(array, order, step):
    return lax.ppermute(array, AXES, pairs(order, step))


def after(value, *others):
    return lax.optimization_barrier((value,) + others)[0]


def grow(held, order, step):
    return jnp.concatenate([held, swap(held, order, step)], axis=0)


def start_halving(keep, send, order):
    return keep, swap(send, order, 4)


def halve(held, came, order, step):
    size = 1 << step
    upper = (held[size:] + came[size:].astype(F32)).astype(BF16)
    lower = held[:size] + came[:size].astype(F32)
    return lower, swap(upper, order, step)


def small_block(vectors, in_bias, wide, narrow):
    row = lax.broadcasted_iota(jnp.int32, (8, 128), 0)
    side = lax.broadcasted_iota(jnp.int32, (8, 128), 1) // 64
    spread = jnp.tile(vectors, (4, 2))
    first = jnp.where((row // 2 == narrow) & (side == wide % 2), spread, 0)
    spread = jnp.tile(in_bias[None], (8, 2))
    second = jnp.where((row == 2 * (wide % 4) + narrow // 2) & (side == narrow % 2), spread, 0)
    return jnp.concatenate([first, second], axis=0).astype(BF16)


def first_block(w_query, w_key, w_value, table, small):
    return jnp.concatenate([w_query, w_key, w_value, table, small], axis=0)


def second_block(w_out, w_in, w_back):
    return jnp.concatenate(
        [w_out[None]]
        + [w_in[None, :, part * 128 : part * 128 + 128] for part in range(4)]
        + [w_back.reshape(4, 64, 128)],
        axis=0,
    )


def turned(total):
    return jnp.concatenate([total[0:128].T, total[128:256].T], axis=0)


def per_device(
    inputs,
    segment_ids,
    cotangent,
    w_query,
    w_key,
    w_value,
    w_out,
    w_in,
    w_back,
    position_table,
    vectors,
    in_bias,
):
    windows, length, features = inputs.shape
    rows = windows * length
    x = inputs.reshape(rows, features)
    early, late = pack_call(
        w_query, w_key, w_value, w_out, w_in, w_back, position_table, vectors, in_bias[None]
    )
    early, late = early[None], late[None]
    for step in range(4):
        early_came = swap(early, ORDER_FIRST, step)
        late_came = swap(late, ORDER_SECOND, step)
        early_came, late_came = lax.optimization_barrier((early_came, late_came))
        if step < 3:
            early = joined_blocks(early, early_came)
            late = joined_blocks(late, late_came)
        else:
            early_far, late_far = early_came, late_came
    first = (early, early_far, swap(early, ORDER_FIRST, 4), swap(early_far, ORDER_FIRST, 4))
    second = (late, late_far, swap(late, ORDER_SECOND, 4), swap(late_far, ORDER_SECOND, 4))
    qkv, attended, lse, passed, mixed, vec, bins, w_qkv = attend_call(
        True, segment_ids, after(x, late), first
    )
    *second, attended = lax.optimization_barrier((*second, attended))
    output, slope, grad_second, first_sum, low_t, keep, send, sums_a, *whole = forward_call(
        True, attended, passed, cotangent.reshape(rows, features), vec, bins, second
    )
    back = start_halving(keep, send, ORDER_BACK)
    grad_first, grad_attended, keep, send, sums_b, bin_sums = backward_call(
        True, slope, grad_second, first_sum, low_t, attended, vec, whole
    )
    back = halve(*back, ORDER_BACK, 3)
    inner = start_halving(keep, send, ORDER_INNER)
    grads, pair_sums = attend_back_call(
        True, segment_ids, qkv, after(grad_attended, back[0]), lse
    )
    grads, back_came, inner_came = lax.optimization_barrier((grads, back[1], inner[1]))
    back = halve(back[0], back_came, ORDER_BACK, 2)
    inner = halve(inner[0], inner_came, ORDER_INNER, 3)
    stream, keep, send = project_back_call(
        True,
        windows,
        after(grads, back[0], inner[0]),
        mixed,
        grad_first,
        (pair_sums, sums_a, sums_b, bin_sums),
        w_qkv,
    )
    keep, send, back_came, inner_came = lax.optimization_barrier((keep, send, back[1], inner[1]))
    outer = start_halving(keep, send, ORDER_OUTER)
    back = halve(back[0], back_came, ORDER_BACK, 1)
    inner = halve(inner[0], inner_came, ORDER_INNER, 2)
    for step in (3, 2, 1):
        outer = halve(*outer, ORDER_OUTER, step)
        if step == 3:
            back = halve(back[0], after(back[1], outer[1]), ORDER_BACK, 0)
        if step > 1:
            inner = halve(inner[0], after(inner[1], outer[1]), ORDER_INNER, step - 2)
    outer = halve(*outer, ORDER_OUTER, 0)
    *matrices, vec, bins = finish_call(outer, inner, back)
    return (
        output.reshape(inputs.shape),
        stream.reshape(inputs.shape),
        *matrices,
        vec,
        bins[0],
    )


def listed(order):
    return block_masks(order, 0) + [1 ^ mask for mask in block_masks(order, 1)]


def canonical(array, axis_tiles):
    rows, columns = array.shape
    across, along = axis_tiles
    return (
        array.reshape(across, rows // across, along, columns // along)
        .transpose(0, 2, 1, 3)
        .reshape(PLACES, rows // across, columns // along)
    )


def uncanonical(blocks, rows, columns):
    return (
        blocks.reshape(WIDE, NARROW, rows // WIDE, columns // NARROW)
        .transpose(0, 2, 1, 3)
        .reshape(rows, columns)
    )


def per_device_any(
    inputs,
    segment_ids,
    cotangent,
    w_query,
    w_key,
    w_value,
    w_out,
    w_in,
    w_back,
    position_table,
    vectors,
    in_bias,
):
    def whole(array):
        array = lax.all_gather(array, "narrow", axis=1, tiled=True)
        return lax.all_gather(array, "wide", axis=0, tiled=True)

    def fours(blocks, order):
        blocks = jnp.stack([blocks[place] for place in listed(order)])
        return tuple(blocks[at * 8 : at * 8 + 8] for at in range(4))

    vectors = lax.all_gather(vectors, "narrow", axis=0, tiled=True)
    vectors = lax.all_gather(vectors, "wide", axis=1, tiled=True)
    in_bias = lax.all_gather(in_bias, AXES, axis=0, tiled=True)
    places = jnp.arange(PLACES)
    pieces = vectors.reshape(NARROW, 2, WIDE, 64).transpose(2, 0, 1, 3).reshape(PLACES, 2, 64)
    small = jax.vmap(small_block)(
        pieces, in_bias.reshape(PLACES, 64), places // NARROW, places % NARROW
    )
    tiles = (WIDE, NARROW)
    first = jax.vmap(first_block)(
        canonical(whole(w_query), tiles),
        canonical(whole(w_key), tiles),
        canonical(whole(w_value), tiles),
        canonical(whole(position_table), tiles),
        small,
    )
    second = jax.vmap(second_block)(
        canonical(whole(w_out), tiles),
        canonical(whole(w_in), tiles),
        canonical(whole(w_back), tiles),
    )
    windows, length, features = inputs.shape
    rows = windows * length
    first, second = fours(first, ORDER_FIRST), fours(second, ORDER_SECOND)
    qkv, attended, lse, passed, mixed, vec, bins, w_qkv = attend_call(
        False, segment_ids, inputs.reshape(rows, features), first
    )
    output, slope, grad_second, first_sum, low_t, keep_back, send_back, sums_a, *whole_w = forward_call(
        False, attended, passed, cotangent.reshape(rows, features), vec, bins, second
    )
    grad_first, grad_attended, keep_in, send_in, sums_b, bin_sums = backward_call(
        False, slope, grad_second, first_sum, low_t, attended, vec, whole_w
    )
    grads, pair_sums = attend_back_call(False, segment_ids, qkv, grad_attended, lse)
    stream, keep_first, send_first = project_back_call(
        False,
        windows,
        grads,
        mixed,
        grad_first,
        (pair_sums, sums_a, sums_b, bin_sums),
        w_qkv,
    )

    def joined(pair, order):
        both = jnp.concatenate([pair[0], pair[1].astype(F32)], axis=0)
        return jnp.stack([both[listed(order).index(place)] for place in range(PLACES)])

    def summed(array):
        array = lax.psum_scatter(array, "wide", scatter_dimension=0, tiled=True)
        return lax.psum_scatter(array, "narrow", scatter_dimension=1, tiled=True)

    back = joined((keep_back, send_back), ORDER_BACK)
    inner = joined((keep_in, send_in), ORDER_INNER)
    outer = joined((keep_first, send_first), ORDER_OUTER)
    back = jax.vmap(turned)(back)
    grad_in = inner[:, 0:4].transpose(0, 2, 1, 3).reshape(PLACES, 64, 512)
    vec = outer.reshape(WIDE, NARROW, 272, 128)[::2, 0, 256:264]
    vec = vec.transpose(1, 0, 2).reshape(8, 512)
    vec = lax.psum_scatter(vec, "wide", scatter_dimension=1, tiled=True)
    vec = lax.psum_scatter(vec, "narrow", scatter_dimension=0, tiled=True)
    bins = outer.reshape(WIDE, NARROW, 272, 128)[::4, 0, 264:272].reshape(2048)
    bins = lax.psum_scatter(bins, AXES, scatter_dimension=0, tiled=True)
    return (
        output.reshape(inputs.shape),
        stream.reshape(inputs.shape),
        summed(uncanonical(outer[:, 0:64], 512, 512)),
        summed(uncanonical(outer[:, 64:128], 512, 512)),
        summed(uncanonical(outer[:, 128:192], 512, 512)),
        summed(uncanonical(inner[:, 4], 512, 512)),
        summed(uncanonical(grad_in, 512, 2048)),
        summed(uncanonical(back, 2048, 512)),
        summed(uncanonical(outer[:, 192:256], 512, 512)),
        vec,
        bins,
    )


def solution(mesh):
    matrix = P("wide", "narrow")
    rows = P(AXES, None, None)
    direct = mesh.shape["wide"] == WIDE and mesh.shape["narrow"] == NARROW
    return jax.shard_map(
        per_device if direct else per_device_any,
        mesh=mesh,
        in_specs=(
            rows,
            P(AXES, None),
            rows,
            matrix,
            matrix,
            matrix,
            matrix,
            matrix,
            matrix,
            matrix,
            P("narrow", "wide"),
            P(AXES),
        ),
        out_specs=(
            rows,
            rows,
            matrix,
            matrix,
            matrix,
            matrix,
            matrix,
            matrix,
            matrix,
            P("narrow", "wide"),
            P(AXES),
        ),
        check_vma=False,
    )
```

```python
from functools import partial
import math

import jax
import jax.numpy as jnp
from jax import lax
from jax.experimental import pallas as pl
from jax.experimental.pallas import tpu as pltpu
from jax.sharding import PartitionSpec as P

HEADS = 8
EPSILON = 1e-05
AXES = ("wide", "narrow")
F32 = jnp.float32
BF16 = jnp.bfloat16
NEG = -1e30
VMEM_LIMIT = 60 * 1024 * 1024

WIDE = 8
NARROW = 4
PLACES = WIDE * NARROW
HALF = PLACES // 2

Z1, Z0, X, Y = 16, 8, 4, 2
ORDER_FIRST = ((X, Y, Z1, Z0), (X, Y, Z0, Z1))
ORDER_SECOND = ((Z1, Z0, X, Y), (Z0, Z1, Y, X))
ORDER_OUTER = ((Z1, Z0, X, Y), (Z0, Z1, Y, X))
ORDER_INNER = ((X, Z1, Z0, Y), (Y, Z0, Z1, X))
ORDER_BACK = ((Z1, Y, Z0, X), (Y, X, Z1, Z0))


def nn(left, right):
    return lax.dot_general(left, right, (((1,), (0,)), ((), ())), preferred_element_type=F32)


def nt(left, right):
    return lax.dot_general(left, right, (((1,), (1,)), ((), ())), preferred_element_type=F32)


def block_masks(order, core):
    masks = []
    for block in range(HALF):
        total = 0
        for step in range(4):
            if block >> step & 1:
                total ^= order[core][step]
        masks.append(total)
    return masks


def place_of(order, me, half, block):
    core = (me & 1) ^ half
    apart = jnp.where(core == 0, block_masks(order, 0)[block], block_masks(order, 1)[block])
    where = me ^ half ^ apart
    return where >> 2, where & 3


def block_at(order, me, apart):
    half = apart & 1
    core = (me & 1) ^ half
    first, second = (block_masks(order, of).index(apart ^ half) for of in range(2))
    return jnp.where(core == 0, first, second)


def pairs(order, step):
    found = []
    for place in range(PLACES):
        mask = 1 if step == 4 else order[place & 1][step]
        found.append((place, place ^ mask))
    return found


def my_place():
    return lax.axis_index("wide") * NARROW + lax.axis_index("narrow")


def head_masks(rows):
    lane = lax.broadcasted_iota(jnp.int32, (rows, 128), 1)
    return lane < 64


def stack_heads(pair_rows, low):
    zero = jnp.zeros_like(pair_rows)
    return jnp.concatenate(
        [jnp.where(low, pair_rows, zero), jnp.where(low, zero, pair_rows)], axis=0
    )


def fill_bias(segments_ref, bias_ref, windows):
    length = segments_ref.shape[1]
    for window in range(windows):
        row = segments_ref[window : window + 1, :].astype(F32)
        column = jnp.transpose(jnp.broadcast_to(row, (128, length)))
        for block in range(length // 128):
            start = max(0, block * 128 - 256)
            stop = block * 128 + 128
            span = stop - start
            key_at = start + lax.broadcasted_iota(jnp.int32, (span, 128), 0)
            query_at = block * 128 + lax.broadcasted_iota(jnp.int32, (span, 128), 1)
            same = column[start:stop, :] == row[:, block * 128 : block * 128 + 128]
            bias_ref[window, block, 0:span, :] = jnp.where(
                (key_at <= query_at) & same, 0.0, NEG
            )


def block_spans(windows, length):
    spans = []
    for window in range(windows):
        for block in range(length // 128):
            stop = block * 128 + 128
            start = max(0, stop - 384)
            base = window * length
            spans.append(
                (
                    window,
                    block,
                    slice(base + stop - 128, base + stop),
                    slice(base + start, base + stop),
                    stop - start,
                )
            )
    return spans


def part_lanes(pair, part):
    return pl.ds(pl.multiple_of(pair * 384 + part * 128, 128), 128)


def wait_whole(ref, sem):
    pltpu.make_async_copy(ref, ref, sem).wait()


def attend_kernel(
    direct,
    segments_ref,
    x_ref,
    p0_ref,
    p1_ref,
    p2_ref,
    p3_ref,
    qkv_ref,
    attended_ref,
    lse_ref,
    passed_ref,
    mixed_ref,
    vec_ref,
    bin_ref,
    weights,
    bias,
    qkv,
    table,
    small,
    sems,
):
    windows, length = segments_ref.shape
    me = my_place() if direct else jnp.int32(0)
    for block in range(HALF):
        for half in range(2):
            source = ((p0_ref, p1_ref), (p2_ref, p3_ref))[half][block // 8].at[block % 8]
            wide, narrow = place_of(ORDER_FIRST, me, half, block)
            rows = pl.ds(pl.multiple_of(wide * 64, 64), 64)
            pltpu.make_async_copy(
                source.at[pl.ds(192, 64)],
                table.at[rows, pl.ds(pl.multiple_of(narrow * 128, 128), 128)],
                sems.at[0],
            ).start()
            pltpu.make_async_copy(
                source.at[pl.ds(256, 16)], small.at[half * HALF + block], sems.at[1]
            ).start()
            for part in range(3):
                pltpu.make_async_copy(
                    source.at[pl.ds(part * 64, 64)],
                    weights.at[
                        rows, pl.ds(pl.multiple_of(narrow * 384 + part * 128, 128), 128)
                    ],
                    sems.at[2],
                ).start()
    fill_bias(segments_ref, bias, windows)
    wait_whole(table, sems.at[0])
    for window in range(windows):
        rows = slice(window * length, (window + 1) * length)
        passed = x_ref[rows, :].astype(F32) + table[...].astype(F32)
        passed_ref[rows, :] = passed
        mixed_ref[rows, :] = passed.astype(BF16)
    wait_whole(small, sems.at[1])
    vec_ref[...] = jnp.zeros_like(vec_ref)
    bin_ref[...] = jnp.zeros_like(bin_ref)
    for half in range(2):
        for block in range(HALF):
            wide, narrow = place_of(ORDER_FIRST, me, half, block)
            piece = small[half * HALF + block].astype(F32)
            vec_ref[wide // 2] += piece[0:8]
            bin_ref[wide // 4] += piece[8:16]
    wait_whole(weights, sems.at[2])
    low = head_masks(128)

    for chunk in range(6):
        projected = nn(mixed_ref[...], weights[:, chunk * 256 : chunk * 256 + 256])
        for side in range(2):
            pair, part = divmod(chunk * 2 + side, 3)
            own = projected[:, side * 128 : side * 128 + 128]
            if part != 1:
                own = own + vec_ref[pair, part // 2 : part // 2 + 1, :]
            own = own.astype(BF16)
            if part == 0:
                own = own * BF16(0.125)
            qkv[:, (chunk * 2 + side) * 128 : (chunk * 2 + side) * 128 + 128] = own

    leave = pltpu.make_async_copy(qkv, qkv_ref, sems.at[3])
    leave.start()

    def per_pair(pair, unused):
        spans = block_spans(windows, length)
        turned_values = [
            jnp.transpose(
                qkv[window * length : (window + 1) * length, part_lanes(pair, 2)]
            )
            for window in range(windows)
        ]
        scores = []
        for window, block, here, there, span in spans:
            query = stack_heads(qkv[here, part_lanes(pair, 0)], low)
            mask = bias[window, block, 0:span, :]
            scores.append(
                nt(qkv[there, part_lanes(pair, 1)], query)
                + jnp.concatenate([mask, mask], axis=1)
            )
        shares = []
        for (window, block, here, there, span), score in zip(spans, scores):
            peak = jnp.max(score, axis=0, keepdims=True)
            weight = jnp.exp(score - peak)
            total = jnp.sum(weight, axis=0, keepdims=True)
            shares.append((weight * (1.0 / total)).astype(BF16))
            lse_ref[pair, window, block : block + 1, :] = peak + jnp.log(total)
        for (window, block, here, there, span), share in zip(spans, shares):
            stop = block * 128 + 128
            joined = nn(turned_values[window][:, stop - span : stop], share)
            both = jnp.concatenate([joined[0:64, 0:128], joined[64:128, 128:256]], axis=0)
            attended_ref[here, pl.ds(pl.multiple_of(pair * 128, 128), 128)] = jnp.transpose(
                both
            ).astype(BF16)
        return unused

    lax.fori_loop(0, NARROW, per_pair, 0, unroll=2)
    leave.wait()


def norm_parts(values):
    average = jnp.mean(values, axis=-1, keepdims=True)
    centred = values - average
    variance = jnp.mean(centred * centred, axis=-1, keepdims=True)
    scale = lax.rsqrt(variance + EPSILON)
    return centred * scale, scale


def norm_back(hat, scale, gains, grad):
    scaled = grad * gains
    first = jnp.mean(scaled, axis=-1, keepdims=True)
    second = jnp.mean(scaled * hat, axis=-1, keepdims=True)
    return scale * (scaled - first - hat * second)


def vec_row(vec_ref, row):
    return jnp.concatenate([vec_ref[tile, row : row + 1, :] for tile in range(4)], axis=1)


def column_sum(values):
    return jnp.sum(values, axis=0, keepdims=True)


GELU_SCALE = math.sqrt(2.0 / math.pi)


def gelu_both(pre):
    square = pre * pre
    curve = jnp.tanh(pre * (GELU_SCALE + (GELU_SCALE * 0.044715) * square))
    half = 0.5 + 0.5 * curve
    slope = (0.5 * pre) * (1.0 - curve * curve) * (
        GELU_SCALE + (3.0 * GELU_SCALE * 0.044715) * square
    )
    return pre * half, half + slope


def load_second(me, blocks, w_out, w_in, w_back, sems):
    for block in range(HALF):
        for half in range(2):
            source = blocks[half * 2 + block // 8].at[block % 8]
            wide, narrow = place_of(ORDER_SECOND, me, half, block)
            rows = pl.ds(pl.multiple_of(wide * 64, 64), 64)
            columns = pl.ds(pl.multiple_of(narrow * 128, 128), 128)
            pltpu.make_async_copy(source.at[0], w_out.at[rows, columns], sems.at[0]).start()
            pltpu.make_async_copy(
                source.at[pl.ds(1, 4)], w_in.at[pl.ds(narrow * 4, 4), rows, :], sems.at[1]
            ).start()
            pltpu.make_async_copy(
                source.at[pl.ds(5, 4)], w_back.at[pl.ds(wide * 4, 4), :, columns], sems.at[2]
            ).start()


def w_in_columns(w_in, chunk):
    return jnp.concatenate([w_in[chunk * 2], w_in[chunk * 2 + 1]], axis=1)


def rows_at(step, rows):
    return pl.ds(pl.multiple_of(step * rows, rows), rows)


def forward_kernel(
    direct,
    attended_ref,
    passed_ref,
    cotangent_ref,
    vec_ref,
    bin_ref,
    p0_ref,
    p1_ref,
    p2_ref,
    p3_ref,
    output_ref,
    slope_ref,
    grad_second_ref,
    first_ref,
    low_t,
    keep_ref,
    send_ref,
    sums_ref,
    w_out,
    w_in,
    w_back,
    active,
    grad_t,
    sems,
):
    rows = ROWS
    me = my_place() if direct else jnp.int32(0)
    load_second(me, (p0_ref, p1_ref, p2_ref, p3_ref), w_out, w_in, w_back, sems)
    sums_ref[...] = jnp.zeros_like(sums_ref)
    wait_whole(w_out, sems.at[0])
    wait_whole(w_in, sems.at[1])
    wait_whole(w_back, sems.at[2])

    def per_rows(step, unused):
        here = rows_at(step, rows)
        first_sum = passed_ref[here, :] + nn(attended_ref[here, :], w_out[...]) + vec_row(vec_ref, 2)
        first_ref[here, :] = first_sum
        hat, unused_scale = norm_parts(first_sum)
        hidden = hat * vec_row(vec_ref, 4) + vec_row(vec_ref, 5)
        low = hidden.astype(BF16)
        turned_low = jnp.transpose(low)
        for wide in range(WIDE):
            low_t[wide ^ (me >> 2), :, here] = turned_low[wide * 64 : wide * 64 + 64, :]
        total = hidden + vec_row(vec_ref, 3)
        for chunk in range(8):
            offset = jnp.concatenate(
                [
                    bin_ref[chunk // 4, 2 * (chunk % 4) + part : 2 * (chunk % 4) + part + 1, :]
                    for part in range(2)
                ],
                axis=1,
            )
            columns = slice(chunk * 256, chunk * 256 + 256)
            value, slope = gelu_both(nn(low, w_in_columns(w_in, chunk)) + offset)
            value = value.astype(BF16)
            active[here, columns] = value
            slope_ref[here, columns] = slope
            total += nn(value, w_back[chunk * 4 : chunk * 4 + 4].reshape(256, 512))
        hat, scale = norm_parts(total)
        gains = vec_row(vec_ref, 6)
        output_ref[here, :] = (hat * gains + vec_row(vec_ref, 7)).astype(BF16)
        cotangent = cotangent_ref[here, :].astype(F32)
        grad_second = norm_back(hat, scale, gains, cotangent)
        grad_second_ref[here, :] = grad_second
        grad_low = grad_second.astype(BF16)
        turned_low = jnp.transpose(grad_low)
        for narrow in range(NARROW):
            grad_t[narrow ^ (me & 3), :, here] = turned_low[narrow * 128 : narrow * 128 + 128, :]
        sums_ref[0:1, :] += column_sum(grad_low.astype(F32))
        sums_ref[1:2, :] += column_sum(cotangent * hat)
        sums_ref[2:3, :] += column_sum(cotangent)
        return unused

    total_rows = attended_ref.shape[0]
    lax.fori_loop(0, total_rows // rows, per_rows, 0)
    grads = grad_t[...].reshape(512, total_rows)
    for wide in range(WIDE):
        columns = pl.ds(pl.multiple_of((wide ^ (me >> 2)) * 256, 256), 256)
        piece = nn(grads, active[:, columns])
        for narrow in range(NARROW):
            target = (keep_ref, send_ref)[narrow & 1]
            block = block_at(ORDER_BACK, me, wide * NARROW + narrow)
            own = piece[narrow * 128 : narrow * 128 + 128]
            target[block, 0:128, :] = own[:, 0:128].astype(target.dtype)
            target[block, 128:256, :] = own[:, 128:256].astype(target.dtype)


def backward_kernel(
    direct,
    slope_ref,
    grad_second_ref,
    first_ref,
    low_t,
    attended_ref,
    vec_ref,
    w_out,
    w_in,
    w_back,
    grad_first_ref,
    grad_attended_ref,
    keep_ref,
    send_ref,
    sums_ref,
    bin_sums_ref,
    grad_pre,
    grad_branch,
    attended_t,
):
    rows = ROWS
    me = my_place() if direct else jnp.int32(0)
    sums_ref[...] = jnp.zeros_like(sums_ref)
    bin_sums_ref[...] = jnp.zeros_like(bin_sums_ref)

    def per_rows(step, unused):
        here = rows_at(step, rows)
        turned_low = jnp.transpose(attended_ref[here, :])
        for wide in range(WIDE):
            attended_t[wide ^ (me >> 2), :, here] = turned_low[wide * 64 : wide * 64 + 64, :]
        grad_hidden = grad_second_ref[here, :]
        grad_low = grad_hidden.astype(BF16)
        for chunk in range(8):
            columns = slice(chunk * 256, chunk * 256 + 256)
            weight = w_back[chunk * 4 : chunk * 4 + 4].reshape(256, 512)
            grad = (nt(grad_low, weight) * slope_ref[here, columns]).astype(BF16)
            grad_pre[here, columns] = grad
            grad_hidden += nt(grad, w_in_columns(w_in, chunk))
            sums = column_sum(grad.astype(F32))
            for part in range(2):
                row = 2 * (chunk % 4) + part
                bin_sums_ref[chunk // 4, row : row + 1, :] += sums[:, part * 128 : part * 128 + 128]
        hat, scale = norm_parts(first_ref[here, :])
        gains = vec_row(vec_ref, 4)
        grad_first = norm_back(hat, scale, gains, grad_hidden)
        grad_first_ref[here, :] = grad_first
        branch = grad_first.astype(BF16)
        grad_branch[here, :] = branch
        sums_ref[0:1, :] += column_sum(branch.astype(F32))
        sums_ref[1:2, :] += column_sum(grad_hidden * hat)
        sums_ref[2:3, :] += column_sum(grad_hidden)
        grad_attended_ref[here, :] = nt(branch, w_out[...]).astype(BF16)
        return unused

    total_rows = attended_ref.shape[0]
    lax.fori_loop(0, total_rows // rows, per_rows, 0)
    lows = low_t[...].reshape(512, total_rows)
    joined = attended_t[...].reshape(512, total_rows)
    for narrow in range(NARROW):
        target = (keep_ref, send_ref)[narrow & 1]
        at = narrow ^ (me & 3)
        for part in range(2):
            columns = pl.ds(pl.multiple_of(at * 512 + part * 256, 256), 256)
            piece = nn(lows, grad_pre[:, columns])
            for wide in range(WIDE):
                block = block_at(ORDER_INNER, me, wide * NARROW + narrow)
                own = piece[wide * 64 : wide * 64 + 64]
                target[block, part * 2] = own[:, 0:128].astype(target.dtype)
                target[block, part * 2 + 1] = own[:, 128:256].astype(target.dtype)
        piece = nn(joined, grad_branch[:, pl.ds(pl.multiple_of(at * 128, 128), 128)])
        for wide in range(WIDE):
            block = block_at(ORDER_INNER, me, wide * NARROW + narrow)
            target[block, 4] = piece[wide * 64 : wide * 64 + 64].astype(target.dtype)


def attend_back_kernel(
    direct,
    segments_ref,
    qkv_ref,
    grad_attended_ref,
    lse_ref,
    grads,
    vec_sums,
    bias,
):
    windows, length = segments_ref.shape
    me = my_place() if direct else jnp.int32(0)
    fill_bias(segments_ref, bias, windows)
    vec_sums[...] = jnp.zeros_like(vec_sums)
    low = head_masks(128)

    def per_pair(apart, unused):
        pair = (me & 3) ^ apart
        spans = block_spans(windows, length)
        lanes = pl.ds(pl.multiple_of(pair * 128, 128), 128)
        turned_keys = [
            jnp.transpose(
                qkv_ref[window * length : (window + 1) * length, part_lanes(pair, 1)]
            )
            for window in range(windows)
        ]
        queries, aboves, scores, grad_shares = [], [], [], []
        for window, block, here, there, span in spans:
            queries.append(stack_heads(qkv_ref[here, part_lanes(pair, 0)], low))
            aboves.append(stack_heads(grad_attended_ref[here, lanes], low))
            mask = bias[window, block, 0:span, :]
            mask = jnp.concatenate([mask, mask], axis=1)
            scores.append(
                nt(qkv_ref[there, part_lanes(pair, 1)], queries[-1])
                + (mask - lse_ref[pair, window, block : block + 1, :])
            )
            grad_shares.append(nt(qkv_ref[there, part_lanes(pair, 2)], aboves[-1]))
        shares, grad_scores = [], []
        for score, grad_share in zip(scores, grad_shares):
            share = jnp.exp(score)
            inner = jnp.sum(share * grad_share, axis=0, keepdims=True)
            shares.append(share.astype(BF16))
            grad_scores.append((share * (grad_share - inner)).astype(BF16))
        grad_keys = [[None] * (length // 128) for window in range(windows)]
        grad_values = [[None] * (length // 128) for window in range(windows)]
        for at, (window, block, here, there, span) in enumerate(spans):
            stop = block * 128 + 128
            for found, sums in (
                (nn(grad_scores[at], queries[at]), grad_keys[window]),
                (nn(shares[at], aboves[at]), grad_values[window]),
            ):
                for part in range(span // 128):
                    of = block - span // 128 + 1 + part
                    piece = found[part * 128 : part * 128 + 128]
                    sums[of] = piece if sums[of] is None else sums[of] + piece
            joined = nn(turned_keys[window][:, stop - span : stop], grad_scores[at])
            both = jnp.concatenate([joined[0:64, 0:128], joined[64:128, 128:256]], axis=0)
            grad = (jnp.transpose(both) * 0.125).astype(BF16)
            grads[here, part_lanes(apart, 0)] = grad
            vec_sums[pair, 0:1, :] += column_sum(grad.astype(F32))
        for window, block, here, there, span in spans:
            grads[here, part_lanes(apart, 1)] = grad_keys[window][block].astype(BF16)
            grad = grad_values[window][block].astype(BF16)
            grads[here, part_lanes(apart, 2)] = grad
            vec_sums[pair, 1:2, :] += column_sum(grad.astype(F32))
        return unused

    lax.fori_loop(0, NARROW, per_pair, 0)


def project_back_kernel(
    direct,
    windows,
    grads,
    mixed_ref,
    grad_first_ref,
    pair_sums_ref,
    sums_a_ref,
    sums_b_ref,
    bin_sums_ref,
    weights,
    stream_ref,
    keep_ref,
    send_ref,
    mixed_t,
    stream,
    vec_sums,
):
    length = mixed_ref.shape[0] // windows
    me = my_place() if direct else jnp.int32(0)
    turned_low = jnp.transpose(mixed_ref[...])
    for wide in range(WIDE):
        mixed_t[wide ^ (me >> 2), :, :] = turned_low[wide * 64 : wide * 64 + 64, :]
    for tile in range(4):
        lanes = slice(tile * 128, tile * 128 + 128)
        vec_sums[tile, 0:2, :] = pair_sums_ref[tile, 0:2, :]
        vec_sums[tile, 2:3, :] = sums_b_ref[0:1, lanes]
        vec_sums[tile, 3:4, :] = sums_a_ref[0:1, lanes]
        vec_sums[tile, 4:6, :] = sums_b_ref[1:3, lanes]
        vec_sums[tile, 6:8, :] = sums_a_ref[1:3, lanes]
    turned_mixed = mixed_t[...].reshape(512, windows * length)
    for chunk in range(6):
        weight_grads = nn(turned_mixed, grads[:, chunk * 256 : chunk * 256 + 256])
        for side in range(2):
            apart, part = divmod(chunk * 2 + side, 3)
            target = (keep_ref, send_ref)[apart & 1]
            for wide in range(WIDE):
                block = block_at(ORDER_OUTER, me, wide * NARROW + apart)
                target[block, part * 64 : part * 64 + 64, :] = weight_grads[
                    wide * 64 : wide * 64 + 64, side * 128 : side * 128 + 128
                ].astype(target.dtype)
    for row in range(0, length, 256):
        total = None
        for window in range(windows):
            rows = slice(window * length + row, window * length + row + 256)
            sums = grad_first_ref[rows, :]
            for apart in range(NARROW):
                lanes = pl.ds(pl.multiple_of(((me & 3) ^ apart) * 384, 128), 384)
                sums += nt(grads[rows, apart * 384 : apart * 384 + 384], weights[:, lanes])
            stream_ref[rows, :] = sums.astype(BF16)
            total = sums if total is None else total + sums
        stream[row : row + 256, :] = total
    for half, target in ((0, keep_ref), (1, send_ref)):
        for block in range(HALF):
            wide, narrow = place_of(ORDER_OUTER, me, half, block)
            target[block, 192:256, :] = stream[
                pl.ds(pl.multiple_of(wide * 64, 64), 64),
                pl.ds(pl.multiple_of(narrow * 128, 128), 128),
            ].astype(target.dtype)
            target[block, 256:264, :] = vec_sums[wide // 2].astype(target.dtype)
            target[block, 264:272, :] = bin_sums_ref[wide // 4].astype(target.dtype)


def doubled(row):
    return jnp.concatenate([row, row], axis=1)


def pack_kernel(
    w_query_ref,
    w_key_ref,
    w_value_ref,
    w_out_ref,
    w_in_ref,
    w_back_ref,
    table_ref,
    vectors_ref,
    in_bias_ref,
    first_ref,
    second_ref,
):
    wide, narrow = lax.axis_index("wide"), lax.axis_index("narrow")
    first_ref[0:64, :] = w_query_ref[...]
    first_ref[64:128, :] = w_key_ref[...]
    first_ref[128:192, :] = w_value_ref[...]
    first_ref[192:256, :] = table_ref[...]
    row = lax.broadcasted_iota(jnp.int32, (8, 128), 0)
    side = lax.broadcasted_iota(jnp.int32, (8, 128), 1) // 64
    vectors = doubled(vectors_ref[...].astype(F32))
    spread = jnp.where(row % 2 == 0, vectors[0:1], vectors[1:2])
    upper = jnp.where((row // 2 == narrow) & (side == wide % 2), spread, 0.0)
    spread = doubled(in_bias_ref[...].astype(F32))
    lower = jnp.where(
        (row == 2 * (wide % 4) + narrow // 2) & (side == narrow % 2), spread, 0.0
    )
    first_ref[256:272, :] = jnp.concatenate([upper, lower], axis=0).astype(BF16)
    second_ref[0] = w_out_ref[...]
    for part in range(4):
        second_ref[1 + part] = w_in_ref[:, part * 128 : part * 128 + 128]
        second_ref[5 + part] = w_back_ref[part * 64 : part * 64 + 64, :]


def finish_kernel(
    outer_ref,
    outer_first_ref,
    outer_second_ref,
    outer_third_ref,
    inner_ref,
    inner_came_ref,
    back_ref,
    back_came_ref,
    query_ref,
    key_ref,
    value_ref,
    out_ref,
    in_ref,
    w_back_ref,
    table_ref,
    vectors_ref,
    in_bias_ref,
):
    wide, narrow = lax.axis_index("wide"), lax.axis_index("narrow")
    total = back_ref[0] + back_came_ref[0].astype(F32)
    w_back_ref[0:128, :] = jnp.transpose(total[0:128])
    w_back_ref[128:256, :] = jnp.transpose(total[128:256])
    for part in range(4):
        in_ref[:, part * 128 : part * 128 + 128] = inner_ref[0, part] + inner_came_ref[
            0, part
        ].astype(F32)
    out_ref[...] = inner_ref[0, 4] + inner_came_ref[0, 4].astype(F32)
    total = outer_ref[0] + outer_first_ref[0].astype(F32)
    total += outer_second_ref[0].astype(F32) + outer_third_ref[0].astype(F32)
    query_ref[...] = total[0:64]
    key_ref[...] = total[64:128]
    value_ref[...] = total[128:192]
    table_ref[...] = total[192:256]
    row = lax.broadcasted_iota(jnp.int32, (8, 128), 0)

    def side_of(rows, second):
        return jnp.where(second == 1, rows[:, 64:128], rows[:, 0:64])

    def row_of(rows, which):
        return column_sum(jnp.where(row == which, rows, 0.0))

    vectors = jnp.concatenate(
        [row_of(total[256:264], narrow * 2), row_of(total[256:264], narrow * 2 + 1)], axis=0
    )
    vectors_ref[...] = side_of(vectors, wide % 2)
    bins = row_of(total[264:272], 2 * (wide % 4) + narrow // 2)
    in_bias_ref[...] = side_of(bins, narrow % 2)


def vmem():
    return pl.BlockSpec(memory_space=pltpu.VMEM)


def hbm():
    return pl.BlockSpec(memory_space=pl.ANY)


def cost(macs, touched):
    return pl.CostEstimate(flops=2 * macs, bytes_accessed=touched, transcendentals=0)


def params(mebibytes):
    return pltpu.CompilerParams(vmem_limit_bytes=mebibytes << 20)


def shape(dims, dtype):
    return jax.ShapeDtypeStruct(dims, dtype)


def near(dims, dtype):
    return pltpu.VMEM(dims, dtype)


def kept(array):
    return pltpu.with_memory_space_constraint(array, pltpu.VMEM)


def attend_call(direct, segments, x, blocks):
    windows, length = segments.shape
    total = windows * length
    return pl.pallas_call(
        partial(attend_kernel, direct),
        out_shape=(
            pltpu.HBM((total, 1536), BF16),
            shape((total, 512), BF16),
            shape((NARROW, windows, length // 128, 256), F32),
            near((total, 512), F32),
            shape((total, 512), BF16),
            shape((4, 8, 128), F32),
            shape((2, 8, 128), F32),
            shape((512, 1536), BF16),
        ),
        in_specs=[vmem(), vmem()] + [hbm()] * 4,
        out_specs=(pl.BlockSpec(memory_space=pltpu.HBM),) + tuple([vmem()] * 7),
        scratch_shapes=[
            pltpu.VMEM((windows, length // 128, 384, 128), F32),
            pltpu.VMEM((total, 1536), BF16),
            pltpu.VMEM((512, 512), BF16),
            pltpu.VMEM((PLACES, 16, 128), BF16),
            pltpu.SemaphoreType.DMA((4,)),
        ],
        compiler_params=params(ATTEND_MIB),
        cost_estimate=cost(6000 << 20, 12 << 20),
        name="attend",
    )(segments, x, *blocks)


ROWS = 512
ATTEND_MIB = 24
FORWARD_MIB = 14
BACKWARD_MIB = 14
ATTEND_BACK_MIB = 20
PROJECT_BACK_MIB = 16


def forward_call(direct, attended, passed, cotangent, vec, bins, blocks):
    total = attended.shape[0]
    return pl.pallas_call(
        partial(forward_kernel, direct),
        out_shape=(
            shape((total, 512), BF16),
            near((total, 2048), F32),
            near((total, 512), F32),
            near((total, 512), F32),
            near((WIDE, 64, total), BF16),
            near((HALF, 256, 128), F32),
            near((HALF, 256, 128), BF16),
            shape((8, 512), F32),
            near((512, 512), BF16),
            near((16, 512, 128), BF16),
            near((32, 64, 512), BF16),
        ),
        in_specs=[vmem()] * 5 + [hbm()] * 4,
        out_specs=tuple([vmem()] * 11),
        scratch_shapes=[
            pltpu.VMEM((total, 2048), BF16),
            pltpu.VMEM((NARROW, 128, total), BF16),
            pltpu.SemaphoreType.DMA((3,)),
        ],
        compiler_params=params(FORWARD_MIB),
        cost_estimate=cost(6000 << 20, 24 << 20),
        input_output_aliases={1: 3},
        name="forward",
    )(attended, kept(passed), cotangent, vec, bins, *blocks)


def backward_call(direct, slope, grad_second, first_sum, low_t, attended, vec, weights):
    total = attended.shape[0]
    return pl.pallas_call(
        partial(backward_kernel, direct),
        out_shape=(
            shape((total, 512), F32),
            shape((total, 512), BF16),
            shape((HALF, 5, 64, 128), F32),
            shape((HALF, 5, 64, 128), BF16),
            shape((8, 512), F32),
            shape((2, 8, 128), F32),
        ),
        in_specs=[vmem()] * 9,
        out_specs=tuple([vmem()] * 6),
        scratch_shapes=[
            pltpu.VMEM((total, 2048), BF16),
            pltpu.VMEM((total, 512), BF16),
            pltpu.VMEM((WIDE, 64, total), BF16),
        ],
        compiler_params=params(BACKWARD_MIB),
        cost_estimate=cost(7000 << 20, 24 << 20),
        name="backward",
    )(
        kept(slope),
        kept(grad_second),
        kept(first_sum),
        kept(low_t),
        attended,
        vec,
        *(kept(weight) for weight in weights),
    )


def attend_back_call(direct, segments, qkv, grad_attended, lse):
    windows, length = segments.shape
    total = windows * length
    return pl.pallas_call(
        partial(attend_back_kernel, direct),
        out_shape=(shape((total, 1536), BF16), shape((4, 8, 128), F32)),
        in_specs=[vmem()] * 4,
        out_specs=(vmem(), vmem()),
        scratch_shapes=[pltpu.VMEM((windows, length // 128, 384, 128), F32)],
        compiler_params=params(ATTEND_BACK_MIB),
        cost_estimate=cost(4000 << 20, 8 << 20),
        name="attend_back",
    )(segments, qkv, grad_attended, lse)


def project_back_call(direct, windows, grads, mixed, grad_first, sums, weights):
    total = mixed.shape[0]
    return pl.pallas_call(
        partial(project_back_kernel, direct, windows),
        out_shape=(
            shape((total, 512), BF16),
            shape((HALF, 272, 128), F32),
            shape((HALF, 272, 128), BF16),
        ),
        in_specs=[vmem()] * 8,
        out_specs=(vmem(), vmem(), vmem()),
        scratch_shapes=[
            pltpu.VMEM((WIDE, 64, total), BF16),
            pltpu.VMEM((total // windows, 512), F32),
            pltpu.VMEM((4, 8, 128), F32),
        ],
        compiler_params=params(PROJECT_BACK_MIB),
        cost_estimate=cost(3000 << 20, 8 << 20),
        name="project_back",
    )(grads, mixed, grad_first, *sums, weights)


def pack_call(*shards):
    return pl.pallas_call(
        pack_kernel,
        out_shape=(near((272, 128), BF16), near((9, 64, 128), BF16)),
        in_specs=[vmem()] * 9,
        out_specs=(vmem(), vmem()),
        name="pack",
    )(*shards)


def join_kernel(first_ref, second_ref, joined_ref):
    half = first_ref.shape[0]
    joined_ref[0:half] = first_ref[...]
    joined_ref[half:] = second_ref[...]


def joined_blocks(first, second):
    count = 2 * first.shape[0]
    return pl.pallas_call(
        join_kernel,
        out_shape=near((count,) + first.shape[1:], first.dtype),
        in_specs=[vmem()] * 2,
        out_specs=vmem(),
        compiler_params=params(2),
        name="join",
    )(kept(first), kept(second))


def finish_call(outer, inner, back):
    block = shape((64, 128), F32)
    return pl.pallas_call(
        finish_kernel,
        out_shape=(
            block,
            block,
            block,
            block,
            shape((64, 512), F32),
            shape((256, 128), F32),
            block,
            shape((2, 64), F32),
            shape((1, 64), F32),
        ),
        in_specs=[vmem()] * 8,
        out_specs=tuple([vmem()] * 9),
        compiler_params=params(6),
        name="finish",
    )(*outer, *inner, *back)


def swap(array, order, step):
    return lax.ppermute(array, AXES, pairs(order, step))


def after(value, *others):
    return lax.optimization_barrier((value,) + others)[0]


def grow(held, order, step):
    return jnp.concatenate([held, swap(held, order, step)], axis=0)


def start_halving(keep, send, order):
    return keep, swap(send, order, 4)


def halve(held, came, order, step):
    size = 1 << step
    upper = (held[size:] + came[size:].astype(F32)).astype(BF16)
    lower = held[:size] + came[:size].astype(F32)
    return lower, swap(upper, order, step)


def scatter_rest(held, came, order):
    own = held[:1] + came[:1].astype(F32)
    others = []
    for block in range(1, 4):
        total = (held[block : block + 1] + came[block : block + 1].astype(F32)).astype(BF16)
        partners = []
        for place in range(PLACES):
            partners.append((place, place ^ block_masks(order, place & 1)[block]))
        others.append(lax.ppermute(total, AXES, partners))
    return own, *others


def small_block(vectors, in_bias, wide, narrow):
    row = lax.broadcasted_iota(jnp.int32, (8, 128), 0)
    side = lax.broadcasted_iota(jnp.int32, (8, 128), 1) // 64
    spread = jnp.tile(vectors, (4, 2))
    first = jnp.where((row // 2 == narrow) & (side == wide % 2), spread, 0)
    spread = jnp.tile(in_bias[None], (8, 2))
    second = jnp.where((row == 2 * (wide % 4) + narrow // 2) & (side == narrow % 2), spread, 0)
    return jnp.concatenate([first, second], axis=0).astype(BF16)


def first_block(w_query, w_key, w_value, table, small):
    return jnp.concatenate([w_query, w_key, w_value, table, small], axis=0)


def second_block(w_out, w_in, w_back):
    return jnp.concatenate(
        [w_out[None]]
        + [w_in[None, :, part * 128 : part * 128 + 128] for part in range(4)]
        + [w_back.reshape(4, 64, 128)],
        axis=0,
    )


def turned(total):
    return jnp.concatenate([total[0:128].T, total[128:256].T], axis=0)


def per_device(
    inputs,
    segment_ids,
    cotangent,
    w_query,
    w_key,
    w_value,
    w_out,
    w_in,
    w_back,
    position_table,
    vectors,
    in_bias,
):
    windows, length, features = inputs.shape
    rows = windows * length
    x = inputs.reshape(rows, features)
    early, late = pack_call(
        w_query, w_key, w_value, w_out, w_in, w_back, position_table, vectors, in_bias[None]
    )
    early, late = early[None], late[None]
    for step in range(4):
        early_came = swap(early, ORDER_FIRST, step)
        late_came = swap(late, ORDER_SECOND, step)
        early_came, late_came = lax.optimization_barrier((early_came, late_came))
        if step < 3:
            early = joined_blocks(early, early_came)
            late = joined_blocks(late, late_came)
        else:
            early_far, late_far = early_came, late_came
    first = (early, early_far, swap(early, ORDER_FIRST, 4), swap(early_far, ORDER_FIRST, 4))
    second = (late, late_far, swap(late, ORDER_SECOND, 4), swap(late_far, ORDER_SECOND, 4))
    qkv, attended, lse, passed, mixed, vec, bins, w_qkv = attend_call(
        True, segment_ids, after(x, late), first
    )
    *second, attended = lax.optimization_barrier((*second, attended))
    output, slope, grad_second, first_sum, low_t, keep, send, sums_a, *whole = forward_call(
        True, attended, passed, cotangent.reshape(rows, features), vec, bins, second
    )
    back = start_halving(keep, send, ORDER_BACK)
    grad_first, grad_attended, keep, send, sums_b, bin_sums = backward_call(
        True, slope, grad_second, first_sum, low_t, attended, vec, whole
    )
    back = halve(*back, ORDER_BACK, 3)
    inner = start_halving(keep, send, ORDER_INNER)
    grads, pair_sums = attend_back_call(
        True, segment_ids, qkv, after(grad_attended, back[0]), lse
    )
    grads, back_came, inner_came = lax.optimization_barrier((grads, back[1], inner[1]))
    back = halve(back[0], back_came, ORDER_BACK, 2)
    inner = halve(inner[0], inner_came, ORDER_INNER, 3)
    stream, keep, send = project_back_call(
        True,
        windows,
        after(grads, back[0], inner[0]),
        mixed,
        grad_first,
        (pair_sums, sums_a, sums_b, bin_sums),
        w_qkv,
    )
    keep, send, back_came, inner_came = lax.optimization_barrier((keep, send, back[1], inner[1]))
    outer = start_halving(keep, send, ORDER_OUTER)
    back = halve(back[0], back_came, ORDER_BACK, 1)
    inner = halve(inner[0], inner_came, ORDER_INNER, 2)
    outer = halve(*outer, ORDER_OUTER, 3)
    came = lax.optimization_barrier((outer[1], inner[1], back[1]))
    outer = halve(outer[0], came[0], ORDER_OUTER, 2)
    inner = halve(inner[0], came[1], ORDER_INNER, 1)
    back = halve(back[0], came[2], ORDER_BACK, 0)
    came = lax.optimization_barrier((outer[1], inner[1], back[1]))
    outer = scatter_rest(outer[0], came[0], ORDER_OUTER)
    inner = halve(inner[0], came[1], ORDER_INNER, 0)
    back = back[0], came[2]
    *matrices, vec, bins = finish_call(outer, inner, back)
    return (
        output.reshape(inputs.shape),
        stream.reshape(inputs.shape),
        *matrices,
        vec,
        bins[0],
    )


def listed(order):
    return block_masks(order, 0) + [1 ^ mask for mask in block_masks(order, 1)]


def canonical(array, axis_tiles):
    rows, columns = array.shape
    across, along = axis_tiles
    return (
        array.reshape(across, rows // across, along, columns // along)
        .transpose(0, 2, 1, 3)
        .reshape(PLACES, rows // across, columns // along)
    )


def uncanonical(blocks, rows, columns):
    return (
        blocks.reshape(WIDE, NARROW, rows // WIDE, columns // NARROW)
        .transpose(0, 2, 1, 3)
        .reshape(rows, columns)
    )


def per_device_any(
    inputs,
    segment_ids,
    cotangent,
    w_query,
    w_key,
    w_value,
    w_out,
    w_in,
    w_back,
    position_table,
    vectors,
    in_bias,
):
    def whole(array):
        array = lax.all_gather(array, "narrow", axis=1, tiled=True)
        return lax.all_gather(array, "wide", axis=0, tiled=True)

    def fours(blocks, order):
        blocks = jnp.stack([blocks[place] for place in listed(order)])
        return tuple(blocks[at * 8 : at * 8 + 8] for at in range(4))

    vectors = lax.all_gather(vectors, "narrow", axis=0, tiled=True)
    vectors = lax.all_gather(vectors, "wide", axis=1, tiled=True)
    in_bias = lax.all_gather(in_bias, AXES, axis=0, tiled=True)
    places = jnp.arange(PLACES)
    pieces = vectors.reshape(NARROW, 2, WIDE, 64).transpose(2, 0, 1, 3).reshape(PLACES, 2, 64)
    small = jax.vmap(small_block)(
        pieces, in_bias.reshape(PLACES, 64), places // NARROW, places % NARROW
    )
    tiles = (WIDE, NARROW)
    first = jax.vmap(first_block)(
        canonical(whole(w_query), tiles),
        canonical(whole(w_key), tiles),
        canonical(whole(w_value), tiles),
        canonical(whole(position_table), tiles),
        small,
    )
    second = jax.vmap(second_block)(
        canonical(whole(w_out), tiles),
        canonical(whole(w_in), tiles),
        canonical(whole(w_back), tiles),
    )
    windows, length, features = inputs.shape
    rows = windows * length
    first, second = fours(first, ORDER_FIRST), fours(second, ORDER_SECOND)
    qkv, attended, lse, passed, mixed, vec, bins, w_qkv = attend_call(
        False, segment_ids, inputs.reshape(rows, features), first
    )
    output, slope, grad_second, first_sum, low_t, keep_back, send_back, sums_a, *whole_w = forward_call(
        False, attended, passed, cotangent.reshape(rows, features), vec, bins, second
    )
    grad_first, grad_attended, keep_in, send_in, sums_b, bin_sums = backward_call(
        False, slope, grad_second, first_sum, low_t, attended, vec, whole_w
    )
    grads, pair_sums = attend_back_call(False, segment_ids, qkv, grad_attended, lse)
    stream, keep_first, send_first = project_back_call(
        False,
        windows,
        grads,
        mixed,
        grad_first,
        (pair_sums, sums_a, sums_b, bin_sums),
        w_qkv,
    )

    def joined(pair, order):
        both = jnp.concatenate([pair[0], pair[1].astype(F32)], axis=0)
        return jnp.stack([both[listed(order).index(place)] for place in range(PLACES)])

    def summed(array):
        array = lax.psum_scatter(array, "wide", scatter_dimension=0, tiled=True)
        return lax.psum_scatter(array, "narrow", scatter_dimension=1, tiled=True)

    back = joined((keep_back, send_back), ORDER_BACK)
    inner = joined((keep_in, send_in), ORDER_INNER)
    outer = joined((keep_first, send_first), ORDER_OUTER)
    back = jax.vmap(turned)(back)
    grad_in = inner[:, 0:4].transpose(0, 2, 1, 3).reshape(PLACES, 64, 512)
    vec = outer.reshape(WIDE, NARROW, 272, 128)[::2, 0, 256:264]
    vec = vec.transpose(1, 0, 2).reshape(8, 512)
    vec = lax.psum_scatter(vec, "wide", scatter_dimension=1, tiled=True)
    vec = lax.psum_scatter(vec, "narrow", scatter_dimension=0, tiled=True)
    bins = outer.reshape(WIDE, NARROW, 272, 128)[::4, 0, 264:272].reshape(2048)
    bins = lax.psum_scatter(bins, AXES, scatter_dimension=0, tiled=True)
    return (
        output.reshape(inputs.shape),
        stream.reshape(inputs.shape),
        summed(uncanonical(outer[:, 0:64], 512, 512)),
        summed(uncanonical(outer[:, 64:128], 512, 512)),
        summed(uncanonical(outer[:, 128:192], 512, 512)),
        summed(uncanonical(inner[:, 4], 512, 512)),
        summed(uncanonical(grad_in, 512, 2048)),
        summed(uncanonical(back, 2048, 512)),
        summed(uncanonical(outer[:, 192:256], 512, 512)),
        vec,
        bins,
    )


def solution(mesh):
    matrix = P("wide", "narrow")
    rows = P(AXES, None, None)
    direct = mesh.shape["wide"] == WIDE and mesh.shape["narrow"] == NARROW
    return jax.shard_map(
        per_device if direct else per_device_any,
        mesh=mesh,
        in_specs=(
            rows,
            P(AXES, None),
            rows,
            matrix,
            matrix,
            matrix,
            matrix,
            matrix,
            matrix,
            matrix,
            P("narrow", "wide"),
            P(AXES),
        ),
        out_specs=(
            rows,
            rows,
            matrix,
            matrix,
            matrix,
            matrix,
            matrix,
            matrix,
            matrix,
            P("narrow", "wide"),
            P(AXES),
        ),
        check_vma=False,
    )
```

```python
from functools import partial
import math

import jax
import jax.numpy as jnp
from jax import lax
from jax.experimental import pallas as pl
from jax.experimental.pallas import tpu as pltpu
from jax.sharding import PartitionSpec as P

HEADS = 8
EPSILON = 1e-05
AXES = ("wide", "narrow")
F32 = jnp.float32
BF16 = jnp.bfloat16
NEG = -1e30
VMEM_LIMIT = 60 * 1024 * 1024

WIDE = 8
NARROW = 4
PLACES = WIDE * NARROW
HALF = PLACES // 2

Z1, Z0, X, Y = 16, 8, 4, 2
ORDER_FIRST = ((X, Y, Z1, Z0), (X, Y, Z0, Z1))
ORDER_SECOND = ((Z1, Z0, X, Y), (Z0, Z1, Y, X))
ORDER_OUTER = ((Z1, Z0, X, Y), (Z0, Z1, Y, X))
ORDER_INNER = ((X, Z1, Z0, Y), (Y, Z0, Z1, X))
ORDER_BACK = ((Z1, Y, Z0, X), (Y, X, Z1, Z0))


def nn(left, right):
    return lax.dot_general(left, right, (((1,), (0,)), ((), ())), preferred_element_type=F32)


def nt(left, right):
    return lax.dot_general(left, right, (((1,), (1,)), ((), ())), preferred_element_type=F32)


def block_masks(order, core):
    masks = []
    for block in range(HALF):
        total = 0
        for step in range(4):
            if block >> step & 1:
                total ^= order[core][step]
        masks.append(total)
    return masks


def place_of(order, me, half, block):
    core = (me & 1) ^ half
    apart = jnp.where(core == 0, block_masks(order, 0)[block], block_masks(order, 1)[block])
    where = me ^ half ^ apart
    return where >> 2, where & 3


def block_at(order, me, apart):
    half = apart & 1
    core = (me & 1) ^ half
    first, second = (block_masks(order, of).index(apart ^ half) for of in range(2))
    return jnp.where(core == 0, first, second)


def pairs(order, step):
    found = []
    for place in range(PLACES):
        mask = 1 if step == 4 else order[place & 1][step]
        found.append((place, place ^ mask))
    return found


def my_place():
    return lax.axis_index("wide") * NARROW + lax.axis_index("narrow")


def head_masks(rows):
    lane = lax.broadcasted_iota(jnp.int32, (rows, 128), 1)
    return lane < 64


def stack_heads(pair_rows, low):
    zero = jnp.zeros_like(pair_rows)
    return jnp.concatenate(
        [jnp.where(low, pair_rows, zero), jnp.where(low, zero, pair_rows)], axis=0
    )


def fill_bias(segments_ref, bias_ref, windows):
    length = segments_ref.shape[1]
    for window in range(windows):
        row = segments_ref[window : window + 1, :].astype(F32)
        column = jnp.transpose(jnp.broadcast_to(row, (128, length)))
        for block in range(length // 128):
            start = max(0, block * 128 - 256)
            stop = block * 128 + 128
            span = stop - start
            key_at = start + lax.broadcasted_iota(jnp.int32, (span, 128), 0)
            query_at = block * 128 + lax.broadcasted_iota(jnp.int32, (span, 128), 1)
            same = column[start:stop, :] == row[:, block * 128 : block * 128 + 128]
            bias_ref[window, block, 0:span, :] = jnp.where(
                (key_at <= query_at) & same, 0.0, NEG
            )


def block_spans(windows, length):
    spans = []
    for window in range(windows):
        for block in range(length // 128):
            stop = block * 128 + 128
            start = max(0, stop - 384)
            base = window * length
            spans.append(
                (
                    window,
                    block,
                    slice(base + stop - 128, base + stop),
                    slice(base + start, base + stop),
                    stop - start,
                )
            )
    return spans


def part_lanes(pair, part):
    return pl.ds(pl.multiple_of(pair * 384 + part * 128, 128), 128)


def wait_whole(ref, sem):
    pltpu.make_async_copy(ref, ref, sem).wait()


def attend_kernel(
    direct,
    segments_ref,
    x_ref,
    p0_ref,
    p1_ref,
    p2_ref,
    p3_ref,
    qkv,
    attended_ref,
    lse_ref,
    passed_ref,
    mixed_ref,
    vec_ref,
    bin_ref,
    weights,
    bias,
    table,
    small,
    sems,
):
    windows, length = segments_ref.shape
    me = my_place() if direct else jnp.int32(0)
    for block in range(HALF):
        for half in range(2):
            source = ((p0_ref, p1_ref), (p2_ref, p3_ref))[half][block // 8].at[block % 8]
            wide, narrow = place_of(ORDER_FIRST, me, half, block)
            rows = pl.ds(pl.multiple_of(wide * 64, 64), 64)
            pltpu.make_async_copy(
                source.at[pl.ds(192, 64)],
                table.at[rows, pl.ds(pl.multiple_of(narrow * 128, 128), 128)],
                sems.at[0],
            ).start()
            pltpu.make_async_copy(
                source.at[pl.ds(256, 16)], small.at[half * HALF + block], sems.at[1]
            ).start()
            for part in range(3):
                pltpu.make_async_copy(
                    source.at[pl.ds(part * 64, 64)],
                    weights.at[
                        rows, pl.ds(pl.multiple_of(narrow * 384 + part * 128, 128), 128)
                    ],
                    sems.at[2],
                ).start()
    fill_bias(segments_ref, bias, windows)
    wait_whole(table, sems.at[0])
    for window in range(windows):
        rows = slice(window * length, (window + 1) * length)
        passed = x_ref[rows, :].astype(F32) + table[...].astype(F32)
        passed_ref[rows, :] = passed
        mixed_ref[rows, :] = passed.astype(BF16)
    wait_whole(small, sems.at[1])
    vec_ref[...] = jnp.zeros_like(vec_ref)
    bin_ref[...] = jnp.zeros_like(bin_ref)
    for half in range(2):
        for block in range(HALF):
            wide, narrow = place_of(ORDER_FIRST, me, half, block)
            piece = small[half * HALF + block].astype(F32)
            vec_ref[wide // 2] += piece[0:8]
            bin_ref[wide // 4] += piece[8:16]
    wait_whole(weights, sems.at[2])
    low = head_masks(128)

    for chunk in range(6):
        projected = nn(mixed_ref[...], weights[:, chunk * 256 : chunk * 256 + 256])
        for side in range(2):
            pair, part = divmod(chunk * 2 + side, 3)
            own = projected[:, side * 128 : side * 128 + 128]
            if part != 1:
                own = own + vec_ref[pair, part // 2 : part // 2 + 1, :]
            own = own.astype(BF16)
            if part == 0:
                own = own * BF16(0.125)
            qkv[:, (chunk * 2 + side) * 128 : (chunk * 2 + side) * 128 + 128] = own

    def per_pair(pair, unused):
        spans = block_spans(windows, length)
        turned_values = [
            jnp.transpose(
                qkv[window * length : (window + 1) * length, part_lanes(pair, 2)]
            )
            for window in range(windows)
        ]
        scores = []
        for window, block, here, there, span in spans:
            query = stack_heads(qkv[here, part_lanes(pair, 0)], low)
            mask = bias[window, block, 0:span, :]
            scores.append(
                nt(qkv[there, part_lanes(pair, 1)], query)
                + jnp.concatenate([mask, mask], axis=1)
            )
        shares = []
        for (window, block, here, there, span), score in zip(spans, scores):
            peak = jnp.max(score, axis=0, keepdims=True)
            weight = jnp.exp(score - peak)
            total = jnp.sum(weight, axis=0, keepdims=True)
            shares.append((weight * (1.0 / total)).astype(BF16))
            lse_ref[pair, window, block : block + 1, :] = peak + jnp.log(total)
        for (window, block, here, there, span), share in zip(spans, shares):
            stop = block * 128 + 128
            joined = nn(turned_values[window][:, stop - span : stop], share)
            both = jnp.concatenate([joined[0:64, 0:128], joined[64:128, 128:256]], axis=0)
            attended_ref[here, pl.ds(pl.multiple_of(pair * 128, 128), 128)] = jnp.transpose(
                both
            ).astype(BF16)
        return unused

    lax.fori_loop(0, NARROW, per_pair, 0, unroll=2)


def norm_parts(values):
    average = jnp.mean(values, axis=-1, keepdims=True)
    centred = values - average
    variance = jnp.mean(centred * centred, axis=-1, keepdims=True)
    scale = lax.rsqrt(variance + EPSILON)
    return centred * scale, scale


def norm_back(hat, scale, gains, grad):
    scaled = grad * gains
    first = jnp.mean(scaled, axis=-1, keepdims=True)
    second = jnp.mean(scaled * hat, axis=-1, keepdims=True)
    return scale * (scaled - first - hat * second)


def vec_row(vec_ref, row):
    return jnp.concatenate([vec_ref[tile, row : row + 1, :] for tile in range(4)], axis=1)


def column_sum(values):
    return jnp.sum(values, axis=0, keepdims=True)


GELU_SCALE = math.sqrt(2.0 / math.pi)


def gelu_both(pre):
    square = pre * pre
    half = jax.nn.sigmoid(pre * (2.0 * GELU_SCALE + (2.0 * GELU_SCALE * 0.044715) * square))
    value = pre * half
    bend = (1.0 - half) * (2.0 * GELU_SCALE + (6.0 * GELU_SCALE * 0.044715) * square)
    return value, half + value * bend


def load_second(me, blocks, w_out, w_in, w_back, sems):
    for block in range(HALF):
        for half in range(2):
            source = blocks[half * 2 + block // 8].at[block % 8]
            wide, narrow = place_of(ORDER_SECOND, me, half, block)
            rows = pl.ds(pl.multiple_of(wide * 64, 64), 64)
            columns = pl.ds(pl.multiple_of(narrow * 128, 128), 128)
            pltpu.make_async_copy(source.at[0], w_out.at[rows, columns], sems.at[0]).start()
            pltpu.make_async_copy(
                source.at[pl.ds(1, 4)], w_in.at[pl.ds(narrow * 4, 4), rows, :], sems.at[1]
            ).start()
            pltpu.make_async_copy(
                source.at[pl.ds(5, 4)], w_back.at[pl.ds(wide * 4, 4), :, columns], sems.at[2]
            ).start()


def w_in_columns(w_in, chunk):
    return jnp.concatenate([w_in[chunk * 2], w_in[chunk * 2 + 1]], axis=1)


def rows_at(step, rows):
    return pl.ds(pl.multiple_of(step * rows, rows), rows)


def forward_kernel(
    direct,
    attended_ref,
    passed_ref,
    cotangent_ref,
    vec_ref,
    bin_ref,
    p0_ref,
    p1_ref,
    p2_ref,
    p3_ref,
    output_ref,
    slope_ref,
    grad_second_ref,
    first_ref,
    low_t,
    keep_ref,
    send_ref,
    sums_ref,
    w_out,
    w_in,
    w_back,
    active,
    grad_t,
    sems,
):
    rows = ROWS
    me = my_place() if direct else jnp.int32(0)
    load_second(me, (p0_ref, p1_ref, p2_ref, p3_ref), w_out, w_in, w_back, sems)
    sums_ref[...] = jnp.zeros_like(sums_ref)
    wait_whole(w_out, sems.at[0])
    wait_whole(w_in, sems.at[1])
    wait_whole(w_back, sems.at[2])

    def per_rows(step, unused):
        here = rows_at(step, rows)
        first_sum = passed_ref[here, :] + nn(attended_ref[here, :], w_out[...]) + vec_row(vec_ref, 2)
        first_ref[here, :] = first_sum
        hat, unused_scale = norm_parts(first_sum)
        hidden = hat * vec_row(vec_ref, 4) + vec_row(vec_ref, 5)
        low = hidden.astype(BF16)
        turned_low = jnp.transpose(low)
        for wide in range(WIDE):
            low_t[wide ^ (me >> 2), :, here] = turned_low[wide * 64 : wide * 64 + 64, :]
        total = hidden + vec_row(vec_ref, 3)
        for chunk in range(8):
            offset = jnp.concatenate(
                [
                    bin_ref[chunk // 4, 2 * (chunk % 4) + part : 2 * (chunk % 4) + part + 1, :]
                    for part in range(2)
                ],
                axis=1,
            )
            columns = slice(chunk * 256, chunk * 256 + 256)
            value, slope = gelu_both(nn(low, w_in_columns(w_in, chunk)) + offset)
            value = value.astype(BF16)
            active[here, columns] = value
            slope_ref[here, columns] = slope
            total += nn(value, w_back[chunk * 4 : chunk * 4 + 4].reshape(256, 512))
        hat, scale = norm_parts(total)
        gains = vec_row(vec_ref, 6)
        output_ref[here, :] = (hat * gains + vec_row(vec_ref, 7)).astype(BF16)
        cotangent = cotangent_ref[here, :].astype(F32)
        grad_second = norm_back(hat, scale, gains, cotangent)
        grad_second_ref[here, :] = grad_second
        grad_low = grad_second.astype(BF16)
        turned_low = jnp.transpose(grad_low)
        for narrow in range(NARROW):
            grad_t[narrow ^ (me & 3), :, here] = turned_low[narrow * 128 : narrow * 128 + 128, :]
        sums_ref[0:1, :] += column_sum(grad_low.astype(F32))
        sums_ref[1:2, :] += column_sum(cotangent * hat)
        sums_ref[2:3, :] += column_sum(cotangent)
        return unused

    total_rows = attended_ref.shape[0]
    lax.fori_loop(0, total_rows // rows, per_rows, 0)
    grads = grad_t[...].reshape(512, total_rows)
    for wide in range(WIDE):
        columns = pl.ds(pl.multiple_of((wide ^ (me >> 2)) * 256, 256), 256)
        piece = nn(grads, active[:, columns])
        for narrow in range(NARROW):
            target = (keep_ref, send_ref)[narrow & 1]
            block = block_at(ORDER_BACK, me, wide * NARROW + narrow)
            own = piece[narrow * 128 : narrow * 128 + 128]
            target[block, 0:128, :] = own[:, 0:128].astype(target.dtype)
            target[block, 128:256, :] = own[:, 128:256].astype(target.dtype)


def backward_kernel(
    direct,
    slope_ref,
    grad_second_ref,
    first_ref,
    low_t,
    attended_ref,
    vec_ref,
    w_out,
    w_in,
    w_back,
    grad_first_ref,
    grad_attended_ref,
    keep_ref,
    send_ref,
    sums_ref,
    bin_sums_ref,
    grad_pre,
    grad_branch,
    attended_t,
):
    rows = ROWS
    me = my_place() if direct else jnp.int32(0)
    sums_ref[...] = jnp.zeros_like(sums_ref)
    bin_sums_ref[...] = jnp.zeros_like(bin_sums_ref)

    def per_rows(step, unused):
        here = rows_at(step, rows)
        turned_low = jnp.transpose(attended_ref[here, :])
        for wide in range(WIDE):
            attended_t[wide ^ (me >> 2), :, here] = turned_low[wide * 64 : wide * 64 + 64, :]
        grad_hidden = grad_second_ref[here, :]
        grad_low = grad_hidden.astype(BF16)
        for chunk in range(8):
            columns = slice(chunk * 256, chunk * 256 + 256)
            weight = w_back[chunk * 4 : chunk * 4 + 4].reshape(256, 512)
            grad = (nt(grad_low, weight) * slope_ref[here, columns]).astype(BF16)
            grad_pre[here, columns] = grad
            sums = column_sum(grad.astype(F32))
            for part in range(2):
                row = 2 * (chunk % 4) + part
                bin_sums_ref[chunk // 4, row : row + 1, :] += sums[:, part * 128 : part * 128 + 128]
        grad_hidden += nt(
            grad_pre[here, :], jnp.concatenate([w_in[tile] for tile in range(16)], axis=1)
        )
        hat, scale = norm_parts(first_ref[here, :])
        gains = vec_row(vec_ref, 4)
        grad_first = norm_back(hat, scale, gains, grad_hidden)
        grad_first_ref[here, :] = grad_first
        branch = grad_first.astype(BF16)
        grad_branch[here, :] = branch
        sums_ref[0:1, :] += column_sum(branch.astype(F32))
        sums_ref[1:2, :] += column_sum(grad_hidden * hat)
        sums_ref[2:3, :] += column_sum(grad_hidden)
        grad_attended_ref[here, :] = nt(branch, w_out[...]).astype(BF16)
        return unused

    total_rows = attended_ref.shape[0]
    lax.fori_loop(0, total_rows // rows, per_rows, 0)
    lows = low_t[...].reshape(512, total_rows)
    joined = attended_t[...].reshape(512, total_rows)
    for narrow in range(NARROW):
        target = (keep_ref, send_ref)[narrow & 1]
        at = narrow ^ (me & 3)
        for part in range(2):
            columns = pl.ds(pl.multiple_of(at * 512 + part * 256, 256), 256)
            piece = nn(lows, grad_pre[:, columns])
            for wide in range(WIDE):
                block = block_at(ORDER_INNER, me, wide * NARROW + narrow)
                own = piece[wide * 64 : wide * 64 + 64]
                target[block, part * 2] = own[:, 0:128].astype(target.dtype)
                target[block, part * 2 + 1] = own[:, 128:256].astype(target.dtype)
        piece = nn(joined, grad_branch[:, pl.ds(pl.multiple_of(at * 128, 128), 128)])
        for wide in range(WIDE):
            block = block_at(ORDER_INNER, me, wide * NARROW + narrow)
            target[block, 4] = piece[wide * 64 : wide * 64 + 64].astype(target.dtype)


def attend_back_kernel(
    direct,
    segments_ref,
    qkv_ref,
    grad_attended_ref,
    lse_ref,
    grads,
    vec_sums,
    bias,
):
    windows, length = segments_ref.shape
    me = my_place() if direct else jnp.int32(0)
    fill_bias(segments_ref, bias, windows)
    vec_sums[...] = jnp.zeros_like(vec_sums)
    low = head_masks(128)

    def per_pair(apart, unused):
        pair = (me & 3) ^ apart
        spans = block_spans(windows, length)
        lanes = pl.ds(pl.multiple_of(pair * 128, 128), 128)
        turned_keys = [
            jnp.transpose(
                qkv_ref[window * length : (window + 1) * length, part_lanes(pair, 1)]
            )
            for window in range(windows)
        ]
        queries, aboves, scores, grad_shares = [], [], [], []
        for window, block, here, there, span in spans:
            queries.append(stack_heads(qkv_ref[here, part_lanes(pair, 0)], low))
            aboves.append(stack_heads(grad_attended_ref[here, lanes], low))
            mask = bias[window, block, 0:span, :]
            mask = jnp.concatenate([mask, mask], axis=1)
            scores.append(
                nt(qkv_ref[there, part_lanes(pair, 1)], queries[-1])
                + (mask - lse_ref[pair, window, block : block + 1, :])
            )
            grad_shares.append(nt(qkv_ref[there, part_lanes(pair, 2)], aboves[-1]))
        shares, grad_scores = [], []
        for score, grad_share in zip(scores, grad_shares):
            share = jnp.exp(score)
            inner = jnp.sum(share * grad_share, axis=0, keepdims=True)
            shares.append(share.astype(BF16))
            grad_scores.append((share * (grad_share - inner)).astype(BF16))
        grad_keys = [[None] * (length // 128) for window in range(windows)]
        grad_values = [[None] * (length // 128) for window in range(windows)]
        for at, (window, block, here, there, span) in enumerate(spans):
            stop = block * 128 + 128
            for found, sums in (
                (nn(grad_scores[at], queries[at]), grad_keys[window]),
                (nn(shares[at], aboves[at]), grad_values[window]),
            ):
                for part in range(span // 128):
                    of = block - span // 128 + 1 + part
                    piece = found[part * 128 : part * 128 + 128]
                    sums[of] = piece if sums[of] is None else sums[of] + piece
            joined = nn(turned_keys[window][:, stop - span : stop], grad_scores[at])
            both = jnp.concatenate([joined[0:64, 0:128], joined[64:128, 128:256]], axis=0)
            grad = (jnp.transpose(both) * 0.125).astype(BF16)
            grads[here, part_lanes(apart, 0)] = grad
            vec_sums[pair, 0:1, :] += column_sum(grad.astype(F32))
        for window, block, here, there, span in spans:
            grads[here, part_lanes(apart, 1)] = grad_keys[window][block].astype(BF16)
            grad = grad_values[window][block].astype(BF16)
            grads[here, part_lanes(apart, 2)] = grad
            vec_sums[pair, 1:2, :] += column_sum(grad.astype(F32))
        return unused

    lax.fori_loop(0, NARROW, per_pair, 0)


def project_back_kernel(
    direct,
    windows,
    grads,
    mixed_ref,
    grad_first_ref,
    pair_sums_ref,
    sums_a_ref,
    sums_b_ref,
    bin_sums_ref,
    weights,
    stream_ref,
    keep_ref,
    send_ref,
    mixed_t,
    stream,
    vec_sums,
):
    length = mixed_ref.shape[0] // windows
    me = my_place() if direct else jnp.int32(0)
    turned_low = jnp.transpose(mixed_ref[...])
    for wide in range(WIDE):
        mixed_t[wide ^ (me >> 2), :, :] = turned_low[wide * 64 : wide * 64 + 64, :]
    for tile in range(4):
        lanes = slice(tile * 128, tile * 128 + 128)
        vec_sums[tile, 0:2, :] = pair_sums_ref[tile, 0:2, :]
        vec_sums[tile, 2:3, :] = sums_b_ref[0:1, lanes]
        vec_sums[tile, 3:4, :] = sums_a_ref[0:1, lanes]
        vec_sums[tile, 4:6, :] = sums_b_ref[1:3, lanes]
        vec_sums[tile, 6:8, :] = sums_a_ref[1:3, lanes]
    turned_mixed = mixed_t[...].reshape(512, windows * length)
    for chunk in range(6):
        weight_grads = nn(turned_mixed, grads[:, chunk * 256 : chunk * 256 + 256])
        for side in range(2):
            apart, part = divmod(chunk * 2 + side, 3)
            target = (keep_ref, send_ref)[apart & 1]
            for wide in range(WIDE):
                block = block_at(ORDER_OUTER, me, wide * NARROW + apart)
                target[block, part * 64 : part * 64 + 64, :] = weight_grads[
                    wide * 64 : wide * 64 + 64, side * 128 : side * 128 + 128
                ].astype(target.dtype)
    for row in range(0, length, 256):
        total = None
        for window in range(windows):
            rows = slice(window * length + row, window * length + row + 256)
            sums = grad_first_ref[rows, :]
            for apart in range(NARROW):
                lanes = pl.ds(pl.multiple_of(((me & 3) ^ apart) * 384, 128), 384)
                sums += nt(grads[rows, apart * 384 : apart * 384 + 384], weights[:, lanes])
            stream_ref[rows, :] = sums.astype(BF16)
            total = sums if total is None else total + sums
        stream[row : row + 256, :] = total
    for half, target in ((0, keep_ref), (1, send_ref)):
        for block in range(HALF):
            wide, narrow = place_of(ORDER_OUTER, me, half, block)
            target[block, 192:256, :] = stream[
                pl.ds(pl.multiple_of(wide * 64, 64), 64),
                pl.ds(pl.multiple_of(narrow * 128, 128), 128),
            ].astype(target.dtype)
            target[block, 256:264, :] = vec_sums[wide // 2].astype(target.dtype)
            target[block, 264:272, :] = bin_sums_ref[wide // 4].astype(target.dtype)


def doubled(row):
    return jnp.concatenate([row, row], axis=1)


def pack_kernel(
    w_query_ref,
    w_key_ref,
    w_value_ref,
    w_out_ref,
    w_in_ref,
    w_back_ref,
    table_ref,
    vectors_ref,
    in_bias_ref,
    first_ref,
    second_ref,
):
    wide, narrow = lax.axis_index("wide"), lax.axis_index("narrow")
    first_ref[0:64, :] = w_query_ref[...]
    first_ref[64:128, :] = w_key_ref[...]
    first_ref[128:192, :] = w_value_ref[...]
    first_ref[192:256, :] = table_ref[...]
    row = lax.broadcasted_iota(jnp.int32, (8, 128), 0)
    side = lax.broadcasted_iota(jnp.int32, (8, 128), 1) // 64
    vectors = doubled(vectors_ref[...].astype(F32))
    spread = jnp.where(row % 2 == 0, vectors[0:1], vectors[1:2])
    upper = jnp.where((row // 2 == narrow) & (side == wide % 2), spread, 0.0)
    spread = doubled(in_bias_ref[...].astype(F32))
    lower = jnp.where(
        (row == 2 * (wide % 4) + narrow // 2) & (side == narrow % 2), spread, 0.0
    )
    first_ref[256:272, :] = jnp.concatenate([upper, lower], axis=0).astype(BF16)
    second_ref[0] = w_out_ref[...]
    for part in range(4):
        second_ref[1 + part] = w_in_ref[:, part * 128 : part * 128 + 128]
        second_ref[5 + part] = w_back_ref[part * 64 : part * 64 + 64, :]


def finish_kernel(
    outer_ref,
    outer_first_ref,
    outer_second_ref,
    outer_third_ref,
    inner_ref,
    inner_came_ref,
    back_ref,
    back_came_ref,
    query_ref,
    key_ref,
    value_ref,
    out_ref,
    in_ref,
    w_back_ref,
    table_ref,
    vectors_ref,
    in_bias_ref,
):
    wide, narrow = lax.axis_index("wide"), lax.axis_index("narrow")
    total = back_ref[0] + back_came_ref[0].astype(F32)
    w_back_ref[0:128, :] = jnp.transpose(total[0:128])
    w_back_ref[128:256, :] = jnp.transpose(total[128:256])
    for part in range(4):
        in_ref[:, part * 128 : part * 128 + 128] = inner_ref[0, part] + inner_came_ref[
            0, part
        ].astype(F32)
    out_ref[...] = inner_ref[0, 4] + inner_came_ref[0, 4].astype(F32)
    total = outer_ref[0] + outer_first_ref[0].astype(F32)
    total += outer_second_ref[0].astype(F32) + outer_third_ref[0].astype(F32)
    query_ref[...] = total[0:64]
    key_ref[...] = total[64:128]
    value_ref[...] = total[128:192]
    table_ref[...] = total[192:256]
    row = lax.broadcasted_iota(jnp.int32, (8, 128), 0)

    def side_of(rows, second):
        return jnp.where(second == 1, rows[:, 64:128], rows[:, 0:64])

    def row_of(rows, which):
        return column_sum(jnp.where(row == which, rows, 0.0))

    vectors = jnp.concatenate(
        [row_of(total[256:264], narrow * 2), row_of(total[256:264], narrow * 2 + 1)], axis=0
    )
    vectors_ref[...] = side_of(vectors, wide % 2)
    bins = row_of(total[264:272], 2 * (wide % 4) + narrow // 2)
    in_bias_ref[...] = side_of(bins, narrow % 2)


def vmem():
    return pl.BlockSpec(memory_space=pltpu.VMEM)


def hbm():
    return pl.BlockSpec(memory_space=pl.ANY)


def cost(macs, touched):
    return pl.CostEstimate(flops=2 * macs, bytes_accessed=touched, transcendentals=0)


def params(mebibytes):
    return pltpu.CompilerParams(vmem_limit_bytes=mebibytes << 20)


def shape(dims, dtype):
    return jax.ShapeDtypeStruct(dims, dtype)


def near(dims, dtype):
    return pltpu.VMEM(dims, dtype)


def kept(array):
    return pltpu.with_memory_space_constraint(array, pltpu.VMEM)


def attend_call(direct, segments, x, blocks):
    windows, length = segments.shape
    total = windows * length
    return pl.pallas_call(
        partial(attend_kernel, direct),
        out_shape=(
            near((total, 1536), BF16),
            shape((total, 512), BF16),
            shape((NARROW, windows, length // 128, 256), F32),
            near((total, 512), F32),
            shape((total, 512), BF16),
            shape((4, 8, 128), F32),
            shape((2, 8, 128), F32),
            shape((512, 1536), BF16),
        ),
        in_specs=[vmem(), vmem()] + [hbm()] * 4,
        out_specs=tuple([vmem()] * 8),
        scratch_shapes=[
            pltpu.VMEM((windows, length // 128, 384, 128), F32),
            pltpu.VMEM((512, 512), BF16),
            pltpu.VMEM((PLACES, 16, 128), BF16),
            pltpu.SemaphoreType.DMA((3,)),
        ],
        compiler_params=params(ATTEND_MIB),
        cost_estimate=cost(6000 << 20, 12 << 20),
        name="attend",
    )(segments, x, *blocks)


ROWS = 512
ATTEND_MIB = 24
FORWARD_MIB = 12
BACKWARD_MIB = 11
ATTEND_BACK_MIB = 20
PROJECT_BACK_MIB = 16


def forward_call(direct, attended, passed, cotangent, vec, bins, blocks):
    total = attended.shape[0]
    return pl.pallas_call(
        partial(forward_kernel, direct),
        out_shape=(
            shape((total, 512), BF16),
            near((total, 2048), F32),
            near((total, 512), F32),
            near((total, 512), F32),
            near((WIDE, 64, total), BF16),
            near((HALF, 256, 128), F32),
            near((HALF, 256, 128), BF16),
            shape((8, 512), F32),
            near((512, 512), BF16),
            near((16, 512, 128), BF16),
            near((32, 64, 512), BF16),
        ),
        in_specs=[vmem()] * 5 + [hbm()] * 4,
        out_specs=tuple([vmem()] * 11),
        scratch_shapes=[
            pltpu.VMEM((total, 2048), BF16),
            pltpu.VMEM((NARROW, 128, total), BF16),
            pltpu.SemaphoreType.DMA((3,)),
        ],
        compiler_params=params(FORWARD_MIB),
        cost_estimate=cost(6000 << 20, 24 << 20),
        input_output_aliases={1: 3},
        name="forward",
    )(attended, kept(passed), cotangent, vec, bins, *blocks)


def backward_call(direct, slope, grad_second, first_sum, low_t, attended, vec, weights):
    total = attended.shape[0]
    return pl.pallas_call(
        partial(backward_kernel, direct),
        out_shape=(
            shape((total, 512), F32),
            shape((total, 512), BF16),
            shape((HALF, 5, 64, 128), F32),
            shape((HALF, 5, 64, 128), BF16),
            shape((8, 512), F32),
            shape((2, 8, 128), F32),
        ),
        in_specs=[vmem()] * 9,
        out_specs=tuple([vmem()] * 6),
        scratch_shapes=[
            pltpu.VMEM((total, 2048), BF16),
            pltpu.VMEM((total, 512), BF16),
            pltpu.VMEM((WIDE, 64, total), BF16),
        ],
        compiler_params=params(BACKWARD_MIB),
        cost_estimate=cost(7000 << 20, 24 << 20),
        input_output_aliases={1: 0, 4: 1},
        name="backward",
    )(
        kept(slope),
        kept(grad_second),
        kept(first_sum),
        kept(low_t),
        attended,
        vec,
        *(kept(weight) for weight in weights),
    )


def attend_back_call(direct, segments, qkv, grad_attended, lse):
    windows, length = segments.shape
    total = windows * length
    return pl.pallas_call(
        partial(attend_back_kernel, direct),
        out_shape=(shape((total, 1536), BF16), shape((4, 8, 128), F32)),
        in_specs=[vmem()] * 4,
        out_specs=(vmem(), vmem()),
        scratch_shapes=[pltpu.VMEM((windows, length // 128, 384, 128), F32)],
        compiler_params=params(ATTEND_BACK_MIB),
        cost_estimate=cost(4000 << 20, 8 << 20),
        name="attend_back",
    )(segments, kept(qkv), grad_attended, lse)


def project_back_call(direct, windows, grads, mixed, grad_first, sums, weights):
    total = mixed.shape[0]
    return pl.pallas_call(
        partial(project_back_kernel, direct, windows),
        out_shape=(
            shape((total, 512), BF16),
            shape((HALF, 272, 128), F32),
            shape((HALF, 272, 128), BF16),
        ),
        in_specs=[vmem()] * 8,
        out_specs=(vmem(), vmem(), vmem()),
        scratch_shapes=[
            pltpu.VMEM((WIDE, 64, total), BF16),
            pltpu.VMEM((total // windows, 512), F32),
            pltpu.VMEM((4, 8, 128), F32),
        ],
        compiler_params=params(PROJECT_BACK_MIB),
        cost_estimate=cost(3000 << 20, 8 << 20),
        name="project_back",
    )(grads, mixed, grad_first, *sums, weights)


def pack_call(*shards):
    return pl.pallas_call(
        pack_kernel,
        out_shape=(near((272, 128), BF16), near((9, 64, 128), BF16)),
        in_specs=[vmem()] * 9,
        out_specs=(vmem(), vmem()),
        name="pack",
    )(*shards)


def join_kernel(first_ref, second_ref, joined_ref):
    half = first_ref.shape[0]
    joined_ref[0:half] = first_ref[...]
    joined_ref[half:] = second_ref[...]


def joined_blocks(first, second):
    count = 2 * first.shape[0]
    return pl.pallas_call(
        join_kernel,
        out_shape=near((count,) + first.shape[1:], first.dtype),
        in_specs=[vmem()] * 2,
        out_specs=vmem(),
        compiler_params=params(2),
        name="join",
    )(kept(first), kept(second))


def finish_call(outer, inner, back):
    block = shape((64, 128), F32)
    return pl.pallas_call(
        finish_kernel,
        out_shape=(
            block,
            block,
            block,
            block,
            shape((64, 512), F32),
            shape((256, 128), F32),
            block,
            shape((2, 64), F32),
            shape((1, 64), F32),
        ),
        in_specs=[vmem()] * 8,
        out_specs=tuple([vmem()] * 9),
        compiler_params=params(6),
        name="finish",
    )(*outer, *inner, *back)


def swap(array, order, step):
    return lax.ppermute(array, AXES, pairs(order, step))


def after(value, *others):
    return lax.optimization_barrier((value,) + others)[0]


def grow(held, order, step):
    return jnp.concatenate([held, swap(held, order, step)], axis=0)


def start_halving(keep, send, order):
    return keep, swap(send, order, 4)


def halve(held, came, order, step):
    size = 1 << step
    upper = (held[size:] + came[size:].astype(F32)).astype(BF16)
    lower = held[:size] + came[:size].astype(F32)
    return lower, swap(upper, order, step)


def scatter_rest(held, came, order):
    own = held[:1] + came[:1].astype(F32)
    others = []
    for block in range(1, 4):
        total = (held[block : block + 1] + came[block : block + 1].astype(F32)).astype(BF16)
        partners = []
        for place in range(PLACES):
            partners.append((place, place ^ block_masks(order, place & 1)[block]))
        others.append(lax.ppermute(total, AXES, partners))
    return own, *others


def small_block(vectors, in_bias, wide, narrow):
    row = lax.broadcasted_iota(jnp.int32, (8, 128), 0)
    side = lax.broadcasted_iota(jnp.int32, (8, 128), 1) // 64
    spread = jnp.tile(vectors, (4, 2))
    first = jnp.where((row // 2 == narrow) & (side == wide % 2), spread, 0)
    spread = jnp.tile(in_bias[None], (8, 2))
    second = jnp.where((row == 2 * (wide % 4) + narrow // 2) & (side == narrow % 2), spread, 0)
    return jnp.concatenate([first, second], axis=0).astype(BF16)


def first_block(w_query, w_key, w_value, table, small):
    return jnp.concatenate([w_query, w_key, w_value, table, small], axis=0)


def second_block(w_out, w_in, w_back):
    return jnp.concatenate(
        [w_out[None]]
        + [w_in[None, :, part * 128 : part * 128 + 128] for part in range(4)]
        + [w_back.reshape(4, 64, 128)],
        axis=0,
    )


def turned(total):
    return jnp.concatenate([total[0:128].T, total[128:256].T], axis=0)


def per_device(
    inputs,
    segment_ids,
    cotangent,
    w_query,
    w_key,
    w_value,
    w_out,
    w_in,
    w_back,
    position_table,
    vectors,
    in_bias,
):
    windows, length, features = inputs.shape
    rows = windows * length
    x = inputs.reshape(rows, features)
    early, late = pack_call(
        w_query, w_key, w_value, w_out, w_in, w_back, position_table, vectors, in_bias[None]
    )
    early, late = early[None], late[None]
    for step in range(4):
        early_came = swap(early, ORDER_FIRST, step)
        late_came = swap(late, ORDER_SECOND, step)
        early_came, late_came = lax.optimization_barrier((early_came, late_came))
        if step < 3:
            early = joined_blocks(early, early_came)
            late = joined_blocks(late, late_came)
        else:
            early_far, late_far = early_came, late_came
    first = (early, early_far, swap(early, ORDER_FIRST, 4), swap(early_far, ORDER_FIRST, 4))
    second = (late, late_far, swap(late, ORDER_SECOND, 4), swap(late_far, ORDER_SECOND, 4))
    qkv, attended, lse, passed, mixed, vec, bins, w_qkv = attend_call(
        True, segment_ids, after(x, late), first
    )
    *second, attended = lax.optimization_barrier((*second, attended))
    output, slope, grad_second, first_sum, low_t, keep, send, sums_a, *whole = forward_call(
        True, attended, passed, cotangent.reshape(rows, features), vec, bins, second
    )
    back = start_halving(keep, send, ORDER_BACK)
    grad_first, grad_attended, keep, send, sums_b, bin_sums = backward_call(
        True, slope, grad_second, first_sum, low_t, attended, vec, whole
    )
    back = halve(*back, ORDER_BACK, 3)
    inner = start_halving(keep, send, ORDER_INNER)
    grads, pair_sums = attend_back_call(
        True, segment_ids, qkv, after(grad_attended, back[0]), lse
    )
    grads, back_came, inner_came = lax.optimization_barrier((grads, back[1], inner[1]))
    back = halve(back[0], back_came, ORDER_BACK, 2)
    inner = halve(inner[0], inner_came, ORDER_INNER, 3)
    stream, keep, send = project_back_call(
        True,
        windows,
        after(grads, back[0], inner[0]),
        mixed,
        grad_first,
        (pair_sums, sums_a, sums_b, bin_sums),
        w_qkv,
    )
    keep, send, back_came = lax.optimization_barrier((keep, send, back[1]))
    upper_came, lower_came = swap(send[8:], ORDER_OUTER, 4), swap(send[:8], ORDER_OUTER, 4)
    back = halve(back[0], back_came, ORDER_BACK, 1)
    upper_came, inner_came = lax.optimization_barrier((upper_came, inner[1]))
    upper = (keep[8:] + upper_came.astype(F32)).astype(BF16)
    outer = keep[:8] + lower_came.astype(F32), swap(upper, ORDER_OUTER, 3)
    inner = halve(inner[0], inner_came, ORDER_INNER, 2)
    came = lax.optimization_barrier((outer[1], inner[1], back[1]))
    outer = halve(outer[0], came[0], ORDER_OUTER, 2)
    inner = halve(inner[0], came[1], ORDER_INNER, 1)
    back = halve(back[0], came[2], ORDER_BACK, 0)
    came = lax.optimization_barrier((outer[1], inner[1], back[1]))
    outer = scatter_rest(outer[0], came[0], ORDER_OUTER)
    inner = halve(inner[0], came[1], ORDER_INNER, 0)
    back = back[0], came[2]
    *matrices, vec, bins = finish_call(outer, inner, back)
    return (
        output.reshape(inputs.shape),
        stream.reshape(inputs.shape),
        *matrices,
        vec,
        bins[0],
    )


def listed(order):
    return block_masks(order, 0) + [1 ^ mask for mask in block_masks(order, 1)]


def canonical(array, axis_tiles):
    rows, columns = array.shape
    across, along = axis_tiles
    return (
        array.reshape(across, rows // across, along, columns // along)
        .transpose(0, 2, 1, 3)
        .reshape(PLACES, rows // across, columns // along)
    )


def uncanonical(blocks, rows, columns):
    return (
        blocks.reshape(WIDE, NARROW, rows // WIDE, columns // NARROW)
        .transpose(0, 2, 1, 3)
        .reshape(rows, columns)
    )


def per_device_any(
    inputs,
    segment_ids,
    cotangent,
    w_query,
    w_key,
    w_value,
    w_out,
    w_in,
    w_back,
    position_table,
    vectors,
    in_bias,
):
    def whole(array):
        array = lax.all_gather(array, "narrow", axis=1, tiled=True)
        return lax.all_gather(array, "wide", axis=0, tiled=True)

    def fours(blocks, order):
        blocks = jnp.stack([blocks[place] for place in listed(order)])
        return tuple(blocks[at * 8 : at * 8 + 8] for at in range(4))

    vectors = lax.all_gather(vectors, "narrow", axis=0, tiled=True)
    vectors = lax.all_gather(vectors, "wide", axis=1, tiled=True)
    in_bias = lax.all_gather(in_bias, AXES, axis=0, tiled=True)
    places = jnp.arange(PLACES)
    pieces = vectors.reshape(NARROW, 2, WIDE, 64).transpose(2, 0, 1, 3).reshape(PLACES, 2, 64)
    small = jax.vmap(small_block)(
        pieces, in_bias.reshape(PLACES, 64), places // NARROW, places % NARROW
    )
    tiles = (WIDE, NARROW)
    first = jax.vmap(first_block)(
        canonical(whole(w_query), tiles),
        canonical(whole(w_key), tiles),
        canonical(whole(w_value), tiles),
        canonical(whole(position_table), tiles),
        small,
    )
    second = jax.vmap(second_block)(
        canonical(whole(w_out), tiles),
        canonical(whole(w_in), tiles),
        canonical(whole(w_back), tiles),
    )
    windows, length, features = inputs.shape
    rows = windows * length
    first, second = fours(first, ORDER_FIRST), fours(second, ORDER_SECOND)
    qkv, attended, lse, passed, mixed, vec, bins, w_qkv = attend_call(
        False, segment_ids, inputs.reshape(rows, features), first
    )
    output, slope, grad_second, first_sum, low_t, keep_back, send_back, sums_a, *whole_w = forward_call(
        False, attended, passed, cotangent.reshape(rows, features), vec, bins, second
    )
    grad_first, grad_attended, keep_in, send_in, sums_b, bin_sums = backward_call(
        False, slope, grad_second, first_sum, low_t, attended, vec, whole_w
    )
    grads, pair_sums = attend_back_call(False, segment_ids, qkv, grad_attended, lse)
    stream, keep_first, send_first = project_back_call(
        False,
        windows,
        grads,
        mixed,
        grad_first,
        (pair_sums, sums_a, sums_b, bin_sums),
        w_qkv,
    )

    def joined(pair, order):
        both = jnp.concatenate([pair[0], pair[1].astype(F32)], axis=0)
        return jnp.stack([both[listed(order).index(place)] for place in range(PLACES)])

    def summed(array):
        array = lax.psum_scatter(array, "wide", scatter_dimension=0, tiled=True)
        return lax.psum_scatter(array, "narrow", scatter_dimension=1, tiled=True)

    back = joined((keep_back, send_back), ORDER_BACK)
    inner = joined((keep_in, send_in), ORDER_INNER)
    outer = joined((keep_first, send_first), ORDER_OUTER)
    back = jax.vmap(turned)(back)
    grad_in = inner[:, 0:4].transpose(0, 2, 1, 3).reshape(PLACES, 64, 512)
    vec = outer.reshape(WIDE, NARROW, 272, 128)[::2, 0, 256:264]
    vec = vec.transpose(1, 0, 2).reshape(8, 512)
    vec = lax.psum_scatter(vec, "wide", scatter_dimension=1, tiled=True)
    vec = lax.psum_scatter(vec, "narrow", scatter_dimension=0, tiled=True)
    bins = outer.reshape(WIDE, NARROW, 272, 128)[::4, 0, 264:272].reshape(2048)
    bins = lax.psum_scatter(bins, AXES, scatter_dimension=0, tiled=True)
    return (
        output.reshape(inputs.shape),
        stream.reshape(inputs.shape),
        summed(uncanonical(outer[:, 0:64], 512, 512)),
        summed(uncanonical(outer[:, 64:128], 512, 512)),
        summed(uncanonical(outer[:, 128:192], 512, 512)),
        summed(uncanonical(inner[:, 4], 512, 512)),
        summed(uncanonical(grad_in, 512, 2048)),
        summed(uncanonical(back, 2048, 512)),
        summed(uncanonical(outer[:, 192:256], 512, 512)),
        vec,
        bins,
    )


def solution(mesh):
    matrix = P("wide", "narrow")
    rows = P(AXES, None, None)
    direct = mesh.shape["wide"] == WIDE and mesh.shape["narrow"] == NARROW
    return jax.shard_map(
        per_device if direct else per_device_any,
        mesh=mesh,
        in_specs=(
            rows,
            P(AXES, None),
            rows,
            matrix,
            matrix,
            matrix,
            matrix,
            matrix,
            matrix,
            matrix,
            P("narrow", "wide"),
            P(AXES),
        ),
        out_specs=(
            rows,
            rows,
            matrix,
            matrix,
            matrix,
            matrix,
            matrix,
            matrix,
            matrix,
            P("narrow", "wide"),
            P(AXES),
        ),
        check_vma=False,
    )
```

```python
from functools import partial
import math

import jax
import jax.numpy as jnp
from jax import lax
from jax.experimental import pallas as pl
from jax.experimental.pallas import tpu as pltpu
from jax.sharding import PartitionSpec as P

HEADS = 8
EPSILON = 1e-05
AXES = ("wide", "narrow")
F32 = jnp.float32
BF16 = jnp.bfloat16
NEG = -1e30
VMEM_LIMIT = 60 * 1024 * 1024

WIDE = 8
NARROW = 4
PLACES = WIDE * NARROW
HALF = PLACES // 2

Z1, Z0, X, Y = 16, 8, 4, 2
ORDER_FIRST = ((X, Y, Z1, Z0), (X, Y, Z0, Z1))
ORDER_SECOND = ((Z1, Z0, X, Y), (Z0, Z1, Y, X))
ORDER_OUTER = ((Z1, Z0, X, Y), (Z0, Z1, Y, X))
ORDER_INNER = ((X, Z1, Z0, Y), (Y, Z0, Z1, X))
ORDER_BACK = ((Z1, Y, Z0, X), (Y, X, Z1, Z0))


def nn(left, right):
    return lax.dot_general(left, right, (((1,), (0,)), ((), ())), preferred_element_type=F32)


def nt(left, right):
    return lax.dot_general(left, right, (((1,), (1,)), ((), ())), preferred_element_type=F32)


def block_masks(order, core):
    masks = []
    for block in range(HALF):
        total = 0
        for step in range(4):
            if block >> step & 1:
                total ^= order[core][step]
        masks.append(total)
    return masks


def place_of(order, me, half, block):
    core = (me & 1) ^ half
    apart = jnp.where(core == 0, block_masks(order, 0)[block], block_masks(order, 1)[block])
    where = me ^ half ^ apart
    return where >> 2, where & 3


def block_at(order, me, apart):
    half = apart & 1
    core = (me & 1) ^ half
    first, second = (block_masks(order, of).index(apart ^ half) for of in range(2))
    return jnp.where(core == 0, first, second)


def pairs(order, step):
    found = []
    for place in range(PLACES):
        mask = 1 if step == 4 else order[place & 1][step]
        found.append((place, place ^ mask))
    return found


def my_place():
    return lax.axis_index("wide") * NARROW + lax.axis_index("narrow")


def head_masks(rows):
    lane = lax.broadcasted_iota(jnp.int32, (rows, 128), 1)
    return lane < 64


def stack_heads(pair_rows, low):
    zero = jnp.zeros_like(pair_rows)
    return jnp.concatenate(
        [jnp.where(low, pair_rows, zero), jnp.where(low, zero, pair_rows)], axis=0
    )


def fill_bias(segments_ref, bias_ref, windows):
    length = segments_ref.shape[1]
    for window in range(windows):
        row = segments_ref[window : window + 1, :].astype(F32)
        column = jnp.transpose(jnp.broadcast_to(row, (128, length)))
        for block in range(length // 128):
            start = max(0, block * 128 - 256)
            stop = block * 128 + 128
            span = stop - start
            key_at = start + lax.broadcasted_iota(jnp.int32, (span, 128), 0)
            query_at = block * 128 + lax.broadcasted_iota(jnp.int32, (span, 128), 1)
            same = column[start:stop, :] == row[:, block * 128 : block * 128 + 128]
            bias_ref[window, block, 0:span, :] = jnp.where(
                (key_at <= query_at) & same, 0.0, NEG
            )


def block_spans(windows, length):
    spans = []
    for window in range(windows):
        for block in range(length // 128):
            stop = block * 128 + 128
            start = max(0, stop - 384)
            base = window * length
            spans.append(
                (
                    window,
                    block,
                    slice(base + stop - 128, base + stop),
                    slice(base + start, base + stop),
                    stop - start,
                )
            )
    return spans


def part_lanes(pair, part):
    return pl.ds(pl.multiple_of(pair * 384 + part * 128, 128), 128)


def wait_whole(ref, sem):
    pltpu.make_async_copy(ref, ref, sem).wait()


def attend_kernel(
    direct,
    segments_ref,
    x_ref,
    p0_ref,
    p1_ref,
    p2_ref,
    p3_ref,
    qkv,
    attended_ref,
    lse_ref,
    passed_ref,
    mixed_ref,
    vec_ref,
    bin_ref,
    weights,
    bias,
    table,
    small,
    sems,
):
    windows, length = segments_ref.shape
    me = my_place() if direct else jnp.int32(0)
    for block in range(HALF):
        for half in range(2):
            source = ((p0_ref, p1_ref), (p2_ref, p3_ref))[half][block // 8].at[block % 8]
            wide, narrow = place_of(ORDER_FIRST, me, half, block)
            rows = pl.ds(pl.multiple_of(wide * 64, 64), 64)
            pltpu.make_async_copy(
                source.at[pl.ds(192, 64)],
                table.at[rows, pl.ds(pl.multiple_of(narrow * 128, 128), 128)],
                sems.at[0],
            ).start()
            pltpu.make_async_copy(
                source.at[pl.ds(256, 16)], small.at[half * HALF + block], sems.at[1]
            ).start()
            for part in range(3):
                pltpu.make_async_copy(
                    source.at[pl.ds(part * 64, 64)],
                    weights.at[
                        rows, pl.ds(pl.multiple_of(narrow * 384 + part * 128, 128), 128)
                    ],
                    sems.at[2],
                ).start()
    fill_bias(segments_ref, bias, windows)
    wait_whole(table, sems.at[0])
    for window in range(windows):
        rows = slice(window * length, (window + 1) * length)
        passed = x_ref[rows, :].astype(F32) + table[...].astype(F32)
        passed_ref[rows, :] = passed
        mixed_ref[rows, :] = passed.astype(BF16)
    wait_whole(small, sems.at[1])
    vec_ref[...] = jnp.zeros_like(vec_ref)
    bin_ref[...] = jnp.zeros_like(bin_ref)
    for half in range(2):
        for block in range(HALF):
            wide, narrow = place_of(ORDER_FIRST, me, half, block)
            piece = small[half * HALF + block].astype(F32)
            vec_ref[wide // 2] += piece[0:8]
            bin_ref[wide // 4] += piece[8:16]
    wait_whole(weights, sems.at[2])
    low = head_masks(128)

    for chunk in range(6):
        projected = nn(mixed_ref[...], weights[:, chunk * 256 : chunk * 256 + 256])
        for side in range(2):
            pair, part = divmod(chunk * 2 + side, 3)
            own = projected[:, side * 128 : side * 128 + 128]
            if part != 1:
                own = own + vec_ref[pair, part // 2 : part // 2 + 1, :]
            own = own.astype(BF16)
            if part == 0:
                own = own * BF16(0.125)
            qkv[:, (chunk * 2 + side) * 128 : (chunk * 2 + side) * 128 + 128] = own

    def per_pair(pair, unused):
        spans = block_spans(windows, length)
        turned_values = [
            jnp.transpose(
                qkv[window * length : (window + 1) * length, part_lanes(pair, 2)]
            )
            for window in range(windows)
        ]
        scores = []
        for window, block, here, there, span in spans:
            query = stack_heads(qkv[here, part_lanes(pair, 0)], low)
            mask = bias[window, block, 0:span, :]
            scores.append(
                nt(qkv[there, part_lanes(pair, 1)], query)
                + jnp.concatenate([mask, mask], axis=1)
            )
        shares = []
        for (window, block, here, there, span), score in zip(spans, scores):
            peak = jnp.max(score, axis=0, keepdims=True)
            weight = jnp.exp(score - peak)
            total = jnp.sum(weight, axis=0, keepdims=True)
            shares.append((weight * (1.0 / total)).astype(BF16))
            lse_ref[pair, window, block : block + 1, :] = peak + jnp.log(total)
        for (window, block, here, there, span), share in zip(spans, shares):
            stop = block * 128 + 128
            joined = nn(turned_values[window][:, stop - span : stop], share)
            both = jnp.concatenate([joined[0:64, 0:128], joined[64:128, 128:256]], axis=0)
            attended_ref[here, pl.ds(pl.multiple_of(pair * 128, 128), 128)] = jnp.transpose(
                both
            ).astype(BF16)
        return unused

    lax.fori_loop(0, NARROW, per_pair, 0, unroll=2)


def norm_parts(values):
    average = jnp.mean(values, axis=-1, keepdims=True)
    centred = values - average
    variance = jnp.mean(centred * centred, axis=-1, keepdims=True)
    scale = lax.rsqrt(variance + EPSILON)
    return centred * scale, scale


def norm_back(hat, scale, gains, grad):
    scaled = grad * gains
    first = jnp.mean(scaled, axis=-1, keepdims=True)
    second = jnp.mean(scaled * hat, axis=-1, keepdims=True)
    return scale * (scaled - first - hat * second)


def vec_row(vec_ref, row):
    return jnp.concatenate([vec_ref[tile, row : row + 1, :] for tile in range(4)], axis=1)


def column_sum(values):
    return jnp.sum(values, axis=0, keepdims=True)


GELU_SCALE = math.sqrt(2.0 / math.pi)


def gelu_both(pre):
    square = pre * pre
    half = jax.nn.sigmoid(pre * (2.0 * GELU_SCALE + (2.0 * GELU_SCALE * 0.044715) * square))
    value = pre * half
    bend = (1.0 - half) * (2.0 * GELU_SCALE + (6.0 * GELU_SCALE * 0.044715) * square)
    return value, half + value * bend


def load_second(me, blocks, w_out, w_in, w_back, sems):
    for block in range(HALF):
        for half in range(2):
            source = blocks[half * 2 + block // 8].at[block % 8]
            wide, narrow = place_of(ORDER_SECOND, me, half, block)
            rows = pl.ds(pl.multiple_of(wide * 64, 64), 64)
            columns = pl.ds(pl.multiple_of(narrow * 128, 128), 128)
            pltpu.make_async_copy(source.at[0], w_out.at[rows, columns], sems.at[0]).start()
            pltpu.make_async_copy(
                source.at[pl.ds(1, 4)], w_in.at[pl.ds(narrow * 4, 4), rows, :], sems.at[1]
            ).start()
            pltpu.make_async_copy(
                source.at[pl.ds(5, 4)], w_back.at[pl.ds(wide * 4, 4), :, columns], sems.at[2]
            ).start()


def w_in_columns(w_in, chunk):
    return jnp.concatenate([w_in[chunk * 2], w_in[chunk * 2 + 1]], axis=1)


def rows_at(step, rows):
    return pl.ds(pl.multiple_of(step * rows, rows), rows)


def forward_kernel(
    direct,
    attended_ref,
    passed_ref,
    cotangent_ref,
    vec_ref,
    bin_ref,
    p0_ref,
    p1_ref,
    p2_ref,
    p3_ref,
    output_ref,
    slope_ref,
    grad_second_ref,
    first_ref,
    low_t,
    keep_ref,
    send_ref,
    sums_ref,
    w_out,
    w_in,
    w_back,
    active,
    grad_t,
    sems,
):
    rows = ROWS
    me = my_place() if direct else jnp.int32(0)
    load_second(me, (p0_ref, p1_ref, p2_ref, p3_ref), w_out, w_in, w_back, sems)
    sums_ref[...] = jnp.zeros_like(sums_ref)
    wait_whole(w_out, sems.at[0])
    wait_whole(w_in, sems.at[1])
    wait_whole(w_back, sems.at[2])

    def per_rows(step, unused):
        here = rows_at(step, rows)
        first_sum = passed_ref[here, :] + nn(attended_ref[here, :], w_out[...]) + vec_row(vec_ref, 2)
        first_ref[here, :] = first_sum
        hat, unused_scale = norm_parts(first_sum)
        hidden = hat * vec_row(vec_ref, 4) + vec_row(vec_ref, 5)
        low = hidden.astype(BF16)
        turned_low = jnp.transpose(low)
        for wide in range(WIDE):
            low_t[wide ^ (me >> 2), :, here] = turned_low[wide * 64 : wide * 64 + 64, :]
        total = hidden + vec_row(vec_ref, 3)
        for chunk in range(8):
            offset = jnp.concatenate(
                [
                    bin_ref[chunk // 4, 2 * (chunk % 4) + part : 2 * (chunk % 4) + part + 1, :]
                    for part in range(2)
                ],
                axis=1,
            )
            columns = slice(chunk * 256, chunk * 256 + 256)
            value, slope = gelu_both(nn(low, w_in_columns(w_in, chunk)) + offset)
            value = value.astype(BF16)
            active[here, columns] = value
            slope_ref[here, columns] = slope
            total += nn(value, w_back[chunk * 4 : chunk * 4 + 4].reshape(256, 512))
        hat, scale = norm_parts(total)
        gains = vec_row(vec_ref, 6)
        output_ref[here, :] = (hat * gains + vec_row(vec_ref, 7)).astype(BF16)
        cotangent = cotangent_ref[here, :].astype(F32)
        grad_second = norm_back(hat, scale, gains, cotangent)
        grad_second_ref[here, :] = grad_second
        grad_low = grad_second.astype(BF16)
        turned_low = jnp.transpose(grad_low)
        for narrow in range(NARROW):
            grad_t[narrow ^ (me & 3), :, here] = turned_low[narrow * 128 : narrow * 128 + 128, :]
        sums_ref[0:1, :] += column_sum(grad_low.astype(F32))
        sums_ref[1:2, :] += column_sum(cotangent * hat)
        sums_ref[2:3, :] += column_sum(cotangent)
        return unused

    total_rows = attended_ref.shape[0]
    lax.fori_loop(0, total_rows // rows, per_rows, 0)
    grads = grad_t[...].reshape(512, total_rows)
    for wide in range(WIDE):
        columns = pl.ds(pl.multiple_of((wide ^ (me >> 2)) * 256, 256), 256)
        piece = nn(grads, active[:, columns])
        for narrow in range(NARROW):
            target = (keep_ref, send_ref)[narrow & 1]
            block = block_at(ORDER_BACK, me, wide * NARROW + narrow)
            own = piece[narrow * 128 : narrow * 128 + 128]
            target[block, 0:128, :] = own[:, 0:128].astype(target.dtype)
            target[block, 128:256, :] = own[:, 128:256].astype(target.dtype)


def backward_kernel(
    direct,
    slope_ref,
    grad_second_ref,
    first_ref,
    low_t,
    attended_ref,
    vec_ref,
    w_out,
    w_in,
    w_back,
    grad_first_ref,
    grad_attended_ref,
    keep_ref,
    send_ref,
    sums_ref,
    bin_sums_ref,
    grad_pre,
    grad_branch,
    attended_t,
):
    rows = ROWS
    me = my_place() if direct else jnp.int32(0)
    sums_ref[...] = jnp.zeros_like(sums_ref)
    bin_sums_ref[...] = jnp.zeros_like(bin_sums_ref)

    def per_rows(step, unused):
        here = rows_at(step, rows)
        turned_low = jnp.transpose(attended_ref[here, :])
        for wide in range(WIDE):
            attended_t[wide ^ (me >> 2), :, here] = turned_low[wide * 64 : wide * 64 + 64, :]
        grad_hidden = grad_second_ref[here, :]
        grad_low = grad_hidden.astype(BF16)
        for chunk in range(8):
            columns = slice(chunk * 256, chunk * 256 + 256)
            weight = w_back[chunk * 4 : chunk * 4 + 4].reshape(256, 512)
            grad = (nt(grad_low, weight) * slope_ref[here, columns]).astype(BF16)
            grad_pre[here, columns] = grad
            sums = column_sum(grad.astype(F32))
            for part in range(2):
                row = 2 * (chunk % 4) + part
                bin_sums_ref[chunk // 4, row : row + 1, :] += sums[:, part * 128 : part * 128 + 128]
        grad_hidden += nt(
            grad_pre[here, :], jnp.concatenate([w_in[tile] for tile in range(16)], axis=1)
        )
        hat, scale = norm_parts(first_ref[here, :])
        gains = vec_row(vec_ref, 4)
        grad_first = norm_back(hat, scale, gains, grad_hidden)
        grad_first_ref[here, :] = grad_first
        branch = grad_first.astype(BF16)
        grad_branch[here, :] = branch
        sums_ref[0:1, :] += column_sum(branch.astype(F32))
        sums_ref[1:2, :] += column_sum(grad_hidden * hat)
        sums_ref[2:3, :] += column_sum(grad_hidden)
        grad_attended_ref[here, :] = nt(branch, w_out[...]).astype(BF16)
        return unused

    total_rows = attended_ref.shape[0]
    lax.fori_loop(0, total_rows // rows, per_rows, 0)
    lows = low_t[...].reshape(512, total_rows)
    joined = attended_t[...].reshape(512, total_rows)
    for narrow in range(NARROW):
        target = (keep_ref, send_ref)[narrow & 1]
        at = narrow ^ (me & 3)
        for part in range(2):
            columns = pl.ds(pl.multiple_of(at * 512 + part * 256, 256), 256)
            piece = nn(lows, grad_pre[:, columns])
            for wide in range(WIDE):
                block = block_at(ORDER_INNER, me, wide * NARROW + narrow)
                own = piece[wide * 64 : wide * 64 + 64]
                target[block, part * 2] = own[:, 0:128].astype(target.dtype)
                target[block, part * 2 + 1] = own[:, 128:256].astype(target.dtype)
        piece = nn(joined, grad_branch[:, pl.ds(pl.multiple_of(at * 128, 128), 128)])
        for wide in range(WIDE):
            block = block_at(ORDER_INNER, me, wide * NARROW + narrow)
            target[block, 4] = piece[wide * 64 : wide * 64 + 64].astype(target.dtype)


def attend_back_kernel(
    direct,
    segments_ref,
    qkv_ref,
    grad_attended_ref,
    lse_ref,
    grads,
    vec_sums,
    bias,
):
    windows, length = segments_ref.shape
    me = my_place() if direct else jnp.int32(0)
    fill_bias(segments_ref, bias, windows)
    vec_sums[...] = jnp.zeros_like(vec_sums)
    low = head_masks(128)

    def per_pair(apart, unused):
        pair = (me & 3) ^ apart
        spans = block_spans(windows, length)
        lanes = pl.ds(pl.multiple_of(pair * 128, 128), 128)
        turned_keys = [
            jnp.transpose(
                qkv_ref[window * length : (window + 1) * length, part_lanes(pair, 1)]
            )
            for window in range(windows)
        ]
        queries, aboves, scores, grad_shares = [], [], [], []
        for window, block, here, there, span in spans:
            queries.append(stack_heads(qkv_ref[here, part_lanes(pair, 0)], low))
            aboves.append(stack_heads(grad_attended_ref[here, lanes], low))
            mask = bias[window, block, 0:span, :]
            mask = jnp.concatenate([mask, mask], axis=1)
            scores.append(
                nt(qkv_ref[there, part_lanes(pair, 1)], queries[-1])
                + (mask - lse_ref[pair, window, block : block + 1, :])
            )
            grad_shares.append(nt(qkv_ref[there, part_lanes(pair, 2)], aboves[-1]))
        shares, grad_scores = [], []
        for score, grad_share in zip(scores, grad_shares):
            share = jnp.exp(score)
            inner = jnp.sum(share * grad_share, axis=0, keepdims=True)
            shares.append(share.astype(BF16))
            grad_scores.append((share * (grad_share - inner)).astype(BF16))
        grad_keys = [[None] * (length // 128) for window in range(windows)]
        grad_values = [[None] * (length // 128) for window in range(windows)]
        for at, (window, block, here, there, span) in enumerate(spans):
            stop = block * 128 + 128
            for found, sums in (
                (nn(grad_scores[at], queries[at]), grad_keys[window]),
                (nn(shares[at], aboves[at]), grad_values[window]),
            ):
                for part in range(span // 128):
                    of = block - span // 128 + 1 + part
                    piece = found[part * 128 : part * 128 + 128]
                    sums[of] = piece if sums[of] is None else sums[of] + piece
            joined = nn(turned_keys[window][:, stop - span : stop], grad_scores[at])
            both = jnp.concatenate([joined[0:64, 0:128], joined[64:128, 128:256]], axis=0)
            grad = (jnp.transpose(both) * 0.125).astype(BF16)
            grads[here, part_lanes(apart, 0)] = grad
            vec_sums[pair, 0:1, :] += column_sum(grad.astype(F32))
        for window, block, here, there, span in spans:
            grads[here, part_lanes(apart, 1)] = grad_keys[window][block].astype(BF16)
            grad = grad_values[window][block].astype(BF16)
            grads[here, part_lanes(apart, 2)] = grad
            vec_sums[pair, 1:2, :] += column_sum(grad.astype(F32))
        return unused

    lax.fori_loop(0, NARROW, per_pair, 0)


def project_back_kernel(
    direct,
    windows,
    grads,
    mixed_ref,
    grad_first_ref,
    pair_sums_ref,
    sums_a_ref,
    sums_b_ref,
    bin_sums_ref,
    weights,
    stream_ref,
    keep_ref,
    send_ref,
    mixed_t,
    stream,
    vec_sums,
):
    length = mixed_ref.shape[0] // windows
    me = my_place() if direct else jnp.int32(0)
    turned_low = jnp.transpose(mixed_ref[...])
    for wide in range(WIDE):
        mixed_t[wide ^ (me >> 2), :, :] = turned_low[wide * 64 : wide * 64 + 64, :]
    for tile in range(4):
        lanes = slice(tile * 128, tile * 128 + 128)
        vec_sums[tile, 0:2, :] = pair_sums_ref[tile, 0:2, :]
        vec_sums[tile, 2:3, :] = sums_b_ref[0:1, lanes]
        vec_sums[tile, 3:4, :] = sums_a_ref[0:1, lanes]
        vec_sums[tile, 4:6, :] = sums_b_ref[1:3, lanes]
        vec_sums[tile, 6:8, :] = sums_a_ref[1:3, lanes]
    turned_mixed = mixed_t[...].reshape(512, windows * length)
    for chunk in range(6):
        weight_grads = nn(turned_mixed, grads[:, chunk * 256 : chunk * 256 + 256])
        for side in range(2):
            apart, part = divmod(chunk * 2 + side, 3)
            target = (keep_ref, send_ref)[apart & 1]
            for wide in range(WIDE):
                block = block_at(ORDER_OUTER, me, wide * NARROW + apart)
                target[block, part * 64 : part * 64 + 64, :] = weight_grads[
                    wide * 64 : wide * 64 + 64, side * 128 : side * 128 + 128
                ].astype(target.dtype)
    for row in range(0, length, 256):
        total = None
        for window in range(windows):
            rows = slice(window * length + row, window * length + row + 256)
            sums = grad_first_ref[rows, :]
            for apart in range(NARROW):
                lanes = pl.ds(pl.multiple_of(((me & 3) ^ apart) * 384, 128), 384)
                sums += nt(grads[rows, apart * 384 : apart * 384 + 384], weights[:, lanes])
            stream_ref[rows, :] = sums.astype(BF16)
            total = sums if total is None else total + sums
        stream[row : row + 256, :] = total
    for half, target in ((0, keep_ref), (1, send_ref)):
        for block in range(HALF):
            wide, narrow = place_of(ORDER_OUTER, me, half, block)
            target[block, 192:256, :] = stream[
                pl.ds(pl.multiple_of(wide * 64, 64), 64),
                pl.ds(pl.multiple_of(narrow * 128, 128), 128),
            ].astype(target.dtype)
            target[block, 256:264, :] = vec_sums[wide // 2].astype(target.dtype)
            target[block, 264:272, :] = bin_sums_ref[wide // 4].astype(target.dtype)


def doubled(row):
    return jnp.concatenate([row, row], axis=1)


def pack_kernel(
    w_query_ref,
    w_key_ref,
    w_value_ref,
    w_out_ref,
    w_in_ref,
    w_back_ref,
    table_ref,
    vectors_ref,
    in_bias_ref,
    first_ref,
    second_ref,
):
    wide, narrow = lax.axis_index("wide"), lax.axis_index("narrow")
    first_ref[0:64, :] = w_query_ref[...]
    first_ref[64:128, :] = w_key_ref[...]
    first_ref[128:192, :] = w_value_ref[...]
    first_ref[192:256, :] = table_ref[...]
    row = lax.broadcasted_iota(jnp.int32, (8, 128), 0)
    side = lax.broadcasted_iota(jnp.int32, (8, 128), 1) // 64
    vectors = doubled(vectors_ref[...].astype(F32))
    spread = jnp.where(row % 2 == 0, vectors[0:1], vectors[1:2])
    upper = jnp.where((row // 2 == narrow) & (side == wide % 2), spread, 0.0)
    spread = doubled(in_bias_ref[...].astype(F32))
    lower = jnp.where(
        (row == 2 * (wide % 4) + narrow // 2) & (side == narrow % 2), spread, 0.0
    )
    first_ref[256:272, :] = jnp.concatenate([upper, lower], axis=0).astype(BF16)
    second_ref[0] = w_out_ref[...]
    for part in range(4):
        second_ref[1 + part] = w_in_ref[:, part * 128 : part * 128 + 128]
        second_ref[5 + part] = w_back_ref[part * 64 : part * 64 + 64, :]


def finish_kernel(
    outer_ref,
    outer_first_ref,
    outer_second_ref,
    outer_third_ref,
    inner_ref,
    inner_came_ref,
    back_ref,
    back_came_ref,
    query_ref,
    key_ref,
    value_ref,
    out_ref,
    in_ref,
    w_back_ref,
    table_ref,
    vectors_ref,
    in_bias_ref,
):
    wide, narrow = lax.axis_index("wide"), lax.axis_index("narrow")
    total = back_ref[0] + back_came_ref[0].astype(F32)
    w_back_ref[0:128, :] = jnp.transpose(total[0:128])
    w_back_ref[128:256, :] = jnp.transpose(total[128:256])
    for part in range(4):
        in_ref[:, part * 128 : part * 128 + 128] = inner_ref[0, part] + inner_came_ref[
            0, part
        ].astype(F32)
    out_ref[...] = inner_ref[0, 4] + inner_came_ref[0, 4].astype(F32)
    total = outer_ref[0] + outer_first_ref[0].astype(F32)
    total += outer_second_ref[0].astype(F32) + outer_third_ref[0].astype(F32)
    query_ref[...] = total[0:64]
    key_ref[...] = total[64:128]
    value_ref[...] = total[128:192]
    table_ref[...] = total[192:256]
    row = lax.broadcasted_iota(jnp.int32, (8, 128), 0)

    def side_of(rows, second):
        return jnp.where(second == 1, rows[:, 64:128], rows[:, 0:64])

    def row_of(rows, which):
        return column_sum(jnp.where(row == which, rows, 0.0))

    vectors = jnp.concatenate(
        [row_of(total[256:264], narrow * 2), row_of(total[256:264], narrow * 2 + 1)], axis=0
    )
    vectors_ref[...] = side_of(vectors, wide % 2)
    bins = row_of(total[264:272], 2 * (wide % 4) + narrow // 2)
    in_bias_ref[...] = side_of(bins, narrow % 2)


def vmem():
    return pl.BlockSpec(memory_space=pltpu.VMEM)


def hbm():
    return pl.BlockSpec(memory_space=pl.ANY)


def cost(macs, touched):
    return pl.CostEstimate(flops=2 * macs, bytes_accessed=touched, transcendentals=0)


def params(mebibytes):
    return pltpu.CompilerParams(vmem_limit_bytes=mebibytes << 20)


def shape(dims, dtype):
    return jax.ShapeDtypeStruct(dims, dtype)


def near(dims, dtype):
    return pltpu.VMEM(dims, dtype)


def kept(array):
    return pltpu.with_memory_space_constraint(array, pltpu.VMEM)


def attend_call(direct, segments, x, blocks):
    windows, length = segments.shape
    total = windows * length
    return pl.pallas_call(
        partial(attend_kernel, direct),
        out_shape=(
            near((total, 1536), BF16),
            shape((total, 512), BF16),
            shape((NARROW, windows, length // 128, 256), F32),
            near((total, 512), F32),
            shape((total, 512), BF16),
            shape((4, 8, 128), F32),
            shape((2, 8, 128), F32),
            shape((512, 1536), BF16),
        ),
        in_specs=[vmem(), vmem()] + [hbm()] * 4,
        out_specs=tuple([vmem()] * 8),
        scratch_shapes=[
            pltpu.VMEM((windows, length // 128, 384, 128), F32),
            pltpu.VMEM((512, 512), BF16),
            pltpu.VMEM((PLACES, 16, 128), BF16),
            pltpu.SemaphoreType.DMA((3,)),
        ],
        compiler_params=params(ATTEND_MIB),
        cost_estimate=cost(6000 << 20, 12 << 20),
        name="attend",
    )(segments, x, *blocks)


ROWS = 512
ATTEND_MIB = 24
FORWARD_MIB = 12
BACKWARD_MIB = 11
ATTEND_BACK_MIB = 20
PROJECT_BACK_MIB = 16


def forward_call(direct, attended, passed, cotangent, vec, bins, blocks):
    total = attended.shape[0]
    return pl.pallas_call(
        partial(forward_kernel, direct),
        out_shape=(
            shape((total, 512), BF16),
            near((total, 2048), F32),
            near((total, 512), F32),
            near((total, 512), F32),
            near((WIDE, 64, total), BF16),
            near((HALF, 256, 128), F32),
            near((HALF, 256, 128), BF16),
            shape((8, 512), F32),
            near((512, 512), BF16),
            near((16, 512, 128), BF16),
            near((32, 64, 512), BF16),
        ),
        in_specs=[vmem()] * 5 + [hbm()] * 4,
        out_specs=tuple([vmem()] * 11),
        scratch_shapes=[
            pltpu.VMEM((total, 2048), BF16),
            pltpu.VMEM((NARROW, 128, total), BF16),
            pltpu.SemaphoreType.DMA((3,)),
        ],
        compiler_params=params(FORWARD_MIB),
        cost_estimate=cost(6000 << 20, 24 << 20),
        input_output_aliases={1: 3},
        name="forward",
    )(attended, kept(passed), cotangent, vec, bins, *blocks)


def backward_call(direct, slope, grad_second, first_sum, low_t, attended, vec, weights):
    total = attended.shape[0]
    return pl.pallas_call(
        partial(backward_kernel, direct),
        out_shape=(
            shape((total, 512), F32),
            shape((total, 512), BF16),
            shape((HALF, 5, 64, 128), F32),
            shape((HALF, 5, 64, 128), BF16),
            shape((8, 512), F32),
            shape((2, 8, 128), F32),
        ),
        in_specs=[vmem()] * 9,
        out_specs=tuple([vmem()] * 6),
        scratch_shapes=[
            pltpu.VMEM((total, 2048), BF16),
            pltpu.VMEM((total, 512), BF16),
            pltpu.VMEM((WIDE, 64, total), BF16),
        ],
        compiler_params=params(BACKWARD_MIB),
        cost_estimate=cost(7000 << 20, 24 << 20),
        input_output_aliases={1: 0, 4: 1},
        name="backward",
    )(
        kept(slope),
        kept(grad_second),
        kept(first_sum),
        kept(low_t),
        attended,
        vec,
        *(kept(weight) for weight in weights),
    )


def attend_back_call(direct, segments, qkv, grad_attended, lse):
    windows, length = segments.shape
    total = windows * length
    return pl.pallas_call(
        partial(attend_back_kernel, direct),
        out_shape=(shape((total, 1536), BF16), shape((4, 8, 128), F32)),
        in_specs=[vmem()] * 4,
        out_specs=(vmem(), vmem()),
        scratch_shapes=[pltpu.VMEM((windows, length // 128, 384, 128), F32)],
        compiler_params=params(ATTEND_BACK_MIB),
        cost_estimate=cost(4000 << 20, 8 << 20),
        name="attend_back",
    )(segments, kept(qkv), grad_attended, lse)


def project_back_call(direct, windows, grads, mixed, grad_first, sums, weights):
    total = mixed.shape[0]
    return pl.pallas_call(
        partial(project_back_kernel, direct, windows),
        out_shape=(
            shape((total, 512), BF16),
            shape((HALF, 272, 128), F32),
            shape((HALF, 272, 128), BF16),
        ),
        in_specs=[vmem()] * 8,
        out_specs=(vmem(), vmem(), vmem()),
        scratch_shapes=[
            pltpu.VMEM((WIDE, 64, total), BF16),
            pltpu.VMEM((total // windows, 512), F32),
            pltpu.VMEM((4, 8, 128), F32),
        ],
        compiler_params=params(PROJECT_BACK_MIB),
        cost_estimate=cost(3000 << 20, 8 << 20),
        name="project_back",
    )(grads, mixed, grad_first, *sums, weights)


def pack_call(*shards):
    return pl.pallas_call(
        pack_kernel,
        out_shape=(near((272, 128), BF16), near((9, 64, 128), BF16)),
        in_specs=[vmem()] * 9,
        out_specs=(vmem(), vmem()),
        name="pack",
    )(*shards)


def join_kernel(first_ref, second_ref, joined_ref):
    half = first_ref.shape[0]
    joined_ref[0:half] = first_ref[...]
    joined_ref[half:] = second_ref[...]


def joined_blocks(first, second):
    count = 2 * first.shape[0]
    return pl.pallas_call(
        join_kernel,
        out_shape=near((count,) + first.shape[1:], first.dtype),
        in_specs=[vmem()] * 2,
        out_specs=vmem(),
        compiler_params=params(2),
        name="join",
    )(kept(first), kept(second))


def finish_call(outer, inner, back):
    block = shape((64, 128), F32)
    return pl.pallas_call(
        finish_kernel,
        out_shape=(
            block,
            block,
            block,
            block,
            shape((64, 512), F32),
            shape((256, 128), F32),
            block,
            shape((2, 64), F32),
            shape((1, 64), F32),
        ),
        in_specs=[vmem()] * 8,
        out_specs=tuple([vmem()] * 9),
        compiler_params=params(6),
        name="finish",
    )(*outer, *inner, *back)


def swap(array, order, step):
    return lax.ppermute(array, AXES, pairs(order, step))


def after(value, *others):
    return lax.optimization_barrier((value,) + others)[0]


def grow(held, order, step):
    return jnp.concatenate([held, swap(held, order, step)], axis=0)


def start_halving(keep, send, order):
    return keep, swap(send, order, 4)


def halve(held, came, order, step):
    size = 1 << step
    upper = (held[size:] + came[size:].astype(F32)).astype(BF16)
    lower = held[:size] + came[:size].astype(F32)
    return lower, swap(upper, order, step)


def scatter_rest(held, came, order):
    own = held[:1] + came[:1].astype(F32)
    others = []
    for block in range(1, 4):
        total = (held[block : block + 1] + came[block : block + 1].astype(F32)).astype(BF16)
        partners = []
        for place in range(PLACES):
            partners.append((place, place ^ block_masks(order, place & 1)[block]))
        others.append(lax.ppermute(total, AXES, partners))
    return own, *others


def small_block(vectors, in_bias, wide, narrow):
    row = lax.broadcasted_iota(jnp.int32, (8, 128), 0)
    side = lax.broadcasted_iota(jnp.int32, (8, 128), 1) // 64
    spread = jnp.tile(vectors, (4, 2))
    first = jnp.where((row // 2 == narrow) & (side == wide % 2), spread, 0)
    spread = jnp.tile(in_bias[None], (8, 2))
    second = jnp.where((row == 2 * (wide % 4) + narrow // 2) & (side == narrow % 2), spread, 0)
    return jnp.concatenate([first, second], axis=0).astype(BF16)


def first_block(w_query, w_key, w_value, table, small):
    return jnp.concatenate([w_query, w_key, w_value, table, small], axis=0)


def second_block(w_out, w_in, w_back):
    return jnp.concatenate(
        [w_out[None]]
        + [w_in[None, :, part * 128 : part * 128 + 128] for part in range(4)]
        + [w_back.reshape(4, 64, 128)],
        axis=0,
    )


def turned(total):
    return jnp.concatenate([total[0:128].T, total[128:256].T], axis=0)


def per_device(
    inputs,
    segment_ids,
    cotangent,
    w_query,
    w_key,
    w_value,
    w_out,
    w_in,
    w_back,
    position_table,
    vectors,
    in_bias,
):
    windows, length, features = inputs.shape
    rows = windows * length
    x = inputs.reshape(rows, features)
    early, late = pack_call(
        w_query, w_key, w_value, w_out, w_in, w_back, position_table, vectors, in_bias[None]
    )
    early, late = early[None], late[None]
    for step in range(4):
        early_came = swap(early, ORDER_FIRST, step)
        late_came = swap(late, ORDER_SECOND, step)
        early_came, late_came = lax.optimization_barrier((early_came, late_came))
        if step < 3:
            early = joined_blocks(early, early_came)
            late = joined_blocks(late, late_came)
        else:
            early_far, late_far = early_came, late_came
    first = (early, early_far, swap(early, ORDER_FIRST, 4), swap(early_far, ORDER_FIRST, 4))
    second = (late, late_far, swap(late, ORDER_SECOND, 4), swap(late_far, ORDER_SECOND, 4))
    qkv, attended, lse, passed, mixed, vec, bins, w_qkv = attend_call(
        True, segment_ids, after(x, late), first
    )
    *second, attended = lax.optimization_barrier((*second, attended))
    output, slope, grad_second, first_sum, low_t, keep, send, sums_a, *whole = forward_call(
        True, attended, passed, cotangent.reshape(rows, features), vec, bins, second
    )
    back = start_halving(keep, send, ORDER_BACK)
    grad_first, grad_attended, keep, send, sums_b, bin_sums = backward_call(
        True, slope, grad_second, first_sum, low_t, attended, vec, whole
    )
    back = halve(*back, ORDER_BACK, 3)
    inner = start_halving(keep, send, ORDER_INNER)
    grads, pair_sums = attend_back_call(
        True, segment_ids, qkv, after(grad_attended, back[0]), lse
    )
    grads, back_came, inner_came = lax.optimization_barrier((grads, back[1], inner[1]))
    back = halve(back[0], back_came, ORDER_BACK, 2)
    inner = halve(inner[0], inner_came, ORDER_INNER, 3)
    stream, keep, send = project_back_call(
        True,
        windows,
        after(grads, back[0], inner[0]),
        mixed,
        grad_first,
        (pair_sums, sums_a, sums_b, bin_sums),
        w_qkv,
    )
    keep, send, back_came = lax.optimization_barrier((keep, send, back[1]))
    upper_came, lower_came = swap(send[8:], ORDER_OUTER, 4), swap(send[:8], ORDER_OUTER, 4)
    back = halve(back[0], back_came, ORDER_BACK, 1)
    upper_came, inner_came = lax.optimization_barrier((upper_came, inner[1]))
    upper = (keep[8:] + upper_came.astype(F32)).astype(BF16)
    far = swap(upper, ORDER_OUTER, 3)
    inner = halve(inner[0], inner_came, ORDER_INNER, 2)
    came = lax.optimization_barrier((far, inner[1], back[1], lower_came))
    outer = halve(keep[:8] + came[3].astype(F32), came[0], ORDER_OUTER, 2)
    inner = halve(inner[0], came[1], ORDER_INNER, 1)
    back = halve(back[0], came[2], ORDER_BACK, 0)
    came = lax.optimization_barrier((outer[1], inner[1], back[1]))
    outer = scatter_rest(outer[0], came[0], ORDER_OUTER)
    inner = halve(inner[0], came[1], ORDER_INNER, 0)
    back = back[0], came[2]
    *matrices, vec, bins = finish_call(outer, inner, back)
    return (
        output.reshape(inputs.shape),
        stream.reshape(inputs.shape),
        *matrices,
        vec,
        bins[0],
    )


def listed(order):
    return block_masks(order, 0) + [1 ^ mask for mask in block_masks(order, 1)]


def canonical(array, axis_tiles):
    rows, columns = array.shape
    across, along = axis_tiles
    return (
        array.reshape(across, rows // across, along, columns // along)
        .transpose(0, 2, 1, 3)
        .reshape(PLACES, rows // across, columns // along)
    )


def uncanonical(blocks, rows, columns):
    return (
        blocks.reshape(WIDE, NARROW, rows // WIDE, columns // NARROW)
        .transpose(0, 2, 1, 3)
        .reshape(rows, columns)
    )


def per_device_any(
    inputs,
    segment_ids,
    cotangent,
    w_query,
    w_key,
    w_value,
    w_out,
    w_in,
    w_back,
    position_table,
    vectors,
    in_bias,
):
    def whole(array):
        array = lax.all_gather(array, "narrow", axis=1, tiled=True)
        return lax.all_gather(array, "wide", axis=0, tiled=True)

    def fours(blocks, order):
        blocks = jnp.stack([blocks[place] for place in listed(order)])
        return tuple(blocks[at * 8 : at * 8 + 8] for at in range(4))

    vectors = lax.all_gather(vectors, "narrow", axis=0, tiled=True)
    vectors = lax.all_gather(vectors, "wide", axis=1, tiled=True)
    in_bias = lax.all_gather(in_bias, AXES, axis=0, tiled=True)
    places = jnp.arange(PLACES)
    pieces = vectors.reshape(NARROW, 2, WIDE, 64).transpose(2, 0, 1, 3).reshape(PLACES, 2, 64)
    small = jax.vmap(small_block)(
        pieces, in_bias.reshape(PLACES, 64), places // NARROW, places % NARROW
    )
    tiles = (WIDE, NARROW)
    first = jax.vmap(first_block)(
        canonical(whole(w_query), tiles),
        canonical(whole(w_key), tiles),
        canonical(whole(w_value), tiles),
        canonical(whole(position_table), tiles),
        small,
    )
    second = jax.vmap(second_block)(
        canonical(whole(w_out), tiles),
        canonical(whole(w_in), tiles),
        canonical(whole(w_back), tiles),
    )
    windows, length, features = inputs.shape
    rows = windows * length
    first, second = fours(first, ORDER_FIRST), fours(second, ORDER_SECOND)
    qkv, attended, lse, passed, mixed, vec, bins, w_qkv = attend_call(
        False, segment_ids, inputs.reshape(rows, features), first
    )
    output, slope, grad_second, first_sum, low_t, keep_back, send_back, sums_a, *whole_w = forward_call(
        False, attended, passed, cotangent.reshape(rows, features), vec, bins, second
    )
    grad_first, grad_attended, keep_in, send_in, sums_b, bin_sums = backward_call(
        False, slope, grad_second, first_sum, low_t, attended, vec, whole_w
    )
    grads, pair_sums = attend_back_call(False, segment_ids, qkv, grad_attended, lse)
    stream, keep_first, send_first = project_back_call(
        False,
        windows,
        grads,
        mixed,
        grad_first,
        (pair_sums, sums_a, sums_b, bin_sums),
        w_qkv,
    )

    def joined(pair, order):
        both = jnp.concatenate([pair[0], pair[1].astype(F32)], axis=0)
        return jnp.stack([both[listed(order).index(place)] for place in range(PLACES)])

    def summed(array):
        array = lax.psum_scatter(array, "wide", scatter_dimension=0, tiled=True)
        return lax.psum_scatter(array, "narrow", scatter_dimension=1, tiled=True)

    back = joined((keep_back, send_back), ORDER_BACK)
    inner = joined((keep_in, send_in), ORDER_INNER)
    outer = joined((keep_first, send_first), ORDER_OUTER)
    back = jax.vmap(turned)(back)
    grad_in = inner[:, 0:4].transpose(0, 2, 1, 3).reshape(PLACES, 64, 512)
    vec = outer.reshape(WIDE, NARROW, 272, 128)[::2, 0, 256:264]
    vec = vec.transpose(1, 0, 2).reshape(8, 512)
    vec = lax.psum_scatter(vec, "wide", scatter_dimension=1, tiled=True)
    vec = lax.psum_scatter(vec, "narrow", scatter_dimension=0, tiled=True)
    bins = outer.reshape(WIDE, NARROW, 272, 128)[::4, 0, 264:272].reshape(2048)
    bins = lax.psum_scatter(bins, AXES, scatter_dimension=0, tiled=True)
    return (
        output.reshape(inputs.shape),
        stream.reshape(inputs.shape),
        summed(uncanonical(outer[:, 0:64], 512, 512)),
        summed(uncanonical(outer[:, 64:128], 512, 512)),
        summed(uncanonical(outer[:, 128:192], 512, 512)),
        summed(uncanonical(inner[:, 4], 512, 512)),
        summed(uncanonical(grad_in, 512, 2048)),
        summed(uncanonical(back, 2048, 512)),
        summed(uncanonical(outer[:, 192:256], 512, 512)),
        vec,
        bins,
    )


def solution(mesh):
    matrix = P("wide", "narrow")
    rows = P(AXES, None, None)
    direct = mesh.shape["wide"] == WIDE and mesh.shape["narrow"] == NARROW
    return jax.shard_map(
        per_device if direct else per_device_any,
        mesh=mesh,
        in_specs=(
            rows,
            P(AXES, None),
            rows,
            matrix,
            matrix,
            matrix,
            matrix,
            matrix,
            matrix,
            matrix,
            P("narrow", "wide"),
            P(AXES),
        ),
        out_specs=(
            rows,
            rows,
            matrix,
            matrix,
            matrix,
            matrix,
            matrix,
            matrix,
            matrix,
            P("narrow", "wide"),
            P(AXES),
        ),
        check_vma=False,
    )
```

```python
from functools import partial
import math

import jax
import jax.numpy as jnp
from jax import lax
from jax.experimental import pallas as pl
from jax.experimental.pallas import tpu as pltpu
from jax.sharding import PartitionSpec as P

HEADS = 8
EPSILON = 1e-05
AXES = ("wide", "narrow")
F32 = jnp.float32
BF16 = jnp.bfloat16
NEG = -1e30
VMEM_LIMIT = 60 * 1024 * 1024

WIDE = 8
NARROW = 4
PLACES = WIDE * NARROW
HALF = PLACES // 2

Z1, Z0, X, Y = 16, 8, 4, 2
ORDER_FIRST = ((X, Y, Z1, Z0), (X, Y, Z0, Z1))
ORDER_SECOND = ((Z1, Z0, X, Y), (Z0, Z1, Y, X))
ORDER_OUTER = ((Z1, Z0, X, Y), (Z0, Z1, Y, X))
ORDER_INNER = ((X, Z1, Z0, Y), (Y, Z0, Z1, X))
ORDER_BACK = ((Z1, Y, Z0, X), (Y, X, Z1, Z0))


def nn(left, right):
    return lax.dot_general(left, right, (((1,), (0,)), ((), ())), preferred_element_type=F32)


def nt(left, right):
    return lax.dot_general(left, right, (((1,), (1,)), ((), ())), preferred_element_type=F32)


def block_masks(order, core):
    masks = []
    for block in range(HALF):
        total = 0
        for step in range(4):
            if block >> step & 1:
                total ^= order[core][step]
        masks.append(total)
    return masks


def place_of(order, me, half, block):
    core = (me & 1) ^ half
    apart = jnp.where(core == 0, block_masks(order, 0)[block], block_masks(order, 1)[block])
    where = me ^ half ^ apart
    return where >> 2, where & 3


def block_at(order, me, apart):
    half = apart & 1
    core = (me & 1) ^ half
    first, second = (block_masks(order, of).index(apart ^ half) for of in range(2))
    return jnp.where(core == 0, first, second)


def pairs(order, step):
    found = []
    for place in range(PLACES):
        mask = 1 if step == 4 else order[place & 1][step]
        found.append((place, place ^ mask))
    return found


def my_place():
    return lax.axis_index("wide") * NARROW + lax.axis_index("narrow")


def head_masks(rows):
    lane = lax.broadcasted_iota(jnp.int32, (rows, 128), 1)
    return lane < 64


def stack_heads(pair_rows, low):
    zero = jnp.zeros_like(pair_rows)
    return jnp.concatenate(
        [jnp.where(low, pair_rows, zero), jnp.where(low, zero, pair_rows)], axis=0
    )


def fill_bias(segments_ref, bias_ref, windows):
    length = segments_ref.shape[1]
    for window in range(windows):
        row = segments_ref[window : window + 1, :].astype(F32)
        column = jnp.transpose(jnp.broadcast_to(row, (128, length)))
        for block in range(length // 128):
            start = max(0, block * 128 - 256)
            stop = block * 128 + 128
            span = stop - start
            key_at = start + lax.broadcasted_iota(jnp.int32, (span, 128), 0)
            query_at = block * 128 + lax.broadcasted_iota(jnp.int32, (span, 128), 1)
            same = column[start:stop, :] == row[:, block * 128 : block * 128 + 128]
            bias_ref[window, block, 0:span, :] = jnp.where(
                (key_at <= query_at) & same, 0.0, NEG
            )


def block_spans(windows, length):
    spans = []
    for window in range(windows):
        for block in range(length // 128):
            stop = block * 128 + 128
            start = max(0, stop - 384)
            base = window * length
            spans.append(
                (
                    window,
                    block,
                    slice(base + stop - 128, base + stop),
                    slice(base + start, base + stop),
                    stop - start,
                )
            )
    return spans


def part_lanes(pair, part):
    return pl.ds(pl.multiple_of(pair * 384 + part * 128, 128), 128)


def wait_whole(ref, sem):
    pltpu.make_async_copy(ref, ref, sem).wait()


def attend_kernel(
    direct,
    segments_ref,
    x_ref,
    p0_ref,
    p1_ref,
    p2_ref,
    p3_ref,
    qkv,
    attended_ref,
    lse_ref,
    passed_ref,
    mixed_ref,
    vec_ref,
    bin_ref,
    weights,
    bias,
    table,
    small,
    sems,
):
    windows, length = segments_ref.shape
    me = my_place() if direct else jnp.int32(0)
    for block in range(HALF):
        for half in range(2):
            source = ((p0_ref, p1_ref), (p2_ref, p3_ref))[half][block // 8].at[block % 8]
            wide, narrow = place_of(ORDER_FIRST, me, half, block)
            rows = pl.ds(pl.multiple_of(wide * 64, 64), 64)
            pltpu.make_async_copy(
                source.at[pl.ds(192, 64)],
                table.at[rows, pl.ds(pl.multiple_of(narrow * 128, 128), 128)],
                sems.at[0],
            ).start()
            pltpu.make_async_copy(
                source.at[pl.ds(256, 16)], small.at[half * HALF + block], sems.at[1]
            ).start()
            for part in range(3):
                pltpu.make_async_copy(
                    source.at[pl.ds(part * 64, 64)],
                    weights.at[
                        rows, pl.ds(pl.multiple_of(narrow * 384 + part * 128, 128), 128)
                    ],
                    sems.at[2],
                ).start()
    fill_bias(segments_ref, bias, windows)
    wait_whole(table, sems.at[0])
    for window in range(windows):
        rows = slice(window * length, (window + 1) * length)
        passed = x_ref[rows, :].astype(F32) + table[...].astype(F32)
        passed_ref[rows, :] = passed
        mixed_ref[rows, :] = passed.astype(BF16)
    wait_whole(small, sems.at[1])
    vec_ref[...] = jnp.zeros_like(vec_ref)
    bin_ref[...] = jnp.zeros_like(bin_ref)
    for half in range(2):
        for block in range(HALF):
            wide, narrow = place_of(ORDER_FIRST, me, half, block)
            piece = small[half * HALF + block].astype(F32)
            vec_ref[wide // 2] += piece[0:8]
            bin_ref[wide // 4] += piece[8:16]
    wait_whole(weights, sems.at[2])
    low = head_masks(128)

    for chunk in range(6):
        projected = nn(mixed_ref[...], weights[:, chunk * 256 : chunk * 256 + 256])
        for side in range(2):
            pair, part = divmod(chunk * 2 + side, 3)
            own = projected[:, side * 128 : side * 128 + 128]
            if part != 1:
                own = own + vec_ref[pair, part // 2 : part // 2 + 1, :]
            own = own.astype(BF16)
            if part == 0:
                own = own * BF16(0.125)
            qkv[:, (chunk * 2 + side) * 128 : (chunk * 2 + side) * 128 + 128] = own

    def per_pair(pair, unused):
        spans = block_spans(windows, length)
        turned_values = [
            jnp.transpose(
                qkv[window * length : (window + 1) * length, part_lanes(pair, 2)]
            )
            for window in range(windows)
        ]
        scores = []
        for window, block, here, there, span in spans:
            query = stack_heads(qkv[here, part_lanes(pair, 0)], low)
            mask = bias[window, block, 0:span, :]
            scores.append(
                nt(qkv[there, part_lanes(pair, 1)], query)
                + jnp.concatenate([mask, mask], axis=1)
            )
        shares = []
        for (window, block, here, there, span), score in zip(spans, scores):
            peak = jnp.max(score, axis=0, keepdims=True)
            weight = jnp.exp(score - peak)
            total = jnp.sum(weight, axis=0, keepdims=True)
            shares.append((weight * (1.0 / total)).astype(BF16))
            lse_ref[pair, window, block : block + 1, :] = peak + jnp.log(total)
        for (window, block, here, there, span), share in zip(spans, shares):
            stop = block * 128 + 128
            joined = nn(turned_values[window][:, stop - span : stop], share)
            both = jnp.concatenate([joined[0:64, 0:128], joined[64:128, 128:256]], axis=0)
            attended_ref[here, pl.ds(pl.multiple_of(pair * 128, 128), 128)] = jnp.transpose(
                both
            ).astype(BF16)
        return unused

    lax.fori_loop(0, NARROW, per_pair, 0, unroll=2)


def norm_parts(values):
    average = jnp.mean(values, axis=-1, keepdims=True)
    centred = values - average
    variance = jnp.mean(centred * centred, axis=-1, keepdims=True)
    scale = lax.rsqrt(variance + EPSILON)
    return centred * scale, scale


def norm_back(hat, scale, gains, grad):
    scaled = grad * gains
    first = jnp.mean(scaled, axis=-1, keepdims=True)
    second = jnp.mean(scaled * hat, axis=-1, keepdims=True)
    return scale * (scaled - first - hat * second)


def vec_row(vec_ref, row):
    return jnp.concatenate([vec_ref[tile, row : row + 1, :] for tile in range(4)], axis=1)


def column_sum(values):
    return jnp.sum(values, axis=0, keepdims=True)


GELU_SCALE = math.sqrt(2.0 / math.pi)


def gelu_both(pre):
    square = pre * pre
    half = jax.nn.sigmoid(pre * (2.0 * GELU_SCALE + (2.0 * GELU_SCALE * 0.044715) * square))
    value = pre * half
    bend = (1.0 - half) * (2.0 * GELU_SCALE + (6.0 * GELU_SCALE * 0.044715) * square)
    return value, half + value * bend


def load_second(me, blocks, w_in, w_back, sems):
    for block in range(HALF):
        for half in range(2):
            source = blocks[half * 2 + block // 8].at[block % 8]
            wide, narrow = place_of(ORDER_SECOND, me, half, block)
            rows = pl.ds(pl.multiple_of(wide * 64, 64), 64)
            columns = pl.ds(pl.multiple_of(narrow * 128, 128), 128)
            pltpu.make_async_copy(
                source.at[pl.ds(0, 5)], w_in.at[pl.ds(narrow * 5, 5), rows, :], sems.at[1]
            ).start()
            pltpu.make_async_copy(
                source.at[pl.ds(5, 4)], w_back.at[pl.ds(wide * 4, 4), :, columns], sems.at[2]
            ).start()


def w_in_tile(tile):
    return tile // 4 * 5 + tile % 4 + 1


def w_in_columns(w_in, chunk):
    tiles = [w_in[w_in_tile(chunk * 2 + side)] for side in range(2)]
    return jnp.concatenate(tiles, axis=1)


def w_out_whole(w_in):
    return jnp.concatenate([w_in[narrow * 5] for narrow in range(NARROW)], axis=1)


def rows_at(step, rows):
    return pl.ds(pl.multiple_of(step * rows, rows), rows)


def forward_kernel(
    direct,
    attended_ref,
    passed_ref,
    cotangent_ref,
    vec_ref,
    bin_ref,
    p0_ref,
    p1_ref,
    p2_ref,
    p3_ref,
    output_ref,
    slope_ref,
    grad_second_ref,
    first_ref,
    low_t,
    keep_ref,
    send_ref,
    sums_ref,
    w_in,
    w_back,
    active,
    grad_t,
    sems,
):
    rows = ROWS
    me = my_place() if direct else jnp.int32(0)
    load_second(me, (p0_ref, p1_ref, p2_ref, p3_ref), w_in, w_back, sems)
    sums_ref[...] = jnp.zeros_like(sums_ref)
    wait_whole(w_in, sems.at[1])
    wait_whole(w_back, sems.at[2])

    def per_rows(step, unused):
        here = rows_at(step, rows)
        first_sum = passed_ref[here, :] + nn(attended_ref[here, :], w_out_whole(w_in)) + vec_row(vec_ref, 2)
        first_ref[here, :] = first_sum
        hat, unused_scale = norm_parts(first_sum)
        hidden = hat * vec_row(vec_ref, 4) + vec_row(vec_ref, 5)
        low = hidden.astype(BF16)
        turned_low = jnp.transpose(low)
        for wide in range(WIDE):
            low_t[wide ^ (me >> 2), :, here] = turned_low[wide * 64 : wide * 64 + 64, :]
        total = hidden + vec_row(vec_ref, 3)
        for chunk in range(8):
            offset = jnp.concatenate(
                [
                    bin_ref[chunk // 4, 2 * (chunk % 4) + part : 2 * (chunk % 4) + part + 1, :]
                    for part in range(2)
                ],
                axis=1,
            )
            columns = slice(chunk * 256, chunk * 256 + 256)
            value, slope = gelu_both(nn(low, w_in_columns(w_in, chunk)) + offset)
            value = value.astype(BF16)
            active[here, columns] = value
            slope_ref[here, columns] = slope
            total += nn(value, w_back[chunk * 4 : chunk * 4 + 4].reshape(256, 512))
        hat, scale = norm_parts(total)
        gains = vec_row(vec_ref, 6)
        output_ref[here, :] = (hat * gains + vec_row(vec_ref, 7)).astype(BF16)
        cotangent = cotangent_ref[here, :].astype(F32)
        grad_second = norm_back(hat, scale, gains, cotangent)
        grad_second_ref[here, :] = grad_second
        grad_low = grad_second.astype(BF16)
        turned_low = jnp.transpose(grad_low)
        for narrow in range(NARROW):
            grad_t[narrow ^ (me & 3), :, here] = turned_low[narrow * 128 : narrow * 128 + 128, :]
        sums_ref[0:1, :] += column_sum(grad_low.astype(F32))
        sums_ref[1:2, :] += column_sum(cotangent * hat)
        sums_ref[2:3, :] += column_sum(cotangent)
        return unused

    total_rows = attended_ref.shape[0]
    lax.fori_loop(0, total_rows // rows, per_rows, 0)
    grads = grad_t[...].reshape(512, total_rows)
    for wide in range(WIDE):
        columns = pl.ds(pl.multiple_of((wide ^ (me >> 2)) * 256, 256), 256)
        piece = nn(grads, active[:, columns])
        for narrow in range(NARROW):
            target = (keep_ref, send_ref)[narrow & 1]
            block = block_at(ORDER_BACK, me, wide * NARROW + narrow)
            own = piece[narrow * 128 : narrow * 128 + 128]
            target[block, 0:128, :] = own[:, 0:128].astype(target.dtype)
            target[block, 128:256, :] = own[:, 128:256].astype(target.dtype)


def backward_kernel(
    direct,
    slope_ref,
    grad_second_ref,
    first_ref,
    low_t,
    attended_ref,
    vec_ref,
    w_in,
    w_back,
    grad_first_ref,
    grad_attended_ref,
    keep_ref,
    send_ref,
    sums_ref,
    bin_sums_ref,
    grad_pre,
    grad_branch,
    attended_t,
):
    rows = ROWS
    me = my_place() if direct else jnp.int32(0)
    sums_ref[...] = jnp.zeros_like(sums_ref)
    bin_sums_ref[...] = jnp.zeros_like(bin_sums_ref)

    def per_rows(step, unused):
        here = rows_at(step, rows)
        turned_low = jnp.transpose(attended_ref[here, :])
        for wide in range(WIDE):
            attended_t[wide ^ (me >> 2), :, here] = turned_low[wide * 64 : wide * 64 + 64, :]
        grad_hidden = grad_second_ref[here, :]
        grad_low = grad_hidden.astype(BF16)
        for chunk in range(8):
            columns = slice(chunk * 256, chunk * 256 + 256)
            weight = w_back[chunk * 4 : chunk * 4 + 4].reshape(256, 512)
            grad = (nt(grad_low, weight) * slope_ref[here, columns]).astype(BF16)
            grad_pre[here, columns] = grad
            sums = column_sum(grad.astype(F32))
            for part in range(2):
                row = 2 * (chunk % 4) + part
                bin_sums_ref[chunk // 4, row : row + 1, :] += sums[:, part * 128 : part * 128 + 128]
        grad_hidden += nt(
            grad_pre[here, :], jnp.concatenate([w_in[w_in_tile(tile)] for tile in range(16)], axis=1)
        )
        hat, scale = norm_parts(first_ref[here, :])
        gains = vec_row(vec_ref, 4)
        grad_first = norm_back(hat, scale, gains, grad_hidden)
        grad_first_ref[here, :] = grad_first
        branch = grad_first.astype(BF16)
        grad_branch[here, :] = branch
        sums_ref[0:1, :] += column_sum(branch.astype(F32))
        sums_ref[1:2, :] += column_sum(grad_hidden * hat)
        sums_ref[2:3, :] += column_sum(grad_hidden)
        grad_attended_ref[here, :] = nt(branch, w_out_whole(w_in)).astype(BF16)
        return unused

    total_rows = attended_ref.shape[0]
    lax.fori_loop(0, total_rows // rows, per_rows, 0)
    lows = low_t[...].reshape(512, total_rows)
    joined = attended_t[...].reshape(512, total_rows)
    for narrow in range(NARROW):
        target = (keep_ref, send_ref)[narrow & 1]
        at = narrow ^ (me & 3)
        for part in range(2):
            columns = pl.ds(pl.multiple_of(at * 512 + part * 256, 256), 256)
            piece = nn(lows, grad_pre[:, columns])
            for wide in range(WIDE):
                block = block_at(ORDER_INNER, me, wide * NARROW + narrow)
                own = piece[wide * 64 : wide * 64 + 64]
                target[block, part * 2] = own[:, 0:128].astype(target.dtype)
                target[block, part * 2 + 1] = own[:, 128:256].astype(target.dtype)
        piece = nn(joined, grad_branch[:, pl.ds(pl.multiple_of(at * 128, 128), 128)])
        for wide in range(WIDE):
            block = block_at(ORDER_INNER, me, wide * NARROW + narrow)
            target[block, 4] = piece[wide * 64 : wide * 64 + 64].astype(target.dtype)


def attend_back_kernel(
    direct,
    segments_ref,
    qkv_ref,
    grad_attended_ref,
    lse_ref,
    grads,
    vec_sums,
    bias,
):
    windows, length = segments_ref.shape
    me = my_place() if direct else jnp.int32(0)
    fill_bias(segments_ref, bias, windows)
    vec_sums[...] = jnp.zeros_like(vec_sums)
    low = head_masks(128)

    def per_pair(apart, unused):
        pair = (me & 3) ^ apart
        spans = block_spans(windows, length)
        lanes = pl.ds(pl.multiple_of(pair * 128, 128), 128)
        turned_keys = [
            jnp.transpose(
                qkv_ref[window * length : (window + 1) * length, part_lanes(pair, 1)]
            )
            for window in range(windows)
        ]
        queries, aboves, scores, grad_shares = [], [], [], []
        for window, block, here, there, span in spans:
            queries.append(stack_heads(qkv_ref[here, part_lanes(pair, 0)], low))
            aboves.append(stack_heads(grad_attended_ref[here, lanes], low))
            mask = bias[window, block, 0:span, :]
            mask = jnp.concatenate([mask, mask], axis=1)
            scores.append(
                nt(qkv_ref[there, part_lanes(pair, 1)], queries[-1])
                + (mask - lse_ref[pair, window, block : block + 1, :])
            )
            grad_shares.append(nt(qkv_ref[there, part_lanes(pair, 2)], aboves[-1]))
        shares, grad_scores = [], []
        for score, grad_share in zip(scores, grad_shares):
            share = jnp.exp(score)
            inner = jnp.sum(share * grad_share, axis=0, keepdims=True)
            shares.append(share.astype(BF16))
            grad_scores.append((share * (grad_share - inner)).astype(BF16))
        grad_keys = [[None] * (length // 128) for window in range(windows)]
        grad_values = [[None] * (length // 128) for window in range(windows)]
        for at, (window, block, here, there, span) in enumerate(spans):
            stop = block * 128 + 128
            for found, sums in (
                (nn(grad_scores[at], queries[at]), grad_keys[window]),
                (nn(shares[at], aboves[at]), grad_values[window]),
            ):
                for part in range(span // 128):
                    of = block - span // 128 + 1 + part
                    piece = found[part * 128 : part * 128 + 128]
                    sums[of] = piece if sums[of] is None else sums[of] + piece
            joined = nn(turned_keys[window][:, stop - span : stop], grad_scores[at])
            both = jnp.concatenate([joined[0:64, 0:128], joined[64:128, 128:256]], axis=0)
            grad = (jnp.transpose(both) * 0.125).astype(BF16)
            grads[here, part_lanes(apart, 0)] = grad
            vec_sums[pair, 0:1, :] += column_sum(grad.astype(F32))
        for window, block, here, there, span in spans:
            grads[here, part_lanes(apart, 1)] = grad_keys[window][block].astype(BF16)
            grad = grad_values[window][block].astype(BF16)
            grads[here, part_lanes(apart, 2)] = grad
            vec_sums[pair, 1:2, :] += column_sum(grad.astype(F32))
        return unused

    lax.fori_loop(0, NARROW, per_pair, 0)


def project_back_kernel(
    direct,
    windows,
    grads,
    mixed_ref,
    grad_first_ref,
    pair_sums_ref,
    sums_a_ref,
    sums_b_ref,
    bin_sums_ref,
    weights,
    stream_ref,
    keep_ref,
    send_ref,
    mixed_t,
    stream,
    vec_sums,
):
    length = mixed_ref.shape[0] // windows
    me = my_place() if direct else jnp.int32(0)
    turned_low = jnp.transpose(mixed_ref[...])
    for wide in range(WIDE):
        mixed_t[wide ^ (me >> 2), :, :] = turned_low[wide * 64 : wide * 64 + 64, :]
    for tile in range(4):
        lanes = slice(tile * 128, tile * 128 + 128)
        vec_sums[tile, 0:2, :] = pair_sums_ref[tile, 0:2, :]
        vec_sums[tile, 2:3, :] = sums_b_ref[0:1, lanes]
        vec_sums[tile, 3:4, :] = sums_a_ref[0:1, lanes]
        vec_sums[tile, 4:6, :] = sums_b_ref[1:3, lanes]
        vec_sums[tile, 6:8, :] = sums_a_ref[1:3, lanes]
    turned_mixed = mixed_t[...].reshape(512, windows * length)
    for chunk in range(6):
        weight_grads = nn(turned_mixed, grads[:, chunk * 256 : chunk * 256 + 256])
        for side in range(2):
            apart, part = divmod(chunk * 2 + side, 3)
            target = (keep_ref, send_ref)[apart & 1]
            for wide in range(WIDE):
                block = block_at(ORDER_OUTER, me, wide * NARROW + apart)
                target[block, part * 64 : part * 64 + 64, :] = weight_grads[
                    wide * 64 : wide * 64 + 64, side * 128 : side * 128 + 128
                ].astype(target.dtype)
    for row in range(0, length, 256):
        total = None
        for window in range(windows):
            rows = slice(window * length + row, window * length + row + 256)
            sums = grad_first_ref[rows, :]
            for apart in range(NARROW):
                lanes = pl.ds(pl.multiple_of(((me & 3) ^ apart) * 384, 128), 384)
                sums += nt(grads[rows, apart * 384 : apart * 384 + 384], weights[:, lanes])
            stream_ref[rows, :] = sums.astype(BF16)
            total = sums if total is None else total + sums
        stream[row : row + 256, :] = total
    for half, target in ((0, keep_ref), (1, send_ref)):
        for block in range(HALF):
            wide, narrow = place_of(ORDER_OUTER, me, half, block)
            target[block, 192:256, :] = stream[
                pl.ds(pl.multiple_of(wide * 64, 64), 64),
                pl.ds(pl.multiple_of(narrow * 128, 128), 128),
            ].astype(target.dtype)
            target[block, 256:264, :] = vec_sums[wide // 2].astype(target.dtype)
            target[block, 264:272, :] = bin_sums_ref[wide // 4].astype(target.dtype)


def doubled(row):
    return jnp.concatenate([row, row], axis=1)


def pack_kernel(
    w_query_ref,
    w_key_ref,
    w_value_ref,
    w_out_ref,
    w_in_ref,
    w_back_ref,
    table_ref,
    vectors_ref,
    in_bias_ref,
    first_ref,
    second_ref,
):
    wide, narrow = lax.axis_index("wide"), lax.axis_index("narrow")
    first_ref[0:64, :] = w_query_ref[...]
    first_ref[64:128, :] = w_key_ref[...]
    first_ref[128:192, :] = w_value_ref[...]
    first_ref[192:256, :] = table_ref[...]
    row = lax.broadcasted_iota(jnp.int32, (8, 128), 0)
    side = lax.broadcasted_iota(jnp.int32, (8, 128), 1) // 64
    vectors = doubled(vectors_ref[...].astype(F32))
    spread = jnp.where(row % 2 == 0, vectors[0:1], vectors[1:2])
    upper = jnp.where((row // 2 == narrow) & (side == wide % 2), spread, 0.0)
    spread = doubled(in_bias_ref[...].astype(F32))
    lower = jnp.where(
        (row == 2 * (wide % 4) + narrow // 2) & (side == narrow % 2), spread, 0.0
    )
    first_ref[256:272, :] = jnp.concatenate([upper, lower], axis=0).astype(BF16)
    second_ref[0] = w_out_ref[...]
    for part in range(4):
        second_ref[1 + part] = w_in_ref[:, part * 128 : part * 128 + 128]
        second_ref[5 + part] = w_back_ref[part * 64 : part * 64 + 64, :]


def finish_kernel(
    outer_ref,
    outer_first_ref,
    outer_second_ref,
    outer_third_ref,
    inner_ref,
    inner_came_ref,
    back_ref,
    back_came_ref,
    query_ref,
    key_ref,
    value_ref,
    out_ref,
    in_ref,
    w_back_ref,
    table_ref,
    vectors_ref,
    in_bias_ref,
):
    wide, narrow = lax.axis_index("wide"), lax.axis_index("narrow")
    total = back_ref[0] + back_came_ref[0].astype(F32)
    w_back_ref[0:128, :] = jnp.transpose(total[0:128])
    w_back_ref[128:256, :] = jnp.transpose(total[128:256])
    for part in range(4):
        in_ref[:, part * 128 : part * 128 + 128] = inner_ref[0, part] + inner_came_ref[
            0, part
        ].astype(F32)
    out_ref[...] = inner_ref[0, 4] + inner_came_ref[0, 4].astype(F32)
    total = outer_ref[0] + outer_first_ref[0].astype(F32)
    total += outer_second_ref[0].astype(F32) + outer_third_ref[0].astype(F32)
    query_ref[...] = total[0:64]
    key_ref[...] = total[64:128]
    value_ref[...] = total[128:192]
    table_ref[...] = total[192:256]
    row = lax.broadcasted_iota(jnp.int32, (8, 128), 0)

    def side_of(rows, second):
        return jnp.where(second == 1, rows[:, 64:128], rows[:, 0:64])

    def row_of(rows, which):
        return column_sum(jnp.where(row == which, rows, 0.0))

    vectors = jnp.concatenate(
        [row_of(total[256:264], narrow * 2), row_of(total[256:264], narrow * 2 + 1)], axis=0
    )
    vectors_ref[...] = side_of(vectors, wide % 2)
    bins = row_of(total[264:272], 2 * (wide % 4) + narrow // 2)
    in_bias_ref[...] = side_of(bins, narrow % 2)


def vmem():
    return pl.BlockSpec(memory_space=pltpu.VMEM)


def hbm():
    return pl.BlockSpec(memory_space=pl.ANY)


def cost(macs, touched):
    return pl.CostEstimate(flops=2 * macs, bytes_accessed=touched, transcendentals=0)


def params(mebibytes):
    return pltpu.CompilerParams(vmem_limit_bytes=mebibytes << 20)


def shape(dims, dtype):
    return jax.ShapeDtypeStruct(dims, dtype)


def near(dims, dtype):
    return pltpu.VMEM(dims, dtype)


def kept(array):
    return pltpu.with_memory_space_constraint(array, pltpu.VMEM)


def attend_call(direct, segments, x, blocks):
    windows, length = segments.shape
    total = windows * length
    return pl.pallas_call(
        partial(attend_kernel, direct),
        out_shape=(
            near((total, 1536), BF16),
            shape((total, 512), BF16),
            shape((NARROW, windows, length // 128, 256), F32),
            near((total, 512), F32),
            shape((total, 512), BF16),
            shape((4, 8, 128), F32),
            shape((2, 8, 128), F32),
            shape((512, 1536), BF16),
        ),
        in_specs=[vmem(), vmem()] + [hbm()] * 4,
        out_specs=tuple([vmem()] * 8),
        scratch_shapes=[
            pltpu.VMEM((windows, length // 128, 384, 128), F32),
            pltpu.VMEM((512, 512), BF16),
            pltpu.VMEM((PLACES, 16, 128), BF16),
            pltpu.SemaphoreType.DMA((3,)),
        ],
        compiler_params=params(ATTEND_MIB),
        cost_estimate=cost(6000 << 20, 12 << 20),
        name="attend",
    )(segments, x, *blocks)


ROWS = 512
ATTEND_MIB = 24
FORWARD_MIB = 12
BACKWARD_MIB = 11
ATTEND_BACK_MIB = 20
PROJECT_BACK_MIB = 16


def forward_call(direct, attended, passed, cotangent, vec, bins, blocks):
    total = attended.shape[0]
    return pl.pallas_call(
        partial(forward_kernel, direct),
        out_shape=(
            shape((total, 512), BF16),
            near((total, 2048), F32),
            near((total, 512), F32),
            near((total, 512), F32),
            near((WIDE, 64, total), BF16),
            near((HALF, 256, 128), F32),
            near((HALF, 256, 128), BF16),
            shape((8, 512), F32),
            near((20, 512, 128), BF16),
            near((32, 64, 512), BF16),
        ),
        in_specs=[vmem()] * 5 + [hbm()] * 4,
        out_specs=tuple([vmem()] * 10),
        scratch_shapes=[
            pltpu.VMEM((total, 2048), BF16),
            pltpu.VMEM((NARROW, 128, total), BF16),
            pltpu.SemaphoreType.DMA((3,)),
        ],
        compiler_params=params(FORWARD_MIB),
        cost_estimate=cost(6000 << 20, 24 << 20),
        input_output_aliases={1: 3},
        name="forward",
    )(attended, kept(passed), cotangent, vec, bins, *blocks)


def backward_call(direct, slope, grad_second, first_sum, low_t, attended, vec, weights):
    total = attended.shape[0]
    return pl.pallas_call(
        partial(backward_kernel, direct),
        out_shape=(
            shape((total, 512), F32),
            shape((total, 512), BF16),
            shape((HALF, 5, 64, 128), F32),
            shape((HALF, 5, 64, 128), BF16),
            shape((8, 512), F32),
            shape((2, 8, 128), F32),
        ),
        in_specs=[vmem()] * 8,
        out_specs=tuple([vmem()] * 6),
        scratch_shapes=[
            pltpu.VMEM((total, 2048), BF16),
            pltpu.VMEM((total, 512), BF16),
            pltpu.VMEM((WIDE, 64, total), BF16),
        ],
        compiler_params=params(BACKWARD_MIB),
        cost_estimate=cost(7000 << 20, 24 << 20),
        input_output_aliases={1: 0, 4: 1},
        name="backward",
    )(
        kept(slope),
        kept(grad_second),
        kept(first_sum),
        kept(low_t),
        attended,
        vec,
        *(kept(weight) for weight in weights),
    )


def attend_back_call(direct, segments, qkv, grad_attended, lse):
    windows, length = segments.shape
    total = windows * length
    return pl.pallas_call(
        partial(attend_back_kernel, direct),
        out_shape=(shape((total, 1536), BF16), shape((4, 8, 128), F32)),
        in_specs=[vmem()] * 4,
        out_specs=(vmem(), vmem()),
        scratch_shapes=[pltpu.VMEM((windows, length // 128, 384, 128), F32)],
        compiler_params=params(ATTEND_BACK_MIB),
        cost_estimate=cost(4000 << 20, 8 << 20),
        name="attend_back",
    )(segments, kept(qkv), grad_attended, lse)


def project_back_call(direct, windows, grads, mixed, grad_first, sums, weights):
    total = mixed.shape[0]
    return pl.pallas_call(
        partial(project_back_kernel, direct, windows),
        out_shape=(
            shape((total, 512), BF16),
            shape((HALF, 272, 128), F32),
            shape((HALF, 272, 128), BF16),
        ),
        in_specs=[vmem()] * 8,
        out_specs=(vmem(), vmem(), vmem()),
        scratch_shapes=[
            pltpu.VMEM((WIDE, 64, total), BF16),
            pltpu.VMEM((total // windows, 512), F32),
            pltpu.VMEM((4, 8, 128), F32),
        ],
        compiler_params=params(PROJECT_BACK_MIB),
        cost_estimate=cost(3000 << 20, 8 << 20),
        name="project_back",
    )(grads, mixed, grad_first, *sums, weights)


def pack_call(*shards):
    return pl.pallas_call(
        pack_kernel,
        out_shape=(near((272, 128), BF16), near((9, 64, 128), BF16)),
        in_specs=[vmem()] * 9,
        out_specs=(vmem(), vmem()),
        name="pack",
    )(*shards)


def join_kernel(first_ref, second_ref, joined_ref):
    half = first_ref.shape[0]
    joined_ref[0:half] = first_ref[...]
    joined_ref[half:] = second_ref[...]


def joined_blocks(first, second):
    count = 2 * first.shape[0]
    return pl.pallas_call(
        join_kernel,
        out_shape=near((count,) + first.shape[1:], first.dtype),
        in_specs=[vmem()] * 2,
        out_specs=vmem(),
        compiler_params=params(2),
        name="join",
    )(kept(first), kept(second))


def finish_call(outer, inner, back):
    block = shape((64, 128), F32)
    return pl.pallas_call(
        finish_kernel,
        out_shape=(
            block,
            block,
            block,
            block,
            shape((64, 512), F32),
            shape((256, 128), F32),
            block,
            shape((2, 64), F32),
            shape((1, 64), F32),
        ),
        in_specs=[vmem()] * 8,
        out_specs=tuple([vmem()] * 9),
        compiler_params=params(6),
        name="finish",
    )(*outer, *inner, *back)


def swap(array, order, step):
    return lax.ppermute(array, AXES, pairs(order, step))


def after(value, *others):
    return lax.optimization_barrier((value,) + others)[0]


def grow(held, order, step):
    return jnp.concatenate([held, swap(held, order, step)], axis=0)


def start_halving(keep, send, order):
    return keep, swap(send, order, 4)


def halve(held, came, order, step):
    size = 1 << step
    upper = (held[size:] + came[size:].astype(F32)).astype(BF16)
    lower = held[:size] + came[:size].astype(F32)
    return lower, swap(upper, order, step)


def scatter_rest(held, came, order):
    own = held[:1] + came[:1].astype(F32)
    others = []
    for block in range(1, 4):
        total = (held[block : block + 1] + came[block : block + 1].astype(F32)).astype(BF16)
        partners = []
        for place in range(PLACES):
            partners.append((place, place ^ block_masks(order, place & 1)[block]))
        others.append(lax.ppermute(total, AXES, partners))
    return own, *others


def small_block(vectors, in_bias, wide, narrow):
    row = lax.broadcasted_iota(jnp.int32, (8, 128), 0)
    side = lax.broadcasted_iota(jnp.int32, (8, 128), 1) // 64
    spread = jnp.tile(vectors, (4, 2))
    first = jnp.where((row // 2 == narrow) & (side == wide % 2), spread, 0)
    spread = jnp.tile(in_bias[None], (8, 2))
    second = jnp.where((row == 2 * (wide % 4) + narrow // 2) & (side == narrow % 2), spread, 0)
    return jnp.concatenate([first, second], axis=0).astype(BF16)


def first_block(w_query, w_key, w_value, table, small):
    return jnp.concatenate([w_query, w_key, w_value, table, small], axis=0)


def second_block(w_out, w_in, w_back):
    return jnp.concatenate(
        [w_out[None]]
        + [w_in[None, :, part * 128 : part * 128 + 128] for part in range(4)]
        + [w_back.reshape(4, 64, 128)],
        axis=0,
    )


def turned(total):
    return jnp.concatenate([total[0:128].T, total[128:256].T], axis=0)


def per_device(
    inputs,
    segment_ids,
    cotangent,
    w_query,
    w_key,
    w_value,
    w_out,
    w_in,
    w_back,
    position_table,
    vectors,
    in_bias,
):
    windows, length, features = inputs.shape
    rows = windows * length
    x = inputs.reshape(rows, features)
    early, late = pack_call(
        w_query, w_key, w_value, w_out, w_in, w_back, position_table, vectors, in_bias[None]
    )
    early, late = early[None], late[None]
    for step in range(4):
        early_came = swap(early, ORDER_FIRST, step)
        late_came = swap(late, ORDER_SECOND, step)
        early_came, late_came = lax.optimization_barrier((early_came, late_came))
        if step < 3:
            early = joined_blocks(early, early_came)
            late = joined_blocks(late, late_came)
        else:
            early_far, late_far = early_came, late_came
    first = (early, early_far, swap(early, ORDER_FIRST, 4), swap(early_far, ORDER_FIRST, 4))
    second = (late, late_far, swap(late, ORDER_SECOND, 4), swap(late_far, ORDER_SECOND, 4))
    qkv, attended, lse, passed, mixed, vec, bins, w_qkv = attend_call(
        True, segment_ids, after(x, late), first
    )
    *second, attended = lax.optimization_barrier((*second, attended))
    output, slope, grad_second, first_sum, low_t, keep, send, sums_a, *whole = forward_call(
        True, attended, passed, cotangent.reshape(rows, features), vec, bins, second
    )
    back = start_halving(keep, send, ORDER_BACK)
    grad_first, grad_attended, keep, send, sums_b, bin_sums = backward_call(
        True, slope, grad_second, first_sum, low_t, attended, vec, whole
    )
    back = halve(*back, ORDER_BACK, 3)
    inner = start_halving(keep, send, ORDER_INNER)
    grads, pair_sums = attend_back_call(
        True, segment_ids, qkv, after(grad_attended, back[0]), lse
    )
    grads, back_came, inner_came = lax.optimization_barrier((grads, back[1], inner[1]))
    back = halve(back[0], back_came, ORDER_BACK, 2)
    inner = halve(inner[0], inner_came, ORDER_INNER, 3)
    stream, keep, send = project_back_call(
        True,
        windows,
        after(grads, back[0], inner[0]),
        mixed,
        grad_first,
        (pair_sums, sums_a, sums_b, bin_sums),
        w_qkv,
    )
    keep, send, back_came = lax.optimization_barrier((keep, send, back[1]))
    upper_came, lower_came = swap(send[8:], ORDER_OUTER, 4), swap(send[:8], ORDER_OUTER, 4)
    back = halve(back[0], back_came, ORDER_BACK, 1)
    upper_came, inner_came = lax.optimization_barrier((upper_came, inner[1]))
    upper = (keep[8:] + upper_came.astype(F32)).astype(BF16)
    far = swap(upper, ORDER_OUTER, 3)
    inner = halve(inner[0], inner_came, ORDER_INNER, 2)
    came = lax.optimization_barrier((far, inner[1], back[1], lower_came))
    outer = halve(keep[:8] + came[3].astype(F32), came[0], ORDER_OUTER, 2)
    inner = halve(inner[0], came[1], ORDER_INNER, 1)
    back = halve(back[0], came[2], ORDER_BACK, 0)
    came = lax.optimization_barrier((outer[1], inner[1], back[1]))
    outer = scatter_rest(outer[0], came[0], ORDER_OUTER)
    inner = halve(inner[0], came[1], ORDER_INNER, 0)
    back = back[0], came[2]
    *matrices, vec, bins = finish_call(outer, inner, back)
    return (
        output.reshape(inputs.shape),
        stream.reshape(inputs.shape),
        *matrices,
        vec,
        bins[0],
    )


def listed(order):
    return block_masks(order, 0) + [1 ^ mask for mask in block_masks(order, 1)]


def canonical(array, axis_tiles):
    rows, columns = array.shape
    across, along = axis_tiles
    return (
        array.reshape(across, rows // across, along, columns // along)
        .transpose(0, 2, 1, 3)
        .reshape(PLACES, rows // across, columns // along)
    )


def uncanonical(blocks, rows, columns):
    return (
        blocks.reshape(WIDE, NARROW, rows // WIDE, columns // NARROW)
        .transpose(0, 2, 1, 3)
        .reshape(rows, columns)
    )


def per_device_any(
    inputs,
    segment_ids,
    cotangent,
    w_query,
    w_key,
    w_value,
    w_out,
    w_in,
    w_back,
    position_table,
    vectors,
    in_bias,
):
    def whole(array):
        array = lax.all_gather(array, "narrow", axis=1, tiled=True)
        return lax.all_gather(array, "wide", axis=0, tiled=True)

    def fours(blocks, order):
        blocks = jnp.stack([blocks[place] for place in listed(order)])
        return tuple(blocks[at * 8 : at * 8 + 8] for at in range(4))

    vectors = lax.all_gather(vectors, "narrow", axis=0, tiled=True)
    vectors = lax.all_gather(vectors, "wide", axis=1, tiled=True)
    in_bias = lax.all_gather(in_bias, AXES, axis=0, tiled=True)
    places = jnp.arange(PLACES)
    pieces = vectors.reshape(NARROW, 2, WIDE, 64).transpose(2, 0, 1, 3).reshape(PLACES, 2, 64)
    small = jax.vmap(small_block)(
        pieces, in_bias.reshape(PLACES, 64), places // NARROW, places % NARROW
    )
    tiles = (WIDE, NARROW)
    first = jax.vmap(first_block)(
        canonical(whole(w_query), tiles),
        canonical(whole(w_key), tiles),
        canonical(whole(w_value), tiles),
        canonical(whole(position_table), tiles),
        small,
    )
    second = jax.vmap(second_block)(
        canonical(whole(w_out), tiles),
        canonical(whole(w_in), tiles),
        canonical(whole(w_back), tiles),
    )
    windows, length, features = inputs.shape
    rows = windows * length
    first, second = fours(first, ORDER_FIRST), fours(second, ORDER_SECOND)
    qkv, attended, lse, passed, mixed, vec, bins, w_qkv = attend_call(
        False, segment_ids, inputs.reshape(rows, features), first
    )
    output, slope, grad_second, first_sum, low_t, keep_back, send_back, sums_a, *whole_w = forward_call(
        False, attended, passed, cotangent.reshape(rows, features), vec, bins, second
    )
    grad_first, grad_attended, keep_in, send_in, sums_b, bin_sums = backward_call(
        False, slope, grad_second, first_sum, low_t, attended, vec, whole_w
    )
    grads, pair_sums = attend_back_call(False, segment_ids, qkv, grad_attended, lse)
    stream, keep_first, send_first = project_back_call(
        False,
        windows,
        grads,
        mixed,
        grad_first,
        (pair_sums, sums_a, sums_b, bin_sums),
        w_qkv,
    )

    def joined(pair, order):
        both = jnp.concatenate([pair[0], pair[1].astype(F32)], axis=0)
        return jnp.stack([both[listed(order).index(place)] for place in range(PLACES)])

    def summed(array):
        array = lax.psum_scatter(array, "wide", scatter_dimension=0, tiled=True)
        return lax.psum_scatter(array, "narrow", scatter_dimension=1, tiled=True)

    back = joined((keep_back, send_back), ORDER_BACK)
    inner = joined((keep_in, send_in), ORDER_INNER)
    outer = joined((keep_first, send_first), ORDER_OUTER)
    back = jax.vmap(turned)(back)
    grad_in = inner[:, 0:4].transpose(0, 2, 1, 3).reshape(PLACES, 64, 512)
    vec = outer.reshape(WIDE, NARROW, 272, 128)[::2, 0, 256:264]
    vec = vec.transpose(1, 0, 2).reshape(8, 512)
    vec = lax.psum_scatter(vec, "wide", scatter_dimension=1, tiled=True)
    vec = lax.psum_scatter(vec, "narrow", scatter_dimension=0, tiled=True)
    bins = outer.reshape(WIDE, NARROW, 272, 128)[::4, 0, 264:272].reshape(2048)
    bins = lax.psum_scatter(bins, AXES, scatter_dimension=0, tiled=True)
    return (
        output.reshape(inputs.shape),
        stream.reshape(inputs.shape),
        summed(uncanonical(outer[:, 0:64], 512, 512)),
        summed(uncanonical(outer[:, 64:128], 512, 512)),
        summed(uncanonical(outer[:, 128:192], 512, 512)),
        summed(uncanonical(inner[:, 4], 512, 512)),
        summed(uncanonical(grad_in, 512, 2048)),
        summed(uncanonical(back, 2048, 512)),
        summed(uncanonical(outer[:, 192:256], 512, 512)),
        vec,
        bins,
    )


def solution(mesh):
    matrix = P("wide", "narrow")
    rows = P(AXES, None, None)
    direct = mesh.shape["wide"] == WIDE and mesh.shape["narrow"] == NARROW
    return jax.shard_map(
        per_device if direct else per_device_any,
        mesh=mesh,
        in_specs=(
            rows,
            P(AXES, None),
            rows,
            matrix,
            matrix,
            matrix,
            matrix,
            matrix,
            matrix,
            matrix,
            P("narrow", "wide"),
            P(AXES),
        ),
        out_specs=(
            rows,
            rows,
            matrix,
            matrix,
            matrix,
            matrix,
            matrix,
            matrix,
            matrix,
            P("narrow", "wide"),
            P(AXES),
        ),
        check_vma=False,
    )
```
